128 devices in a mesh: dom: 16 (over z, y_hi, core), rot: 8 (over y_lo, x).
Axes of the slice: x: 4, y: 4 (y_hi: 2, y_lo: 2; y = y_hi * 2 + y_lo), z: 4, core: 2. Of those that a mesh axis runs over, the one named last changes fastest.
Arguments:
- particles: bfloat16 [128, 64, 4096], P('dom'), may hold values from -6 to 6
- references: bfloat16 [32, 64, 4096], P('rot', 'dom'), may hold values from -6 to 6
- part_class: int32 [128, 1], P('dom'), may hold values from 0 to 7; in each aligned block of 8 rows (0 to 7, 8 to 15, ...) at most 4 rows name the same one
- part_rot: int32 [128], P('dom'), may hold values from 0 to 3
- bucket: int32 [128], P('dom'), may hold values from 0 to 7
- bucket_weights: bfloat16 [8], replicated, may hold values from 0.25 to 2
- live_count: int32 [16], P('dom'), may hold values from 4 to 8, as said below
Outputs:
- scores: float32 [128, 512], P('dom')
- sums: float32 [64, 32, 64, 128], P('dom', 'rot')
The draws below stay inside these ranges and needn't reach their ends.
Inputs may be any that keep to these rules, and one draw needn't show every extreme that they name: `part_class`: among the 8 particles of one index of dom no class is named more than 4 times, and some class is named 4 times in some such block. `live_count`: some block has all 8 particles in use.
All inputs are finite; a program needn't handle non-finite values.
Results may differ from the reference program's by a relative error of at most 0.014.
Values may be sent and summed in bfloat16 or wider, within the bound.
No kernel may reach another device: no remote copies, remote signals or barrier semaphores. Data moves between devices by JAX's collectives and lax.ppermute only.
A program may use at most 192 MiB of HBM per device.

```python
import math
import jax
import jax.numpy as jnp
import numpy as np
from jax import lax

BOX = 64
SHIFTS = 8
ROT_CLS = 4
BUCKETS = 8
PART_DEV = 8
CAP = 4
CLASSES = 8
ROTATIONS = 32
PARTICLES = 128
SHARDS = 16


def draw_live_count(key, part):
    first_key, second_key = jax.random.split(jax.random.fold_in(key, 11))
    counts = jax.random.randint(first_key, (SHARDS,), PART_DEV // 2, PART_DEV + 1)
    full_index = jax.random.randint(second_key, (), 0, SHARDS)
    return jnp.where(jnp.arange(SHARDS) == full_index, PART_DEV, counts).astype(jnp.int32)


def plant(entries, rng, smallest, high):
    longest = entries.shape.index(max(entries.shape))
    spots = []
    for shift in (0, 1):
        where = [jax.random.randint(jax.random.fold_in(rng, axis), (), 0, length) for axis, length in enumerate(entries.shape)]
        where[longest] = (where[longest] + shift) % entries.shape[longest]
        spots.append(tuple(where))
    return entries.at[spots[0]].set(smallest).at[spots[1]].set(high)


def steps_of(own_key, dims, pieces, low, largest):
    level, own = 1.0, jax.random.fold_in(own_key, 6)
    for dim, parts in pieces:
        heights = jnp.exp(jax.random.uniform(jax.random.fold_in(own, dim), (parts,), jnp.float32, low / len(pieces), largest / len(pieces)))
        level = level * jnp.repeat(heights, dims[dim] // parts).reshape([-1 if axis == dim else 1 for axis in range(len(dims))])
    return level


def assign_block(stream_key, own, number, rows, number_of, top, reach, slope):
    sequence = jax.random.permutation(stream_key, number_of)
    crowded, ordinary = load_shares(number_of, rows * top, reach, slope, True), load_shares(number_of, rows * top, reach, slope, False)
    places = jnp.arange(number_of)

    def named(lengths, rotation):
        used = int((lengths > 0).sum())
        fixed = max(1, used // 4)
        passed = fixed + (places - fixed + rotation * (used - fixed)) % max(1, number_of - fixed)
        return jnp.zeros((number_of,), jnp.int32).at[sequence[jnp.where(places < fixed, places, passed)]].set(jnp.asarray(lengths, jnp.int32))

    lengths = jnp.where(number % 4 == 0, named(crowded, number // 4), named(ordinary, number - number // 4 - 1))
    mixed = jax.random.permutation(jax.random.fold_in(own, 3), number_of)
    giver, taker = mixed[0:number_of // 2 * 2:2], mixed[1:number_of // 2 * 2:2]
    margin = jnp.minimum(lengths[giver] - 1, reach - lengths[taker]) // 2
    margin = jnp.where((giver == sequence[0]) | (taker == sequence[0]) | (lengths[taker] == 0), 0, jnp.maximum(margin, 0))
    passed = jax.random.randint(jax.random.fold_in(own, 4), (number_of // 2,), 0, 1 << 20) % (margin + 1)
    lengths = lengths.at[giver].add(-passed).at[taker].add(passed)
    members = jnp.searchsorted(jnp.cumsum(lengths), jnp.arange(rows * top), side="right").astype(jnp.int32)
    grid = members.reshape(top, rows).T
    grid = grid[jax.random.permutation(jax.random.fold_in(own, 1), rows)]
    rotation = jax.random.randint(jax.random.fold_in(own, 2), (rows, 1), 0, top)
    return jnp.take_along_axis(grid, (jnp.arange(top)[None, :] + rotation) % top, axis=1)


def load_shares(count, total, limit, lean, full):
    weights = [(1 << 20) // math.isqrt(grade ** lean) + 1 for grade in range(1, count + 1)]
    largest = limit if full else min(limit, max(-(-total // count), total * weights[0] // sum(weights)))
    least = 1 if total - largest >= count - 1 else 0
    given, rest = [largest] + [least] * (count - 1), total - largest - least * (count - 1)
    while rest > 0:
        free = [i for i in range(1, count) if given[i] < largest] or [i for i in range(1, count) if given[i] < limit]
        whole, budget = sum([weights[i] for i in free]), rest
        for i in free:
            extra = min(limit - given[i], max(1, budget * weights[i] // whole), rest)
            given[i] = given[i] + extra
            rest = rest - extra
    return np.array(given)


def noise(stream_key, extent, width, bound, cuts=(), kind=jnp.bfloat16):
    entries = jax.random.normal(stream_key, extent, jnp.float32) * width
    if len(cuts) > 0:
        entries = steps_of(stream_key, extent, cuts, -0.22, 0.18) * entries
    return jnp.clip(entries, min=-bound, max=bound).astype(kind)


def setup_inputs(seed: int = 0) -> dict:
    arg_keys = jax.random.split(jax.random.key(seed), 8)
    particles = noise(arg_keys[0], (PARTICLES, BOX, BOX * BOX), 1.0, 6.0, ((0, 16),))
    references = noise(arg_keys[1], (ROTATIONS, BOX, BOX * BOX), 1.0, 6.0, ((0, 8), (1, 16)))
    part_class_keys = jax.random.split(jax.random.fold_in(arg_keys[2], 1), PARTICLES // PART_DEV)
    part_class_turns = jax.random.permutation(jax.random.fold_in(arg_keys[2], 3), PARTICLES // PART_DEV)
    part_class = jax.vmap(lambda own, number: assign_block(jax.random.fold_in(arg_keys[2], 2), own, number, PART_DEV, CLASSES, 1, CAP, 2))(part_class_keys, part_class_turns).reshape((PARTICLES, 1))
    part_rot = plant(jax.random.randint(arg_keys[3], (PARTICLES,), 0, ROT_CLS), jax.random.fold_in(arg_keys[3], 1), 0, ROT_CLS - 1).astype(jnp.int32)
    bucket = plant(jax.random.randint(arg_keys[4], (PARTICLES,), 0, BUCKETS), jax.random.fold_in(arg_keys[4], 1), 0, BUCKETS - 1).astype(jnp.int32)
    bucket_weights = jnp.clip(jnp.exp(jax.random.uniform(arg_keys[5], (BUCKETS,), jnp.float32, math.log(0.25), math.log(2.0))), 0.25, 2.0).astype(jnp.bfloat16)
    live_count = draw_live_count(jax.random.fold_in(arg_keys[7], 71), 0)
    return {"particles": particles, "references": references, "part_class": part_class, "part_rot": part_rot, "bucket": bucket, "bucket_weights": bucket_weights, "live_count": live_count}


def angle_grid(row_index, col_index, period):
    product = jnp.mod(row_index[:, None] * col_index[None, :], period)
    return product.astype(jnp.float32) * (2.0 * math.pi / period)


def forward_tables(box_size):
    index = jnp.arange(box_size, dtype=jnp.int32)
    theta = angle_grid(index, index, box_size)
    z_table = jnp.concatenate([jnp.cos(theta), -jnp.sin(theta)], axis=1)
    stacked = jnp.concatenate([jnp.cos(theta), jnp.sin(theta)], axis=0)
    return z_table, stacked


def inverse_tables(box_size, shift_count):
    freq_index = jnp.arange(box_size, dtype=jnp.int32)
    offsets = jnp.arange(shift_count, dtype=jnp.int32) - shift_count // 2
    theta = angle_grid(offsets, freq_index, box_size)
    inv_stacked = jnp.concatenate([jnp.cos(theta), jnp.sin(theta)], axis=0)
    inv_last = jnp.concatenate([jnp.cos(theta).T, -jnp.sin(theta).T], axis=0)
    return inv_stacked, inv_last


def combine(product_part, along_axis, sign_value):
    half_rows = product_part.shape[along_axis] // 2
    cos_part = lax.slice_in_dim(product_part, 0, half_rows, axis=along_axis)
    sin_part = lax.slice_in_dim(product_part, half_rows, 2 * half_rows, axis=along_axis)
    half_last = product_part.shape[-1] // 2
    real_part = cos_part[..., :half_last] + sign_value * sin_part[..., half_last:]
    imag_part = cos_part[..., half_last:] - sign_value * sin_part[..., :half_last]
    return jnp.concatenate([real_part, imag_part], axis=-1)


def yz_single(volume, z_table, stacked):
    box_size = volume.shape[0]
    z_part = jnp.dot(volume.reshape(box_size * box_size, box_size), z_table, preferred_element_type=jnp.float32).astype(jnp.bfloat16)
    grid_flat = z_part.reshape(box_size, box_size, 2 * box_size).transpose(1, 0, 2).reshape(box_size, 2 * box_size * box_size)
    y_part = jnp.dot(stacked, grid_flat, preferred_element_type=jnp.float32).reshape(2 * box_size, box_size, 2 * box_size)
    return combine(y_part, 0, 1.0).astype(jnp.bfloat16)


def x_single(grid_vol, stacked):
    box_size = grid_vol.shape[1]
    grid_flat = grid_vol.transpose(1, 0, 2).reshape(box_size, 2 * box_size * box_size)
    x_part = jnp.dot(stacked, grid_flat, preferred_element_type=jnp.float32).reshape(2 * box_size, box_size, 2 * box_size)
    return combine(x_part, 0, 1.0).astype(jnp.bfloat16)


def correlate(spectrum, partner):
    first_val = spectrum.astype(jnp.float32)
    second_val = partner.astype(jnp.float32)
    half_last = first_val.shape[-1] // 2
    real_part = first_val[..., :half_last] * second_val[..., :half_last] + first_val[..., half_last:] * second_val[..., half_last:]
    imag_part = first_val[..., half_last:] * second_val[..., :half_last] - first_val[..., :half_last] * second_val[..., half_last:]
    return jnp.concatenate([real_part, imag_part], axis=-1).astype(jnp.bfloat16)


def scores_single(cross_spec, inv_stacked, inv_last, score_scale):
    box_size = cross_spec.shape[0]
    shift_count = inv_last.shape[1]
    along_x = jnp.dot(inv_stacked, cross_spec.reshape(box_size, 2 * box_size * box_size), preferred_element_type=jnp.float32)
    along_x = combine(along_x.reshape(2 * shift_count, box_size, 2 * box_size), 0, -1.0).astype(jnp.bfloat16)
    flat_y = along_x.transpose(1, 0, 2).reshape(box_size, shift_count * 2 * box_size)
    along_y = jnp.dot(inv_stacked, flat_y, preferred_element_type=jnp.float32)
    along_y = combine(along_y.reshape(2 * shift_count, shift_count, 2 * box_size), 0, -1.0).astype(jnp.bfloat16)
    final_val = jnp.dot(along_y.reshape(shift_count * shift_count, 2 * box_size), inv_last, preferred_element_type=jnp.float32)
    final_val = final_val.reshape(shift_count, shift_count, shift_count).transpose(1, 0, 2)
    return (final_val * score_scale).reshape(shift_count * shift_count * shift_count)


def reference(particles, references, part_class, part_rot, bucket, bucket_weights, live_count):
    z32, stacked32 = forward_tables(BOX)
    z_table = z32.astype(jnp.bfloat16)
    stacked = stacked32.astype(jnp.bfloat16)
    inv32, last32 = inverse_tables(BOX, SHIFTS)
    inv_stacked = inv32.astype(jnp.bfloat16)
    inv_last = last32.astype(jnp.bfloat16)
    score_scale = float(BOX) ** -4.5
    insert_scale = float(BOX) ** -1.5
    ref_spectra = lax.map(lambda volume: x_single(yz_single(volume, z_table, stacked), stacked), references)
    place = jnp.arange(PARTICLES, dtype=jnp.int32)
    alive_rows = ((place % PART_DEV) < live_count[place // PART_DEV]).astype(jnp.float32)
    target = (part_class[:, 0] * ROT_CLS + part_rot).astype(jnp.int32)
    weight = bucket_weights[bucket].astype(jnp.float32) * alive_rows

    def visit(totals, visit_item):
        volume, index, weight_one, alive_one = visit_item
        grid_vol = yz_single(volume, z_table, stacked)
        spectrum = x_single(grid_vol, stacked)
        partner = lax.dynamic_index_in_dim(ref_spectra, index, 0, keepdims=False)
        row_scores = scores_single(correlate(spectrum, partner), inv_stacked, inv_last, score_scale) * alive_one
        current = lax.dynamic_index_in_dim(totals, index, 0, keepdims=False)
        totals = lax.dynamic_update_index_in_dim(totals, current + weight_one * grid_vol.astype(jnp.float32), index, 0)
        return totals, row_scores

    start_totals = jnp.zeros((ROTATIONS, BOX, BOX, 2 * BOX), jnp.float32)
    totals, scores = lax.scan(visit, start_totals, (particles, target, weight, alive_rows))

    def finish(row_block):
        x_part = jnp.einsum("bx,yxk->ybk", stacked32, row_block, precision=lax.Precision.HIGHEST)
        return combine(x_part, 1, 1.0) * insert_scale

    sums = lax.map(finish, totals)
    return scores, sums.transpose(1, 0, 2, 3)
```

```python
import math

import jax
import jax.numpy as jnp
import numpy as np
from jax import lax
from jax.experimental import pallas as pl
from jax.experimental.pallas import tpu as pltpu
from jax.sharding import PartitionSpec as P

BOX = 64
SHIFTS = 8
ROT_CLS = 4
CAP = 4
HALF = 33
KXP = 48
KXV = 40
PAIRS = BOX // 2
DOM = 16
BF = jnp.bfloat16
F32 = jnp.float32


def grid_cos_sin(rows, cols):
    theta = ((rows[:, None] * cols[None, :]) % BOX).astype(np.float64) * (2.0 * math.pi / BOX)
    return np.cos(theta), np.sin(theta)


def x_half_table():
    c, s = grid_cos_sin(np.arange(BOX), np.arange(BOX))
    out = np.zeros((2, KXP, BOX))
    out[0, :HALF] = c[:HALF]
    out[1, :HALF] = -s[:HALF]
    return out.reshape(2 * KXP, BOX)


def z_complex_table():
    c, s = grid_cos_sin(np.arange(BOX), np.arange(BOX))
    two = np.eye(2)
    return np.block([[np.kron(two, c), np.kron(two, -s)], [np.kron(two, s), np.kron(two, c)]])


def shift_tables():
    c, s = grid_cos_sin(np.arange(SHIFTS) - SHIFTS // 2, np.arange(BOX))
    fold = np.zeros((KXV,))
    fold[:HALF] = 2.0
    fold[0] = fold[HALF - 1] = 1.0
    ex = np.zeros((2 * SHIFTS, KXV))
    ex[:SHIFTS, :HALF] = c[:, :HALF]
    ex[SHIFTS:, :HALF] = s[:, :HALF]
    ex = ex * fold[None, :]
    wz = np.zeros((2, 4 * BOX, 128))
    wz[0, :, :SHIFTS] = np.concatenate([c.T, c.T, -s.T, -s.T], axis=0)
    wz[1, :, :SHIFTS] = np.concatenate([-s.T, -s.T, -c.T, -c.T], axis=0)
    return ex, wz.reshape(8 * BOX, 128)


def z_real_table():
    c, s = grid_cos_sin(np.arange(BOX), np.arange(BOX))
    return np.kron(np.eye(2), np.concatenate([c, -s], axis=1))


def y_table(rows):
    c, s = grid_cos_sin(np.arange(BOX), np.arange(BOX))
    order = np.concatenate([np.arange(0, BOX, 2), np.arange(1, BOX, 2)])
    both = np.concatenate([c[:, order], s[:, order]], axis=0)
    return np.kron(both, np.eye(rows))


def x_rows_table():
    c, s = grid_cos_sin(np.arange(BOX), np.arange(BOX))
    full = []
    for table in (c, s):
        spread = np.einsum(
            "rq,kdx->rkdqx", np.eye(ROT_CLS), table.reshape(BOX, DOM, BOX // DOM)
        ).reshape(ROT_CLS * BOX, ROT_CLS * BOX)
        high = spread.astype(np.float32).astype(BF)
        low = (spread.astype(np.float32) - high.astype(np.float32)).astype(BF)
        full += [high, low]
    return np.stack(full)


def z_stage(src, table, start, count):
    parts = []
    for j in range(start, start + count):
        lanes = slice(128 * j, 128 * (j + 1))
        parts.append(jnp.concatenate([src[0:KXP, lanes], src[KXP : 2 * KXP, lanes]], axis=1))
    return jnp.dot(jnp.concatenate(parts, axis=0), table, preferred_element_type=F32)


STEP = 8


def particle_kernel(count_ref, xp_ref, table_ref, out_ref):
    @pl.when(pl.program_id(0) < count_ref[0])
    def _():
        table = table_ref[...]
        for start in range(0, PAIRS, STEP):
            part = z_stage(xp_ref, table, start, STEP)
            out_ref[start * KXP : (start + STEP) * KXP, :] = part.astype(BF)

    @pl.when(pl.program_id(0) >= count_ref[0])
    def _():
        out_ref[...] = jnp.zeros_like(out_ref)


def score_kernel(count_ref, zp_ref, xr_ref, table_ref, ex_ref, wz_ref, out_ref, p_s, r_s, o_s, a_s):
    @pl.when(pl.program_id(0) < count_ref[0])
    def _():
        table = table_ref[...]
        for start in range(0, PAIRS, STEP):
            part = z_stage(xr_ref, table, start, STEP)
            part = part.astype(BF).astype(F32).reshape(STEP, KXP, 4 * BOX)
            r_s[start : start + STEP] = part[:, :KXV, :]
            mine = zp_ref[start * KXP : (start + STEP) * KXP, :].astype(F32)
            p_s[start : start + STEP] = mine.reshape(STEP, KXP, 4 * BOX)[:, :KXV, :]
        first = lax.broadcasted_iota(jnp.int32, (KXV, 128), 1) < BOX
        for j in range(PAIRS):
            for half in range(2):
                lanes = slice(128 * half, 128 * (half + 1))
                now = r_s[j, :, lanes]
                before = r_s[(j - 1) % PAIRS, :, lanes]
                o_s[j, :, lanes] = pltpu.roll(jnp.where(first, now, before), BOX, 1)

        def column(col, carry):
            rows = pl.ds(pl.multiple_of(col * 8, 8), 8)
            re = [jnp.zeros((8, 128), F32) for _ in range(SHIFTS)]
            im = [jnp.zeros((8, 128), F32) for _ in range(SHIFTS)]
            for j in range(PAIRS):
                pr = p_s[j, rows, 0:128]
                pi = p_s[j, rows, 128:256]
                for u in range(-2, 2):
                    m = (j - u) % PAIRS
                    for odd, src in ((0, r_s), (1, o_s)):
                        t = 2 * u + odd + SHIFTS // 2
                        rr = src[m, rows, 0:128]
                        ri = src[m, rows, 128:256]
                        re[t] = re[t] + (pr * rr + pi * ri)
                        im[t] = im[t] + (pi * rr - pr * ri)
            for t in range(SHIFTS):
                a_s[t, rows, 0:128] = re[t]
                a_s[t, rows, 128:256] = im[t]
            return carry

        lax.fori_loop(0, KXV // 8, column, 0)
        ex = ex_ref[...]
        along_x = [
            jnp.dot(ex, a_s[t].astype(BF), preferred_element_type=F32) for t in range(SHIFTS)
        ]
        cos_rows = jnp.concatenate([u[:SHIFTS] for u in along_x], axis=0).astype(BF)
        sin_rows = jnp.concatenate([u[SHIFTS:] for u in along_x], axis=0).astype(BF)
        both = jnp.concatenate([cos_rows, sin_rows], axis=1)
        final = jnp.dot(both, wz_ref[...], preferred_element_type=F32)
        out_ref[...] = final * (float(BOX) ** -3.5)

    @pl.when(pl.program_id(0) >= count_ref[0])
    def _():
        out_ref[...] = jnp.zeros_like(out_ref)


def yz_kernel(*refs):
    own_ref, part_refs, (z_ref, y_ref, out_ref) = refs[0], refs[1:8], refs[8:]
    total = own_ref[...].astype(F32)
    for part in part_refs:
        total = total + part[...].astype(F32)
    total = total.astype(BF)
    stacked = jnp.concatenate([total[:, 128 * j : 128 * (j + 1)] for j in range(PAIRS)], axis=0)
    z_part = jnp.dot(stacked, z_ref[...], preferred_element_type=F32).astype(BF)
    z_part = jnp.concatenate([z_part[:, :128], z_part[:, 128:]], axis=0)
    y_part = jnp.dot(y_ref[...], z_part, preferred_element_type=F32)
    half_rows = y_part.shape[0] // 2
    turned = pltpu.roll(y_part[half_rows:], BOX, 1)
    first = lax.broadcasted_iota(jnp.int32, turned.shape, 1) < BOX
    out_ref[...] = (y_part[:half_rows] + jnp.where(first, turned, -turned)).astype(BF)


def x_rows_kernel(rows_ref, table_ref, out_ref):
    rows = ROT_CLS * (BOX // DOM)
    first = lax.broadcasted_iota(jnp.int32, (ROT_CLS * BOX, 128), 1) < BOX
    for ky in range(BOX // DOM):
        grid = rows_ref[:, ky * rows : (ky + 1) * rows, :].reshape(ROT_CLS * BOX, 128)
        cos_part = jnp.dot(table_ref[0], grid, preferred_element_type=F32)
        cos_part = cos_part + jnp.dot(table_ref[1], grid, preferred_element_type=F32)
        sin_part = jnp.dot(table_ref[2], grid, preferred_element_type=F32)
        sin_part = sin_part + jnp.dot(table_ref[3], grid, preferred_element_type=F32)
        turned = pltpu.roll(sin_part, BOX, 1)
        total = (cos_part + jnp.where(first, turned, -turned)) * (float(BOX) ** -1.5)
        out_ref[ky] = total.reshape(ROT_CLS, BOX, 128)


VMEM = pl.BlockSpec(memory_space=pltpu.VMEM)
SMEM = pl.BlockSpec(memory_space=pltpu.SMEM)
PARAMS = pltpu.CompilerParams(vmem_limit_bytes=40 * 1024 * 1024)


def shards(particles, references, part_class, part_rot, bucket, bucket_weights, live_count):
    block_size = particles.shape[0]
    planes = references.shape[1]
    voxels = BOX * BOX
    dom = lax.axis_index("dom")
    owner = lax.axis_index("rot")
    chip, core = dom // 2, dom % 2

    all_refs = lax.all_gather(
        references.reshape(ROT_CLS * planes, voxels), "dom", axis=0, tiled=True
    )

    rows_all = jnp.arange(block_size, dtype=jnp.int32)
    classes = part_class[:, 0]
    alive = rows_all < live_count[0]
    same = (classes[:, None] == classes[None, :]) & alive[None, :]
    rank = jnp.sum((same & (rows_all[None, :] < rows_all[:, None])).astype(jnp.int32), axis=1)
    mine = (classes == owner) & alive
    count = jnp.sum(mine.astype(jnp.int32)).reshape(1)
    bucket_ids = jnp.arange(bucket_weights.shape[0], dtype=jnp.int32)
    level = jnp.where(
        bucket[:, None] == bucket_ids[None, :], bucket_weights[None, :].astype(F32), 0.0
    )
    weight = jnp.where(mine, jnp.sum(level, axis=1), 0.0)
    slot_ids = jnp.arange(CAP, dtype=jnp.int32)
    picked = (rank[None, :] == slot_ids[:, None]) & mine[None, :]
    slot_rot = jnp.sum(jnp.where(picked, part_rot[None, :], 0), axis=1)

    flat = particles.reshape(block_size * BOX, voxels)

    row = jnp.arange(DOM * ROT_CLS * planes, dtype=jnp.int32)
    row_x = row % planes
    row_r = (row // planes) % ROT_CLS
    row_chip = (row // (planes * ROT_CLS)) % 8
    row_core = row // (planes * ROT_CLS * 8)
    to_z = (chip // 2 + row_chip // 2) % 4
    to_y = (chip % 2) ^ (row_chip % 2)
    to_dom = (to_z * 2 + to_y) * 2 + (core ^ row_core)
    want_x = to_dom * planes + row_x
    col = jnp.arange(block_size * BOX, dtype=jnp.int32)
    col_weight = jnp.repeat(weight, BOX, total_repeat_length=block_size * BOX)
    col_rot = jnp.repeat(part_rot, BOX, total_repeat_length=block_size * BOX)
    spread = jnp.where(
        (want_x[:, None] == (col % BOX)[None, :]) & (row_r[:, None] == col_rot[None, :]),
        col_weight[None, :],
        0.0,
    ).astype(BF)
    to_send = jnp.dot(spread, flat, preferred_element_type=F32).astype(BF)
    half_rows = to_send.shape[0] // 2
    other = lax.ppermute(to_send[half_rows:], "dom", [(i, i ^ 1) for i in range(DOM)])
    pair_sum = (to_send[:half_rows].astype(F32) + other.astype(F32)).astype(BF)
    per_chip = ROT_CLS * planes
    arrived = []
    for k in range(1, 8):
        route = []
        for i in range(DOM):
            z, y, c = i // 4, (i // 2) % 2, i % 2
            route.append((i, ((z + k // 2) % 4) * 4 + (y ^ (k % 2)) * 2 + c))
        arrived.append(lax.ppermute(pair_sum[k * per_chip : (k + 1) * per_chip], "dom", route))

    z_real = jnp.asarray(z_real_table(), F32).astype(BF)
    y_full = jnp.asarray(y_table(per_chip).astype(BF))
    grids = pl.pallas_call(
        yz_kernel,
        out_shape=jax.ShapeDtypeStruct((BOX * per_chip, 2 * BOX), BF),
        in_specs=[VMEM] * 10,
        out_specs=VMEM,
        compiler_params=PARAMS,
        name="yz_planes",
    )(pair_sum[:per_chip], *arrived, z_real, y_full)
    by_rows = lax.all_to_all(grids, "dom", 0, 0, tiled=True)
    sums = pl.pallas_call(
        x_rows_kernel,
        out_shape=jax.ShapeDtypeStruct((BOX // DOM, ROT_CLS, BOX, 2 * BOX), F32),
        in_specs=[VMEM] * 2,
        out_specs=VMEM,
        compiler_params=PARAMS,
        name="x_rows",
    )(by_rows.reshape(DOM, BOX // DOM * per_chip, 2 * BOX), jnp.asarray(x_rows_table()))

    x_half = jnp.asarray(x_half_table().astype(BF))
    pick = (
        picked.astype(BF)[:, None, :, None] * x_half[None, :, None, :]
    ).reshape(CAP * 2 * KXP, block_size * BOX)
    along_x = jnp.dot(pick, flat, preferred_element_type=F32).astype(BF)
    z_table = jnp.asarray(z_complex_table().astype(BF))
    spectra = pl.pallas_call(
        particle_kernel,
        out_shape=jax.ShapeDtypeStruct((CAP, PAIRS * KXP, 4 * BOX), BF),
        grid=(CAP,),
        in_specs=[
            SMEM,
            pl.BlockSpec((None, 2 * KXP, voxels), lambda s: (s, 0, 0)),
            pl.BlockSpec((4 * BOX, 4 * BOX), lambda s: (0, 0)),
        ],
        out_specs=pl.BlockSpec((None, PAIRS * KXP, 4 * BOX), lambda s: (s, 0, 0)),
        compiler_params=PARAMS,
        name="particle_z",
    )(count, along_x.reshape(CAP, 2 * KXP, voxels), z_table)

    rot_ids = jnp.arange(ROT_CLS, dtype=jnp.int32)
    choose = (slot_rot[:, None] == rot_ids[None, :]).astype(BF)
    pick_ref = (
        choose[:, None, None, :, None] * x_half.reshape(1, 2 * KXP, DOM, 1, planes)
    ).reshape(CAP * 2 * KXP, DOM * per_chip)
    ref_x = jnp.dot(pick_ref, all_refs, preferred_element_type=F32).astype(BF)
    ex, wz = shift_tables()
    slots = pl.pallas_call(
        score_kernel,
        out_shape=jax.ShapeDtypeStruct((CAP, SHIFTS * SHIFTS, 128), F32),
        grid=(CAP,),
        in_specs=[
            SMEM,
            pl.BlockSpec((None, PAIRS * KXP, 4 * BOX), lambda s: (s, 0, 0)),
            pl.BlockSpec((None, 2 * KXP, voxels), lambda s: (s, 0, 0)),
            pl.BlockSpec((4 * BOX, 4 * BOX), lambda s: (0, 0)),
            pl.BlockSpec((2 * SHIFTS, KXV), lambda s: (0, 0)),
            pl.BlockSpec((8 * BOX, 128), lambda s: (0, 0)),
        ],
        out_specs=pl.BlockSpec((None, SHIFTS * SHIFTS, 128), lambda s: (s, 0, 0)),
        scratch_shapes=[
            pltpu.VMEM((PAIRS, KXV, 4 * BOX), F32),
            pltpu.VMEM((PAIRS, KXV, 4 * BOX), F32),
            pltpu.VMEM((PAIRS, KXV, 4 * BOX), F32),
            pltpu.VMEM((SHIFTS, KXV, 4 * BOX), F32),
        ],
        compiler_params=PARAMS,
        name="slot_scores",
    )(
        count,
        spectra,
        ref_x.reshape(CAP, 2 * KXP, voxels),
        z_table,
        jnp.asarray(ex.astype(BF)),
        jnp.asarray(wz.astype(BF)),
    )
    slot_scores = slots[:, :, :SHIFTS].reshape(CAP, SHIFTS, SHIFTS, SHIFTS)
    slot_scores = slot_scores.transpose(0, 2, 1, 3).reshape(CAP, SHIFTS**3)
    everywhere = lax.all_to_all(
        jnp.tile(slot_scores, (8, 1)), "rot", 0, 0, tiled=True
    )
    place = classes * CAP + rank
    found = (place[:, None] == jnp.arange(8 * CAP, dtype=jnp.int32)[None, :]) & alive[:, None]
    scores = jnp.sum(jnp.where(found[:, :, None], everywhere[None, :, :], 0.0), axis=1)
    return (scores, sums)


def solution(mesh):
    return jax.shard_map(
        shards,
        mesh=mesh,
        in_specs=(
            P("dom", None, None),
            P("rot", "dom", None),
            P("dom", None),
            P("dom"),
            P("dom"),
            P(),
            P("dom"),
        ),
        out_specs=(P("dom", None), P("dom", "rot", None, None)),
        check_vma=False,
    )
```

```python
import math

import jax
import jax.numpy as jnp
import numpy as np
from jax import lax
from jax.experimental import pallas as pl
from jax.experimental.pallas import tpu as pltpu
from jax.sharding import PartitionSpec as P

BOX = 64
SHIFTS = 8
ROT_CLS = 4
CAP = 4
HALF = 33
KXP = 48
KXV = 40
PAIRS = BOX // 2
DOM = 16
CHIPS = DOM // 2
SAME_CORE = [[2 * chip + core for chip in range(CHIPS)] for core in range(2)]
BF = jnp.bfloat16
F32 = jnp.float32


def grid_cos_sin(rows, cols):
    theta = ((rows[:, None] * cols[None, :]) % BOX).astype(np.float64) * (2.0 * math.pi / BOX)
    return np.cos(theta), np.sin(theta)


def x_half_table():
    c, s = grid_cos_sin(np.arange(BOX), np.arange(BOX))
    out = np.zeros((2, KXP, BOX))
    out[0, :HALF] = c[:HALF]
    out[1, :HALF] = -s[:HALF]
    return out.reshape(2 * KXP, BOX)


def z_complex_table():
    c, s = grid_cos_sin(np.arange(BOX), np.arange(BOX))
    two = np.eye(2)
    return np.block([[np.kron(two, c), np.kron(two, -s)], [np.kron(two, s), np.kron(two, c)]])


def shift_tables():
    c, s = grid_cos_sin(np.arange(SHIFTS) - SHIFTS // 2, np.arange(BOX))
    fold = np.zeros((KXV,))
    fold[:HALF] = 2.0
    fold[0] = fold[HALF - 1] = 1.0
    ex = np.zeros((2 * SHIFTS, KXV))
    ex[:SHIFTS, :HALF] = c[:, :HALF]
    ex[SHIFTS:, :HALF] = s[:, :HALF]
    ex = ex * fold[None, :]
    wz = np.zeros((2, 4 * BOX, 128))
    wz[0, :, :SHIFTS] = np.concatenate([c.T, c.T, -s.T, -s.T], axis=0)
    wz[1, :, :SHIFTS] = np.concatenate([-s.T, -s.T, -c.T, -c.T], axis=0)
    return ex, wz.reshape(8 * BOX, 128)


def z_real_table():
    c, s = grid_cos_sin(np.arange(BOX), np.arange(BOX))
    return np.kron(np.eye(2), np.concatenate([c, -s], axis=1))


def y_table(rows):
    c, s = grid_cos_sin(np.arange(BOX), np.arange(BOX))
    order = np.concatenate([np.arange(0, BOX, 2), np.arange(1, BOX, 2)])
    both = np.concatenate([c[:, order], s[:, order]], axis=0)
    return np.kron(both, np.eye(rows))


def x_rows_table():
    c, s = grid_cos_sin(np.arange(BOX), np.arange(BOX))
    full = []
    for table in (c, s):
        spread = np.einsum(
            "rq,kdx->rkdqx", np.eye(ROT_CLS), table.reshape(BOX, DOM, BOX // DOM)
        ).reshape(ROT_CLS * BOX, ROT_CLS * BOX)
        high = spread.astype(np.float32).astype(BF)
        low = (spread.astype(np.float32) - high.astype(np.float32)).astype(BF)
        full += [high, low]
    return np.stack(full)


def z_stage(src, table, start, count):
    parts = []
    for j in range(start, start + count):
        lanes = slice(128 * j, 128 * (j + 1))
        parts.append(jnp.concatenate([src[0:KXP, lanes], src[KXP : 2 * KXP, lanes]], axis=1))
    return jnp.dot(jnp.concatenate(parts, axis=0), table, preferred_element_type=F32)


STEP = 8
CHUNK = 4


def front_kernel(own_ref, pick_ref, flat_ref, table_ref, own_out, spectra_out):
    flat = flat_ref[...]
    own_out[...] = jnp.dot(own_ref[...], flat, preferred_element_type=F32).astype(BF)
    along_x = jnp.dot(pick_ref[...], flat, preferred_element_type=F32).astype(BF)
    table = table_ref[...]
    for slot in range(CAP):
        part = z_stage(along_x[slot * 2 * KXP : (slot + 1) * 2 * KXP], table, 0, CHUNK)
        spectra_out[slot] = part.astype(BF)


def score_kernel(
    count_ref,
    zp_ref,
    pick_own_ref,
    pick_other_ref,
    own_ref,
    other_ref,
    table_ref,
    ex_ref,
    wz_ref,
    out_ref,
    x_s,
    p_s,
    r_s,
    o_s,
    a_s,
):
    slot = pl.program_id(0)

    @pl.when((slot == 0) & (count_ref[0] > 0))
    def _():
        for start in range(0, BOX * BOX, 512):
            lanes = slice(start, start + 512)
            part = jnp.dot(pick_own_ref[...], own_ref[:, lanes], preferred_element_type=F32)
            part = part + jnp.dot(
                pick_other_ref[...], other_ref[:, lanes], preferred_element_type=F32
            )
            x_s[:, :, lanes] = part.astype(BF).reshape(CAP, 2 * KXP, 512)

    @pl.when(slot < count_ref[0])
    def _():
        table = table_ref[...]
        xr = x_s.at[slot]
        for start in range(0, PAIRS, STEP):
            part = z_stage(xr, table, start, STEP)
            part = part.astype(BF).astype(F32).reshape(STEP, KXP, 4 * BOX)
            r_s[start : start + STEP] = part[:, :KXV, :]
            mine = zp_ref[start * KXP : (start + STEP) * KXP, :].astype(F32)
            p_s[start : start + STEP] = mine.reshape(STEP, KXP, 4 * BOX)[:, :KXV, :]
        first = lax.broadcasted_iota(jnp.int32, (KXV, 128), 1) < BOX
        for j in range(PAIRS):
            for half in range(2):
                lanes = slice(128 * half, 128 * (half + 1))
                now = r_s[j, :, lanes]
                before = r_s[(j - 1) % PAIRS, :, lanes]
                o_s[j, :, lanes] = pltpu.roll(jnp.where(first, now, before), BOX, 1)

        def column(col, carry):
            rows = pl.ds(pl.multiple_of(col * 8, 8), 8)
            re = [jnp.zeros((8, 128), F32) for _ in range(SHIFTS)]
            im = [jnp.zeros((8, 128), F32) for _ in range(SHIFTS)]
            for j in range(PAIRS):
                pr = p_s[j, rows, 0:128]
                pi = p_s[j, rows, 128:256]
                for u in range(-2, 2):
                    m = (j - u) % PAIRS
                    for odd, src in ((0, r_s), (1, o_s)):
                        t = 2 * u + odd + SHIFTS // 2
                        rr = src[m, rows, 0:128]
                        ri = src[m, rows, 128:256]
                        re[t] = re[t] + (pr * rr + pi * ri)
                        im[t] = im[t] + (pi * rr - pr * ri)
            for t in range(SHIFTS):
                a_s[t, rows, 0:128] = re[t]
                a_s[t, rows, 128:256] = im[t]
            return carry

        lax.fori_loop(0, KXV // 8, column, 0)
        ex = ex_ref[...]
        along_x = [
            jnp.dot(ex, a_s[t].astype(BF), preferred_element_type=F32) for t in range(SHIFTS)
        ]
        cos_rows = jnp.concatenate([u[:SHIFTS] for u in along_x], axis=0).astype(BF)
        sin_rows = jnp.concatenate([u[SHIFTS:] for u in along_x], axis=0).astype(BF)
        both = jnp.concatenate([cos_rows, sin_rows], axis=1)
        final = jnp.dot(both, wz_ref[...], preferred_element_type=F32)
        out_ref[...] = final * (float(BOX) ** -3.5)

    @pl.when(slot >= count_ref[0])
    def _():
        out_ref[...] = jnp.zeros_like(out_ref)


def yz_kernel(parts_ref, z_ref, y_ref, out_ref):
    rows = parts_ref.shape[0] // CHIPS
    total = parts_ref[0:rows].astype(F32)
    for chip in range(1, CHIPS):
        total = total + parts_ref[chip * rows : (chip + 1) * rows].astype(F32)
    total = total.astype(BF)
    stacked = jnp.concatenate([total[:, 128 * j : 128 * (j + 1)] for j in range(PAIRS)], axis=0)
    z_part = jnp.dot(stacked, z_ref[...], preferred_element_type=F32).astype(BF)
    z_part = jnp.concatenate([z_part[:, :128], z_part[:, 128:]], axis=0)
    y_part = jnp.dot(y_ref[...], z_part, preferred_element_type=F32)
    half_rows = y_part.shape[0] // 2
    turned = pltpu.roll(y_part[half_rows:], BOX, 1)
    first = lax.broadcasted_iota(jnp.int32, turned.shape, 1) < BOX
    out_ref[...] = (y_part[:half_rows] + jnp.where(first, turned, -turned)).astype(BF)


def x_rows_kernel(rows_ref, table_ref, out_ref):
    rows = ROT_CLS * (BOX // DOM)
    first = lax.broadcasted_iota(jnp.int32, (ROT_CLS * BOX, 128), 1) < BOX
    for ky in range(BOX // DOM):
        grid = rows_ref[:, ky * rows : (ky + 1) * rows, :].reshape(ROT_CLS * BOX, 128)
        cos_part = jnp.dot(table_ref[0], grid, preferred_element_type=F32)
        cos_part = cos_part + jnp.dot(table_ref[1], grid, preferred_element_type=F32)
        sin_part = jnp.dot(table_ref[2], grid, preferred_element_type=F32)
        sin_part = sin_part + jnp.dot(table_ref[3], grid, preferred_element_type=F32)
        turned = pltpu.roll(sin_part, BOX, 1)
        total = (cos_part + jnp.where(first, turned, -turned)) * (float(BOX) ** -1.5)
        out_ref[ky] = total.reshape(ROT_CLS, BOX, 128)


VMEM = pl.BlockSpec(memory_space=pltpu.VMEM)
SMEM = pl.BlockSpec(memory_space=pltpu.SMEM)
PARAMS = pltpu.CompilerParams(vmem_limit_bytes=40 * 1024 * 1024)


def shards(particles, references, part_class, part_rot, bucket, bucket_weights, live_count):
    block_size = particles.shape[0]
    planes = references.shape[1]
    voxels = BOX * BOX
    per_chip = ROT_CLS * planes
    columns = block_size * BOX
    core = lax.axis_index("dom") % 2
    owner = lax.axis_index("rot")
    to_other = [(i, i ^ 1) for i in range(DOM)]

    mine_refs = references.reshape(per_chip, voxels)
    refs_own = lax.all_to_all(
        jnp.tile(mine_refs, (CHIPS, 1)), "dom", 0, 0, tiled=True, axis_index_groups=SAME_CORE
    )
    refs_other = lax.ppermute(refs_own, "dom", to_other)

    rows_all = jnp.arange(block_size, dtype=jnp.int32)
    classes = part_class[:, 0]
    alive = rows_all < live_count[0]
    same = (classes[:, None] == classes[None, :]) & alive[None, :]
    rank = jnp.sum((same & (rows_all[None, :] < rows_all[:, None])).astype(jnp.int32), axis=1)
    mine = (classes == owner) & alive
    count = jnp.sum(mine.astype(jnp.int32)).reshape(1)
    bucket_ids = jnp.arange(bucket_weights.shape[0], dtype=jnp.int32)
    level = jnp.where(
        bucket[:, None] == bucket_ids[None, :], bucket_weights[None, :].astype(F32), 0.0
    )
    weight = jnp.where(mine, jnp.sum(level, axis=1), 0.0)
    slot_of = jnp.where(mine, rank, -1)

    col = np.arange(columns)
    col_is = jnp.asarray(col[None, :] // BOX == np.arange(block_size)[:, None])
    col_weight = jnp.sum(jnp.where(col_is, weight[:, None], 0.0), axis=0)
    col_rot = jnp.sum(jnp.where(col_is, part_rot[:, None], 0), axis=0)
    col_slot = jnp.sum(jnp.where(col_is, slot_of[:, None], 0), axis=0)

    flat = particles.reshape(columns, voxels)
    row = np.arange(CHIPS * per_chip)
    row_chip, row_r, row_x = row // per_chip, (row // planes) % ROT_CLS, row % planes
    row_r = jnp.asarray(row_r.astype(np.int32))

    def spread(to_core):
        want_x = jnp.asarray((row_chip * 2 * planes + row_x).astype(np.int32)) + to_core * planes
        hit = want_x[:, None] == jnp.asarray((col % BOX).astype(np.int32))[None, :]
        return jnp.where(hit & (row_r[:, None] == col_rot[None, :]), col_weight[None, :], 0.0).astype(BF)

    to_send = jnp.dot(spread(1 - core), flat, preferred_element_type=F32).astype(BF)
    other = lax.ppermute(to_send, "dom", to_other)

    x_half = x_half_table()
    slot_rows = np.arange(CAP * 2 * KXP) // (2 * KXP)
    slot_rows = jnp.asarray(slot_rows.astype(np.int32))
    pick = jnp.where(
        slot_rows[:, None] == col_slot[None, :],
        jnp.asarray(np.tile(x_half, (CAP, block_size)).astype(BF)),
        jnp.zeros((), BF),
    )
    z_table = jnp.asarray(z_complex_table().astype(BF))
    own, spectra = pl.pallas_call(
        front_kernel,
        out_shape=(
            jax.ShapeDtypeStruct((CHIPS * per_chip, voxels), BF),
            jax.ShapeDtypeStruct((CAP, PAIRS * KXP, 4 * BOX), BF),
        ),
        grid=(PAIRS // CHUNK,),
        in_specs=[
            pl.BlockSpec((CHIPS * per_chip, columns), lambda i: (0, 0)),
            pl.BlockSpec((CAP * 2 * KXP, columns), lambda i: (0, 0)),
            pl.BlockSpec((columns, 128 * CHUNK), lambda i: (0, i)),
            pl.BlockSpec((4 * BOX, 4 * BOX), lambda i: (0, 0)),
        ],
        out_specs=(
            pl.BlockSpec((CHIPS * per_chip, 128 * CHUNK), lambda i: (0, i)),
            pl.BlockSpec((CAP, CHUNK * KXP, 4 * BOX), lambda i: (0, i, 0)),
        ),
        compiler_params=PARAMS,
        name="front",
    )(spread(core), pick, flat, z_table)
    pair_sum = (own.astype(F32) + other.astype(F32)).astype(BF)
    arrived = lax.all_to_all(pair_sum, "dom", 0, 0, tiled=True, axis_index_groups=SAME_CORE)

    slot_ids = jnp.arange(CAP, dtype=jnp.int32)
    slot_rot = jnp.sum(jnp.where(slot_of[None, :] == slot_ids[:, None], part_rot[None, :], 0), axis=1)
    row_rot = jnp.sum(jnp.where(slot_rows[:, None] == slot_ids[None, :], slot_rot[None, :], 0), axis=1)
    by_core = x_half.reshape(2 * KXP, CHIPS, 2, 1, planes)
    by_core = np.broadcast_to(by_core, (2 * KXP, CHIPS, 2, ROT_CLS, planes))
    by_core = by_core.transpose(2, 0, 1, 3, 4).reshape(2, 2 * KXP, CHIPS * per_chip)
    by_core = jnp.asarray(np.tile(by_core, (1, CAP, 1)).astype(BF))
    right = row_rot[:, None] == row_r[None, :]
    pick_own = jnp.where(right, jnp.where(core == 0, by_core[0], by_core[1]), jnp.zeros((), BF))
    pick_other = jnp.where(right, jnp.where(core == 0, by_core[1], by_core[0]), jnp.zeros((), BF))
    ex, wz = shift_tables()

    def whole(*shape):
        return pl.BlockSpec(shape, lambda s: (0,) * len(shape))

    slots = pl.pallas_call(
        score_kernel,
        out_shape=jax.ShapeDtypeStruct((CAP, SHIFTS * SHIFTS, 128), F32),
        grid=(CAP,),
        in_specs=[
            SMEM,
            pl.BlockSpec((None, PAIRS * KXP, 4 * BOX), lambda s: (s, 0, 0)),
            whole(CAP * 2 * KXP, CHIPS * per_chip),
            whole(CAP * 2 * KXP, CHIPS * per_chip),
            whole(CHIPS * per_chip, voxels),
            whole(CHIPS * per_chip, voxels),
            whole(4 * BOX, 4 * BOX),
            whole(2 * SHIFTS, KXV),
            whole(8 * BOX, 128),
        ],
        out_specs=pl.BlockSpec((None, SHIFTS * SHIFTS, 128), lambda s: (s, 0, 0)),
        scratch_shapes=[
            pltpu.VMEM((CAP, 2 * KXP, voxels), BF),
            pltpu.VMEM((PAIRS, KXV, 4 * BOX), F32),
            pltpu.VMEM((PAIRS, KXV, 4 * BOX), F32),
            pltpu.VMEM((PAIRS, KXV, 4 * BOX), F32),
            pltpu.VMEM((SHIFTS, KXV, 4 * BOX), F32),
        ],
        compiler_params=PARAMS,
        name="slot_scores",
    )(
        count,
        spectra,
        pick_own,
        pick_other,
        refs_own,
        refs_other,
        z_table,
        jnp.asarray(ex.astype(BF)),
        jnp.asarray(wz.astype(BF)),
    )
    slot_scores = slots[:, :, :SHIFTS].reshape(CAP, SHIFTS, SHIFTS, SHIFTS)
    slot_scores = slot_scores.transpose(0, 2, 1, 3).reshape(CAP, SHIFTS**3)
    everywhere = lax.all_to_all(jnp.tile(slot_scores, (8, 1)), "rot", 0, 0, tiled=True)
    place = classes * CAP + rank
    found = (place[:, None] == jnp.arange(8 * CAP, dtype=jnp.int32)[None, :]) & alive[:, None]
    scores = jnp.sum(jnp.where(found[:, :, None], everywhere[None, :, :], 0.0), axis=1)

    z_real = jnp.asarray(z_real_table().astype(BF))
    y_full = jnp.asarray(y_table(per_chip).astype(BF))
    grids = pl.pallas_call(
        yz_kernel,
        out_shape=jax.ShapeDtypeStruct((BOX * per_chip, 2 * BOX), BF),
        in_specs=[VMEM] * 3,
        out_specs=VMEM,
        compiler_params=PARAMS,
        name="yz_planes",
    )(arrived, z_real, y_full)
    by_rows = lax.all_to_all(grids, "dom", 0, 0, tiled=True)
    sums = pl.pallas_call(
        x_rows_kernel,
        out_shape=jax.ShapeDtypeStruct((BOX // DOM, ROT_CLS, BOX, 2 * BOX), F32),
        in_specs=[VMEM] * 2,
        out_specs=VMEM,
        compiler_params=PARAMS,
        name="x_rows",
    )(by_rows.reshape(DOM, BOX // DOM * per_chip, 2 * BOX), jnp.asarray(x_rows_table()))
    return (scores, sums)


def solution(mesh):
    return jax.shard_map(
        shards,
        mesh=mesh,
        in_specs=(
            P("dom", None, None),
            P("rot", "dom", None),
            P("dom", None),
            P("dom"),
            P("dom"),
            P(),
            P("dom"),
        ),
        out_specs=(P("dom", None), P("dom", "rot", None, None)),
        check_vma=False,
    )
```

```python
import math

import jax
import jax.numpy as jnp
import numpy as np
from jax import lax
from jax.experimental import pallas as pl
from jax.experimental.pallas import tpu as pltpu
from jax.sharding import PartitionSpec as P

BOX = 64
SHIFTS = 8
ROT_CLS = 4
CAP = 4
HALF = 33
KXP = 48
KXV = 40
PAIRS = BOX // 2
DOM = 16
CHIPS = DOM // 2
SAME_CORE = [[2 * chip + core for chip in range(CHIPS)] for core in range(2)]
BF = jnp.bfloat16
F32 = jnp.float32


def grid_cos_sin(rows, cols):
    theta = ((rows[:, None] * cols[None, :]) % BOX).astype(np.float64) * (2.0 * math.pi / BOX)
    return np.cos(theta), np.sin(theta)


def x_half_table():
    c, s = grid_cos_sin(np.arange(BOX), np.arange(BOX))
    out = np.zeros((2, KXP, BOX))
    out[0, :HALF] = c[:HALF]
    out[1, :HALF] = -s[:HALF]
    return out.reshape(2 * KXP, BOX)


def z_complex_table():
    c, s = grid_cos_sin(np.arange(BOX), np.arange(BOX))
    two = np.eye(2)
    return np.block([[np.kron(two, c), np.kron(two, -s)], [np.kron(two, s), np.kron(two, c)]])


def shift_tables():
    c, s = grid_cos_sin(np.arange(SHIFTS) - SHIFTS // 2, np.arange(BOX))
    fold = np.zeros((KXV,))
    fold[:HALF] = 2.0
    fold[0] = fold[HALF - 1] = 1.0
    ex = np.zeros((2 * SHIFTS, KXV))
    ex[:SHIFTS, :HALF] = c[:, :HALF]
    ex[SHIFTS:, :HALF] = s[:, :HALF]
    ex = ex * fold[None, :]
    wz = np.zeros((2, 4 * BOX, 128))
    wz[0, :, :SHIFTS] = np.concatenate([c.T, c.T, -s.T, -s.T], axis=0)
    wz[1, :, :SHIFTS] = np.concatenate([-s.T, -s.T, -c.T, -c.T], axis=0)
    return ex, wz.reshape(8 * BOX, 128)


def z_real_table():
    c, s = grid_cos_sin(np.arange(BOX), np.arange(BOX))
    return np.kron(np.eye(2), np.concatenate([c, -s], axis=1))


def y_table():
    c, s = grid_cos_sin(np.arange(BOX), np.arange(BOX))
    return np.concatenate([c, s], axis=0)


def x_rows_table():
    c, s = grid_cos_sin(np.arange(BOX), np.arange(BOX))
    full = []
    for table in (c, s):
        spread = np.einsum(
            "rq,kdx->rkdqx", np.eye(ROT_CLS), table.reshape(BOX, DOM, BOX // DOM)
        ).reshape(ROT_CLS * BOX, ROT_CLS * BOX)
        high = spread.astype(np.float32).astype(BF)
        low = (spread.astype(np.float32) - high.astype(np.float32)).astype(BF)
        full += [high, low]
    return np.stack(full)


def z_stage(src, table, start, count):
    parts = []
    for j in range(start, start + count):
        lanes = slice(128 * j, 128 * (j + 1))
        parts.append(jnp.concatenate([src[0:KXP, lanes], src[KXP : 2 * KXP, lanes]], axis=1))
    return jnp.dot(jnp.concatenate(parts, axis=0), table, preferred_element_type=F32)


STEP = 8
CHUNK = 4
STEPS = PAIRS // CHUNK
PLANES = BOX // DOM
PER_CHIP = ROT_CLS * PLANES
SEND = CHIPS * PER_CHIP


def send_kernel(
    class_ref,
    rot_ref,
    bucket_ref,
    live_ref,
    level_ref,
    x_ref,
    x_ref_table,
    flat_ref,
    send_out,
    spread_out,
    pick_out,
    pick_own_out,
    pick_other_out,
    count_out,
    spread_s,
):
    particles, columns = class_ref.shape[0], flat_ref.shape[0]

    @pl.when(pl.program_id(0) == 0)
    def _():
        owner = lax.axis_index("rot")
        core = lax.axis_index("dom") & 1
        lane = lax.broadcasted_iota(jnp.int32, (1, columns), 1)
        col_particle, col_x = lane >> 6, lane & (BOX - 1)
        count = jnp.int32(0)
        col_slot = jnp.full((1, columns), -1, jnp.int32)
        col_rot = jnp.full((1, columns), -1, jnp.int32)
        col_bucket = jnp.full((1, columns), -1, jnp.int32)
        slot_rot = [jnp.int32(-1) for _ in range(CAP)]
        for p in range(particles):
            mine = (class_ref[p, 0] == owner) & (p < live_ref[0])
            here = (col_particle == p) & mine
            col_slot = jnp.where(here, count, col_slot)
            col_rot = jnp.where(here, rot_ref[p], col_rot)
            col_bucket = jnp.where(here, bucket_ref[p], col_bucket)
            for slot in range(CAP):
                slot_rot[slot] = jnp.where(mine & (count == slot), rot_ref[p], slot_rot[slot])
            count = count + mine.astype(jnp.int32)
        count_out[0] = count
        levels = level_ref[...].astype(F32)
        col_weight = jnp.zeros((1, columns), F32)
        for level in range(levels.shape[1]):
            value = jnp.broadcast_to(levels[:, level : level + 1], (1, columns))
            col_weight = jnp.where(col_bucket == level, value, col_weight)
        row = lax.broadcasted_iota(jnp.int32, (SEND, columns), 0)
        base = (row // PER_CHIP) * (2 * PLANES) + (row & (PLANES - 1))
        right = ((row // PLANES) & (ROT_CLS - 1)) == col_rot
        for to_core, ref in ((core, spread_out), (1 - core, spread_s)):
            hit = right & (base + to_core * PLANES == col_x)
            ref[...] = jnp.where(hit, col_weight, 0.0).astype(BF)
        ref_lane = lax.broadcasted_iota(jnp.int32, (1, SEND), 1)
        ref_rot = (ref_lane // PLANES) & (ROT_CLS - 1)
        for slot in range(CAP):
            rows = slice(slot * 2 * KXP, (slot + 1) * 2 * KXP)
            pick_out[rows] = jnp.where(col_slot == slot, x_ref[...], 0.0).astype(BF)
            wanted = ref_rot == slot_rot[slot]
            pick_own_out[rows] = jnp.where(wanted, x_ref_table[core], 0.0).astype(BF)
            pick_other_out[rows] = jnp.where(wanted, x_ref_table[1 - core], 0.0).astype(BF)

    send_out[...] = jnp.dot(spread_s[...], flat_ref[...], preferred_element_type=F32).astype(BF)


def own_kernel(spread_ref, flat_ref, other_ref, out_ref):
    own = jnp.dot(spread_ref[...], flat_ref[...], preferred_element_type=F32)
    out_ref[...] = (own + other_ref[...].astype(F32)).astype(BF)


def spectra_kernel(pick_ref, flat_ref, table_ref, spectra_out):
    along_x = jnp.dot(pick_ref[...], flat_ref[...], preferred_element_type=F32).astype(BF)
    table = table_ref[...]
    for slot in range(CAP):
        part = z_stage(along_x[slot * 2 * KXP : (slot + 1) * 2 * KXP], table, 0, CHUNK)
        spectra_out[slot] = part.astype(BF)


def score_kernel(
    count_ref,
    zp_ref,
    pick_own_ref,
    pick_other_ref,
    own_ref,
    other_ref,
    table_ref,
    ex_ref,
    wz_ref,
    out_ref,
    x_s,
    p_s,
    r_s,
    o_s,
    a_s,
):
    slot = pl.program_id(0)

    @pl.when((slot == 0) & (count_ref[0] > 0))
    def _():
        for start in range(0, BOX * BOX, 512):
            lanes = slice(start, start + 512)
            part = jnp.dot(pick_own_ref[...], own_ref[:, lanes], preferred_element_type=F32)
            part = part + jnp.dot(
                pick_other_ref[...], other_ref[:, lanes], preferred_element_type=F32
            )
            x_s[:, :, lanes] = part.astype(BF).reshape(CAP, 2 * KXP, 512)

    @pl.when(slot < count_ref[0])
    def _():
        table = table_ref[...]
        xr = x_s.at[slot]
        for start in range(0, PAIRS, STEP):
            part = z_stage(xr, table, start, STEP)
            part = part.astype(BF).astype(F32).reshape(STEP, KXP, 4 * BOX)
            r_s[start : start + STEP] = part[:, :KXV, :]
            mine = zp_ref[start * KXP : (start + STEP) * KXP, :].astype(F32)
            p_s[start : start + STEP] = mine.reshape(STEP, KXP, 4 * BOX)[:, :KXV, :]
        first = lax.broadcasted_iota(jnp.int32, (KXV, 128), 1) < BOX
        for j in range(PAIRS):
            for half in range(2):
                lanes = slice(128 * half, 128 * (half + 1))
                now = r_s[j, :, lanes]
                before = r_s[(j - 1) % PAIRS, :, lanes]
                o_s[j, :, lanes] = pltpu.roll(jnp.where(first, now, before), BOX, 1)

        def column(col, carry):
            rows = pl.ds(pl.multiple_of(col * 8, 8), 8)
            re = [jnp.zeros((8, 128), F32) for _ in range(SHIFTS)]
            im = [jnp.zeros((8, 128), F32) for _ in range(SHIFTS)]
            for j in range(PAIRS):
                pr = p_s[j, rows, 0:128]
                pi = p_s[j, rows, 128:256]
                for u in range(-2, 2):
                    m = (j - u) % PAIRS
                    for odd, src in ((0, r_s), (1, o_s)):
                        t = 2 * u + odd + SHIFTS // 2
                        rr = src[m, rows, 0:128]
                        ri = src[m, rows, 128:256]
                        re[t] = re[t] + (pr * rr + pi * ri)
                        im[t] = im[t] + (pi * rr - pr * ri)
            for t in range(SHIFTS):
                a_s[t, rows, 0:128] = re[t]
                a_s[t, rows, 128:256] = im[t]
            return carry

        lax.fori_loop(0, KXV // 8, column, 0)
        ex = ex_ref[...]
        along_x = [
            jnp.dot(ex, a_s[t].astype(BF), preferred_element_type=F32) for t in range(SHIFTS)
        ]
        cos_rows = jnp.concatenate([u[:SHIFTS] for u in along_x], axis=0).astype(BF)
        sin_rows = jnp.concatenate([u[SHIFTS:] for u in along_x], axis=0).astype(BF)
        both = jnp.concatenate([cos_rows, sin_rows], axis=1)
        final = jnp.dot(both, wz_ref[...], preferred_element_type=F32)
        out_ref[...] = final * (float(BOX) ** -3.5)

    @pl.when(slot >= count_ref[0])
    def _():
        out_ref[...] = jnp.zeros_like(out_ref)


def yz_kernel(parts_ref, z_ref, y_ref, out_ref, z_s, g_s):
    total = parts_ref[0:PER_CHIP].astype(F32)
    for chip in range(1, CHIPS):
        total = total + parts_ref[chip * PER_CHIP : (chip + 1) * PER_CHIP].astype(F32)
    total = total.astype(BF)
    stacked = jnp.concatenate([total[:, 128 * j : 128 * (j + 1)] for j in range(PAIRS)], axis=0)
    z_part = jnp.dot(stacked, z_ref[...], preferred_element_type=F32)
    for j in range(PAIRS):
        for half in range(2):
            start = (2 * j + half) * PER_CHIP
            z_s[start : start + PER_CHIP] = z_part[
                j * PER_CHIP : (j + 1) * PER_CHIP, 128 * half : 128 * (half + 1)
            ]
    by_y = [z_s[pl.ds(n, BOX, stride=PER_CHIP), :].astype(BF) for n in range(PER_CHIP)]
    y_part = jnp.dot(y_ref[...], jnp.concatenate(by_y, axis=1), preferred_element_type=F32)
    first = lax.broadcasted_iota(jnp.int32, (BOX, 128), 1) < BOX
    for n in range(PER_CHIP):
        lanes = slice(128 * n, 128 * (n + 1))
        turned = pltpu.roll(y_part[BOX:, lanes], BOX, 1)
        g_s[pl.ds(n, BOX, stride=PER_CHIP), :] = y_part[:BOX, lanes] + jnp.where(first, turned, -turned)
    out_ref[...] = g_s[...].astype(BF)


def x_rows_kernel(rows_ref, table_ref, out_ref):
    rows = ROT_CLS * (BOX // DOM)
    first = lax.broadcasted_iota(jnp.int32, (ROT_CLS * BOX, 128), 1) < BOX
    for ky in range(BOX // DOM):
        grid = rows_ref[:, ky * rows : (ky + 1) * rows, :].reshape(ROT_CLS * BOX, 128)
        cos_part = jnp.dot(table_ref[0], grid, preferred_element_type=F32)
        cos_part = cos_part + jnp.dot(table_ref[1], grid, preferred_element_type=F32)
        sin_part = jnp.dot(table_ref[2], grid, preferred_element_type=F32)
        sin_part = sin_part + jnp.dot(table_ref[3], grid, preferred_element_type=F32)
        turned = pltpu.roll(sin_part, BOX, 1)
        total = (cos_part + jnp.where(first, turned, -turned)) * (float(BOX) ** -1.5)
        out_ref[ky] = total.reshape(ROT_CLS, BOX, 128)


VMEM = pl.BlockSpec(memory_space=pltpu.VMEM)
SMEM = pl.BlockSpec(memory_space=pltpu.SMEM)


def params(mib):
    return pltpu.CompilerParams(vmem_limit_bytes=mib * 1024 * 1024)


def cost(flops, moved):
    return pl.CostEstimate(flops=flops, bytes_accessed=moved, transcendentals=0)


def shards(particles, references, part_class, part_rot, bucket, bucket_weights, live_count):
    block_size = particles.shape[0]
    voxels = BOX * BOX
    columns = block_size * BOX
    to_other = [(i, i ^ 1) for i in range(DOM)]

    mine_refs = jnp.tile(references.reshape(PER_CHIP, voxels), (CHIPS, 1))
    mine_refs, part_class = lax.optimization_barrier((mine_refs, part_class))
    refs_own = lax.all_to_all(
        mine_refs, "dom", 0, 0, tiled=True, axis_index_groups=SAME_CORE
    )

    flat = particles.reshape(columns, voxels)
    x_half = x_half_table()
    by_core = x_half.reshape(2 * KXP, CHIPS, 2, 1, PLANES)
    by_core = np.broadcast_to(by_core, (2 * KXP, CHIPS, 2, ROT_CLS, PLANES))
    by_core = by_core.transpose(2, 0, 1, 3, 4).reshape(2, 2 * KXP, SEND)

    def whole(*shape):
        return pl.BlockSpec(shape, lambda s: (0,) * len(shape))

    lane_chunk = pl.BlockSpec((columns, 128 * CHUNK), lambda i: (0, i))
    send_chunk = pl.BlockSpec((SEND, 128 * CHUNK), lambda i: (0, i))
    to_send, spread_own, pick, pick_own, pick_other, count = pl.pallas_call(
        send_kernel,
        out_shape=(
            jax.ShapeDtypeStruct((SEND, voxels), BF),
            jax.ShapeDtypeStruct((SEND, columns), BF),
            jax.ShapeDtypeStruct((CAP * 2 * KXP, columns), BF),
            jax.ShapeDtypeStruct((CAP * 2 * KXP, SEND), BF),
            jax.ShapeDtypeStruct((CAP * 2 * KXP, SEND), BF),
            jax.ShapeDtypeStruct((1,), jnp.int32),
        ),
        grid=(STEPS,),
        in_specs=[
            SMEM,
            SMEM,
            SMEM,
            SMEM,
            whole(1, bucket_weights.shape[0]),
            whole(2 * KXP, columns),
            whole(2, 2 * KXP, SEND),
            lane_chunk,
        ],
        out_specs=(
            send_chunk,
            whole(SEND, columns),
            whole(CAP * 2 * KXP, columns),
            whole(CAP * 2 * KXP, SEND),
            whole(CAP * 2 * KXP, SEND),
            SMEM,
        ),
        scratch_shapes=[pltpu.VMEM((SEND, columns), BF)],
        compiler_params=params(54),
        cost_estimate=cost(1024, 1024),
        name="send",
    )(
        part_class,
        part_rot,
        bucket,
        live_count,
        bucket_weights.reshape(1, -1),
        jnp.asarray(np.tile(x_half, (1, block_size)), F32),
        jnp.asarray(by_core, F32),
        flat,
    )
    other = lax.ppermute(to_send, "dom", to_other)

    z_table = jnp.asarray(z_complex_table().astype(BF))
    spectra = pl.pallas_call(
        spectra_kernel,
        out_shape=jax.ShapeDtypeStruct((CAP, PAIRS * KXP, 4 * BOX), BF),
        grid=(STEPS,),
        in_specs=[whole(CAP * 2 * KXP, columns), lane_chunk, whole(4 * BOX, 4 * BOX)],
        out_specs=pl.BlockSpec((CAP, CHUNK * KXP, 4 * BOX), lambda i: (0, i, 0)),
        compiler_params=params(54),
        cost_estimate=cost(1024, 1024),
        name="spectra",
    )(pick, flat, z_table)

    pair_sum = pl.pallas_call(
        own_kernel,
        out_shape=jax.ShapeDtypeStruct((SEND, voxels), BF),
        grid=(STEPS,),
        in_specs=[whole(SEND, columns), lane_chunk, send_chunk],
        out_specs=send_chunk,
        compiler_params=params(50),
        cost_estimate=cost(1024, 1024),
        name="own",
    )(spread_own, flat, other)
    refs_own, spectra = lax.optimization_barrier((refs_own, spectra))
    refs_other = lax.ppermute(refs_own, "dom", to_other)
    arrived = lax.all_to_all(pair_sum, "dom", 0, 0, tiled=True, axis_index_groups=SAME_CORE)

    ex, wz = shift_tables()

    slots = pl.pallas_call(
        score_kernel,
        out_shape=jax.ShapeDtypeStruct((CAP, SHIFTS * SHIFTS, 128), F32),
        grid=(CAP,),
        in_specs=[
            SMEM,
            pl.BlockSpec((None, PAIRS * KXP, 4 * BOX), lambda s: (s, 0, 0)),
            whole(CAP * 2 * KXP, SEND),
            whole(CAP * 2 * KXP, SEND),
            whole(SEND, voxels),
            whole(SEND, voxels),
            whole(4 * BOX, 4 * BOX),
            whole(2 * SHIFTS, KXV),
            whole(8 * BOX, 128),
        ],
        out_specs=pl.BlockSpec((None, SHIFTS * SHIFTS, 128), lambda s: (s, 0, 0)),
        scratch_shapes=[
            pltpu.VMEM((CAP, 2 * KXP, voxels), BF),
            pltpu.VMEM((PAIRS, KXV, 4 * BOX), F32),
            pltpu.VMEM((PAIRS, KXV, 4 * BOX), F32),
            pltpu.VMEM((PAIRS, KXV, 4 * BOX), F32),
            pltpu.VMEM((SHIFTS, KXV, 4 * BOX), F32),
        ],
        compiler_params=params(50),
        cost_estimate=cost(1024, 1024),
        name="slot_scores",
    )(
        count,
        spectra,
        pick_own,
        pick_other,
        refs_own,
        refs_other,
        z_table,
        jnp.asarray(ex.astype(BF)),
        jnp.asarray(wz.astype(BF)),
    )
    slot_scores = slots[:, :, :SHIFTS].reshape(CAP, SHIFTS, SHIFTS, SHIFTS)
    slot_scores = slot_scores.transpose(0, 2, 1, 3).reshape(CAP, SHIFTS**3)
    everywhere = lax.all_to_all(jnp.tile(slot_scores, (8, 1)), "rot", 0, 0, tiled=True)
    rows_all = jnp.arange(block_size, dtype=jnp.int32)
    classes = part_class[:, 0]
    alive = rows_all < live_count[0]
    before = (classes[:, None] == classes[None, :]) & (rows_all[None, :] < rows_all[:, None])
    place = classes * CAP + jnp.sum(before.astype(jnp.int32), axis=1)
    found = (place[:, None] == jnp.arange(8 * CAP, dtype=jnp.int32)[None, :]) & alive[:, None]
    scores = jnp.sum(jnp.where(found[:, :, None], everywhere[None, :, :], 0.0), axis=1)

    z_real = jnp.asarray(z_real_table().astype(BF))
    grids = pl.pallas_call(
        yz_kernel,
        out_shape=jax.ShapeDtypeStruct((BOX * PER_CHIP, 2 * BOX), BF),
        in_specs=[VMEM] * 3,
        out_specs=VMEM,
        scratch_shapes=[pltpu.VMEM((BOX * PER_CHIP, 128), F32)] * 2,
        compiler_params=params(50),
        cost_estimate=cost(1024, 1024),
        name="yz_planes",
    )(arrived, z_real, jnp.asarray(y_table().astype(BF)))
    by_rows = lax.all_to_all(grids, "dom", 0, 0, tiled=True)
    sums = pl.pallas_call(
        x_rows_kernel,
        out_shape=jax.ShapeDtypeStruct((BOX // DOM, ROT_CLS, BOX, 2 * BOX), F32),
        in_specs=[VMEM] * 2,
        out_specs=VMEM,
        compiler_params=params(50),
        name="x_rows",
    )(by_rows.reshape(DOM, PLANES * PER_CHIP, 2 * BOX), jnp.asarray(x_rows_table()))
    return (scores, sums)


def solution(mesh):
    return jax.shard_map(
        shards,
        mesh=mesh,
        in_specs=(
            P("dom", None, None),
            P("rot", "dom", None),
            P("dom", None),
            P("dom"),
            P("dom"),
            P(),
            P("dom"),
        ),
        out_specs=(P("dom", None), P("dom", "rot", None, None)),
        check_vma=False,
    )
```

```python
import math

import jax
import jax.numpy as jnp
import numpy as np
from jax import lax
from jax.experimental import pallas as pl
from jax.experimental.pallas import tpu as pltpu
from jax.sharding import PartitionSpec as P

BOX = 64
SHIFTS = 8
ROT_CLS = 4
CAP = 4
HALF = 33
KXP = 48
KXV = 40
PAIRS = BOX // 2
DOM = 16
CHIPS = DOM // 2
SAME_CORE = [[2 * chip + core for chip in range(CHIPS)] for core in range(2)]
BF = jnp.bfloat16
F32 = jnp.float32


def grid_cos_sin(rows, cols):
    theta = ((rows[:, None] * cols[None, :]) % BOX).astype(np.float64) * (2.0 * math.pi / BOX)
    return np.cos(theta), np.sin(theta)


def x_half_table():
    c, s = grid_cos_sin(np.arange(BOX), np.arange(BOX))
    out = np.zeros((2, KXP, BOX))
    out[0, :HALF] = c[:HALF]
    out[1, :HALF] = -s[:HALF]
    return out.reshape(2 * KXP, BOX)


def z_complex_table():
    c, s = grid_cos_sin(np.arange(BOX), np.arange(BOX))
    two = np.eye(2)
    return np.block([[np.kron(two, c), np.kron(two, -s)], [np.kron(two, s), np.kron(two, c)]])


def shift_tables():
    c, s = grid_cos_sin(np.arange(SHIFTS) - SHIFTS // 2, np.arange(BOX))
    fold = np.zeros((KXV,))
    fold[:HALF] = 2.0
    fold[0] = fold[HALF - 1] = 1.0
    ex = np.zeros((2 * SHIFTS, KXV))
    ex[:SHIFTS, :HALF] = c[:, :HALF]
    ex[SHIFTS:, :HALF] = s[:, :HALF]
    ex = ex * fold[None, :]
    wz = np.zeros((2, 4 * BOX, 128))
    wz[0, :, :SHIFTS] = np.concatenate([c.T, c.T, -s.T, -s.T], axis=0)
    wz[1, :, :SHIFTS] = np.concatenate([-s.T, -s.T, -c.T, -c.T], axis=0)
    return ex, wz.reshape(8 * BOX, 128)


def z_real_table():
    c, s = grid_cos_sin(np.arange(BOX), np.arange(BOX))
    return np.kron(np.eye(2), np.concatenate([c, -s], axis=1))


def y_table():
    c, s = grid_cos_sin(np.arange(BOX), np.arange(BOX))
    return np.concatenate([c, s], axis=0)


def x_rows_table():
    c, s = grid_cos_sin(np.arange(BOX), np.arange(BOX))
    full = []
    for table in (c, s):
        spread = np.einsum(
            "rq,kdx->rkdqx", np.eye(ROT_CLS), table.reshape(BOX, DOM, BOX // DOM)
        ).reshape(ROT_CLS * BOX, ROT_CLS * BOX)
        high = spread.astype(np.float32).astype(BF)
        low = (spread.astype(np.float32) - high.astype(np.float32)).astype(BF)
        full += [high, low]
    return np.stack(full)


def z_stage(src, table, start, count):
    parts = []
    for j in range(start, start + count):
        lanes = slice(128 * j, 128 * (j + 1))
        parts.append(jnp.concatenate([src[0:KXP, lanes], src[KXP : 2 * KXP, lanes]], axis=1))
    return jnp.dot(jnp.concatenate(parts, axis=0), table, preferred_element_type=F32)


STEP = 8
CHUNK = 4
PLANES = BOX // DOM
PER_CHIP = ROT_CLS * PLANES
SEND = CHIPS * PER_CHIP


LANES = 1024


def send_kernel(
    class_ref,
    rot_ref,
    bucket_ref,
    live_ref,
    level_ref,
    x_ref,
    flat_hbm,
    send_out,
    own_out,
    pick_out,
    count_out,
    slot_rot_out,
    flat_s,
    spread_s,
    sems,
):
    particles, columns = class_ref.shape[0], flat_hbm.shape[0]
    copies = [
        pltpu.make_async_copy(
            flat_hbm.at[p * BOX : (p + 1) * BOX], flat_s.at[p * BOX : (p + 1) * BOX], sems.at[p]
        )
        for p in range(particles)
    ]
    for copy in copies:
        copy.start()
    owner = lax.axis_index("rot")
    core = lax.axis_index("dom") & 1
    lane = lax.broadcasted_iota(jnp.int32, (1, columns), 1)
    col_particle, col_x = lane >> 6, lane & (BOX - 1)
    count = jnp.int32(0)
    col_slot = jnp.full((1, columns), -1, jnp.int32)
    col_rot = jnp.full((1, columns), -1, jnp.int32)
    col_bucket = jnp.full((1, columns), -1, jnp.int32)
    slot_rot = [jnp.int32(-1) for _ in range(CAP)]
    for p in range(particles):
        mine = (class_ref[p] == owner) & (p < live_ref[0])
        here = (col_particle == p) & mine
        col_slot = jnp.where(here, count, col_slot)
        col_rot = jnp.where(here, rot_ref[p], col_rot)
        col_bucket = jnp.where(here, bucket_ref[p], col_bucket)
        for slot in range(CAP):
            slot_rot[slot] = jnp.where(mine & (count == slot), rot_ref[p], slot_rot[slot])
        count = count + mine.astype(jnp.int32)
    count_out[0] = count
    for slot in range(CAP):
        slot_rot_out[slot] = slot_rot[slot]
    levels = level_ref[...].astype(F32)
    col_weight = jnp.zeros((1, columns), F32)
    for level in range(levels.shape[1]):
        value = jnp.broadcast_to(levels[:, level : level + 1], (1, columns))
        col_weight = jnp.where(col_bucket == level, value, col_weight)
    row = lax.broadcasted_iota(jnp.int32, (SEND, columns), 0)
    base = (row // PER_CHIP) * (2 * PLANES) + (row & (PLANES - 1))
    right = ((row // PLANES) & (ROT_CLS - 1)) == col_rot
    for half, to_core in enumerate((core, 1 - core)):
        hit = right & (base + to_core * PLANES == col_x)
        spread_s[half * SEND : (half + 1) * SEND] = jnp.where(hit, col_weight, 0.0).astype(BF)
    for slot in range(CAP):
        rows = slice(slot * 2 * KXP, (slot + 1) * 2 * KXP)
        pick_out[rows] = jnp.where(col_slot == slot, x_ref[...], 0.0).astype(BF)
    for copy in copies:
        copy.wait()
    for start in range(0, BOX * BOX, LANES):
        lanes = slice(start, start + LANES)
        part = jnp.dot(spread_s[...], flat_s[:, lanes], preferred_element_type=F32)
        own_out[:, lanes] = part[:SEND].astype(BF)
        send_out[:, lanes] = part[SEND:].astype(BF)


def pair_kernel(own_ref, other_ref, out_ref):
    out_ref[...] = (own_ref[...].astype(F32) + other_ref[...].astype(F32)).astype(BF)


def spectra_kernel(pick_ref, flat_hbm, table_ref, spectra_out, flat_s, sems):
    particles = flat_hbm.shape[0] // BOX
    copies = [
        pltpu.make_async_copy(
            flat_hbm.at[p * BOX : (p + 1) * BOX], flat_s.at[p * BOX : (p + 1) * BOX], sems.at[p]
        )
        for p in range(particles)
    ]
    for copy in copies:
        copy.start()
    for copy in copies:
        copy.wait()
    table = table_ref[...]
    for start in range(0, PAIRS, CHUNK):
        lanes = slice(128 * start, 128 * (start + CHUNK))
        along_x = jnp.dot(pick_ref[...], flat_s[:, lanes], preferred_element_type=F32).astype(BF)
        for slot in range(CAP):
            part = z_stage(along_x[slot * 2 * KXP : (slot + 1) * 2 * KXP], table, 0, CHUNK)
            spectra_out[slot, start * KXP : (start + CHUNK) * KXP, :] = part.astype(BF)


def score_kernel(
    count_ref,
    slot_rot_ref,
    zp_ref,
    x_ref,
    own_ref,
    other_ref,
    table_ref,
    ex_ref,
    wz_ref,
    out_ref,
    pick_s,
    x_s,
    p_s,
    r_s,
    a_s,
):
    slot = pl.program_id(0)

    @pl.when((slot == 0) & (count_ref[0] > 0))
    def _():
        core = lax.axis_index("dom") & 1
        ref_lane = lax.broadcasted_iota(jnp.int32, (1, SEND), 1)
        ref_rot = (ref_lane // PLANES) & (ROT_CLS - 1)
        for to in range(CAP):
            rows = slice(to * 2 * KXP, (to + 1) * 2 * KXP)
            wanted = ref_rot == slot_rot_ref[to]
            pick_s[0, rows] = jnp.where(wanted, x_ref[core], 0.0).astype(BF)
            pick_s[1, rows] = jnp.where(wanted, x_ref[1 - core], 0.0).astype(BF)
        for start in range(0, BOX * BOX, 512):
            lanes = slice(start, start + 512)
            part = jnp.dot(pick_s[0], own_ref[:, lanes], preferred_element_type=F32)
            part = part + jnp.dot(pick_s[1], other_ref[:, lanes], preferred_element_type=F32)
            x_s[:, :, lanes] = part.astype(BF).reshape(CAP, 2 * KXP, 512)

    @pl.when(slot < count_ref[0])
    def _():
        table = table_ref[...]
        xr = x_s.at[slot]
        for start in range(0, PAIRS, STEP):
            part = z_stage(xr, table, start, STEP)
            part = part.astype(BF).astype(F32).reshape(STEP, KXP, 4 * BOX)
            r_s[start : start + STEP] = part[:, :KXV, :]
            mine = zp_ref[start * KXP : (start + STEP) * KXP, :].astype(F32)
            p_s[start : start + STEP] = mine.reshape(STEP, KXP, 4 * BOX)[:, :KXV, :]
        first = lax.broadcasted_iota(jnp.int32, (8, 128), 1) < BOX

        def column(col, carry):
            rows = pl.ds(pl.multiple_of(col * 8, 8), 8)

            def pair(m):
                return r_s[m % PAIRS, rows, 0:128], r_s[m % PAIRS, rows, 128:256]

            def shifted(before, now):
                return tuple(
                    pltpu.roll(jnp.where(first, n, b), BOX, 1) for b, n in zip(before, now)
                )

            def three(re, im):
                return re, im, re - im

            tiles = {m: pair(m) for m in range(-2, 2)}
            even = {m: three(*tiles[m]) for m in range(-1, 2)}
            odd = {m: three(*shifted(tiles[m - 1], tiles[m])) for m in range(-1, 2)}
            last = tiles[1]
            sums = [[jnp.zeros((8, 128), F32) for _ in range(3)] for _ in range(SHIFTS)]
            for j in range(PAIRS):
                new = pair(j + 2)
                even[j + 2] = three(*new)
                odd[j + 2] = three(*shifted(last, new))
                last = new
                pr = p_s[j, rows, 0:128]
                pi = p_s[j, rows, 128:256]
                both = pr + pi
                for u in range(-2, 2):
                    for parity, held in ((0, even), (1, odd)):
                        t = 2 * u + parity + SHIFTS // 2
                        rr, ri, rd = held[j - u]
                        sums[t][0] = sums[t][0] + pr * rr
                        sums[t][1] = sums[t][1] + pi * ri
                        sums[t][2] = sums[t][2] + both * rd
                del even[j - 1], odd[j - 1]
            for t in range(SHIFTS):
                one, two, mix = sums[t]
                a_s[t, rows, 0:128] = one + two
                a_s[t, rows, 128:256] = mix - one + two
            return carry

        lax.fori_loop(0, KXV // 8, column, 0)
        ex = ex_ref[...]
        along_x = [
            jnp.dot(ex, a_s[t].astype(BF), preferred_element_type=F32) for t in range(SHIFTS)
        ]
        cos_rows = jnp.concatenate([u[:SHIFTS] for u in along_x], axis=0).astype(BF)
        sin_rows = jnp.concatenate([u[SHIFTS:] for u in along_x], axis=0).astype(BF)
        both_rows = jnp.concatenate([cos_rows, sin_rows], axis=1)
        final = jnp.dot(both_rows, wz_ref[...], preferred_element_type=F32)
        out_ref[...] = final * (float(BOX) ** -3.5)

    @pl.when(slot >= count_ref[0])
    def _():
        out_ref[...] = jnp.zeros_like(out_ref)


def yz_kernel(parts_ref, z_ref, y_ref, out_ref, z_s, g_s):
    total = parts_ref[0:PER_CHIP].astype(F32)
    for chip in range(1, CHIPS):
        total = total + parts_ref[chip * PER_CHIP : (chip + 1) * PER_CHIP].astype(F32)
    total = total.astype(BF)
    stacked = jnp.concatenate([total[:, 128 * j : 128 * (j + 1)] for j in range(PAIRS)], axis=0)
    z_part = jnp.dot(stacked, z_ref[...], preferred_element_type=F32)
    for j in range(PAIRS):
        for half in range(2):
            start = (2 * j + half) * PER_CHIP
            z_s[start : start + PER_CHIP] = z_part[
                j * PER_CHIP : (j + 1) * PER_CHIP, 128 * half : 128 * (half + 1)
            ]
    by_y = [z_s[pl.ds(n, BOX, stride=PER_CHIP), :].astype(BF) for n in range(PER_CHIP)]
    y_part = jnp.dot(y_ref[...], jnp.concatenate(by_y, axis=1), preferred_element_type=F32)
    first = lax.broadcasted_iota(jnp.int32, (BOX, 128), 1) < BOX
    for n in range(PER_CHIP):
        lanes = slice(128 * n, 128 * (n + 1))
        turned = pltpu.roll(y_part[BOX:, lanes], BOX, 1)
        g_s[pl.ds(n, BOX, stride=PER_CHIP), :] = y_part[:BOX, lanes] + jnp.where(first, turned, -turned)
    out_ref[...] = g_s[...].astype(BF)


def x_rows_kernel(rows_ref, table_hbm, out_ref, table_ref, sem):
    copy = pltpu.make_async_copy(table_hbm, table_ref, sem)
    copy.start()
    copy.wait()
    rows = ROT_CLS * (BOX // DOM)
    first = lax.broadcasted_iota(jnp.int32, (ROT_CLS * BOX, 128), 1) < BOX
    for ky in range(BOX // DOM):
        grid = rows_ref[:, ky * rows : (ky + 1) * rows, :].reshape(ROT_CLS * BOX, 128)
        cos_part = jnp.dot(table_ref[0], grid, preferred_element_type=F32)
        cos_part = cos_part + jnp.dot(table_ref[1], grid, preferred_element_type=F32)
        sin_part = jnp.dot(table_ref[2], grid, preferred_element_type=F32)
        sin_part = sin_part + jnp.dot(table_ref[3], grid, preferred_element_type=F32)
        turned = pltpu.roll(sin_part, BOX, 1)
        total = (cos_part + jnp.where(first, turned, -turned)) * (float(BOX) ** -1.5)
        out_ref[ky] = total.reshape(ROT_CLS, BOX, 128)


VMEM = pl.BlockSpec(memory_space=pltpu.VMEM)
HBM = pl.BlockSpec(memory_space=pltpu.HBM)
SMEM = pl.BlockSpec(memory_space=pltpu.SMEM)


def params(mib):
    return pltpu.CompilerParams(vmem_limit_bytes=mib * 1024 * 1024)


def cost(flops, moved):
    return pl.CostEstimate(flops=flops, bytes_accessed=moved, transcendentals=0)


def shards(particles, references, part_class, part_rot, bucket, bucket_weights, live_count):
    block_size = particles.shape[0]
    voxels = BOX * BOX
    columns = block_size * BOX
    to_other = [(i, i ^ 1) for i in range(DOM)]

    mine_refs = jnp.tile(references.reshape(PER_CHIP, voxels), (CHIPS, 1))

    flat = particles.reshape(columns, voxels)
    classes = part_class.reshape(block_size)
    x_half = x_half_table()
    by_core = x_half.reshape(2 * KXP, CHIPS, 2, 1, PLANES)
    by_core = np.broadcast_to(by_core, (2 * KXP, CHIPS, 2, ROT_CLS, PLANES))
    by_core = by_core.transpose(2, 0, 1, 3, 4).reshape(2, 2 * KXP, SEND)
    held = [
        pltpu.VMEM((columns, voxels), BF),
        pltpu.SemaphoreType.DMA((block_size,)),
    ]

    def whole(*shape):
        return pl.BlockSpec(shape, lambda s: (0,) * len(shape))

    to_send, own, pick, count, slot_rot = pl.pallas_call(
        send_kernel,
        out_shape=(
            jax.ShapeDtypeStruct((SEND, voxels), BF),
            jax.ShapeDtypeStruct((SEND, voxels), BF),
            jax.ShapeDtypeStruct((CAP * 2 * KXP, columns), BF),
            jax.ShapeDtypeStruct((1,), jnp.int32),
            jax.ShapeDtypeStruct((CAP,), jnp.int32),
        ),
        in_specs=[SMEM, SMEM, SMEM, SMEM, VMEM, VMEM, HBM],
        out_specs=(VMEM, VMEM, VMEM, SMEM, SMEM),
        scratch_shapes=[held[0], pltpu.VMEM((2 * SEND, columns), BF), held[1]],
        compiler_params=params(54),
        cost_estimate=cost(1024, 1024),
        name="send",
    )(
        classes,
        part_rot,
        bucket,
        live_count,
        bucket_weights.reshape(1, -1),
        jnp.asarray(np.tile(x_half, (1, block_size)), F32),
        flat,
    )
    to_send, mine_refs = lax.optimization_barrier((to_send, mine_refs))
    other = lax.ppermute(to_send, "dom", to_other)
    refs_own = lax.all_to_all(
        mine_refs, "dom", 0, 0, tiled=True, axis_index_groups=SAME_CORE
    )
    pair_sum = pl.pallas_call(
        pair_kernel,
        out_shape=jax.ShapeDtypeStruct((SEND, voxels), BF),
        in_specs=[VMEM, VMEM],
        out_specs=VMEM,
        compiler_params=params(50),
        cost_estimate=cost(1024, 1024),
        name="pair",
    )(own, other)
    pick, pair_sum = lax.optimization_barrier((pick, pair_sum))
    arrived = lax.all_to_all(pair_sum, "dom", 0, 0, tiled=True, axis_index_groups=SAME_CORE)

    z_table = jnp.asarray(z_complex_table().astype(BF))
    spectra = pl.pallas_call(
        spectra_kernel,
        out_shape=jax.ShapeDtypeStruct((CAP, PAIRS * KXP, 4 * BOX), BF),
        in_specs=[VMEM, HBM, VMEM],
        out_specs=VMEM,
        scratch_shapes=held,
        compiler_params=params(54),
        cost_estimate=cost(1024, 1024),
        name="spectra",
    )(pick, flat, z_table)

    refs_own, spectra = lax.optimization_barrier((refs_own, spectra))
    refs_other = lax.ppermute(refs_own, "dom", to_other)
    ex, wz = shift_tables()

    slots = pl.pallas_call(
        score_kernel,
        out_shape=jax.ShapeDtypeStruct((CAP, SHIFTS * SHIFTS, 128), F32),
        grid=(CAP,),
        in_specs=[
            SMEM,
            SMEM,
            pl.BlockSpec((None, PAIRS * KXP, 4 * BOX), lambda s: (s, 0, 0)),
            whole(2, 2 * KXP, SEND),
            whole(SEND, voxels),
            whole(SEND, voxels),
            whole(4 * BOX, 4 * BOX),
            whole(2 * SHIFTS, KXV),
            whole(8 * BOX, 128),
        ],
        out_specs=pl.BlockSpec((None, SHIFTS * SHIFTS, 128), lambda s: (s, 0, 0)),
        scratch_shapes=[
            pltpu.VMEM((2, CAP * 2 * KXP, SEND), BF),
            pltpu.VMEM((CAP, 2 * KXP, voxels), BF),
            pltpu.VMEM((PAIRS, KXV, 4 * BOX), F32),
            pltpu.VMEM((PAIRS, KXV, 4 * BOX), F32),
            pltpu.VMEM((SHIFTS, KXV, 4 * BOX), F32),
        ],
        compiler_params=params(50),
        cost_estimate=cost(1024, 1024),
        name="slot_scores",
    )(
        count,
        slot_rot,
        spectra,
        jnp.asarray(by_core, F32),
        refs_own,
        refs_other,
        z_table,
        jnp.asarray(ex.astype(BF)),
        jnp.asarray(wz.astype(BF)),
    )
    slot_scores = slots[:, :, :SHIFTS].reshape(CAP, SHIFTS, SHIFTS, SHIFTS)
    slot_scores = slot_scores.transpose(0, 2, 1, 3).reshape(CAP, SHIFTS**3)
    everywhere = lax.all_to_all(jnp.tile(slot_scores, (8, 1)), "rot", 0, 0, tiled=True)
    rows_all = jnp.arange(block_size, dtype=jnp.int32)
    alive = rows_all < live_count[0]
    before = (classes[:, None] == classes[None, :]) & (rows_all[None, :] < rows_all[:, None])
    place = classes * CAP + jnp.sum(before.astype(jnp.int32), axis=1)
    found = (place[:, None] == jnp.arange(8 * CAP, dtype=jnp.int32)[None, :]) & alive[:, None]
    scores = jnp.sum(jnp.where(found[:, :, None], everywhere[None, :, :], 0.0), axis=1)

    z_real = jnp.asarray(z_real_table().astype(BF))
    grids = pl.pallas_call(
        yz_kernel,
        out_shape=jax.ShapeDtypeStruct((BOX * PER_CHIP, 2 * BOX), BF),
        in_specs=[VMEM] * 3,
        out_specs=VMEM,
        scratch_shapes=[pltpu.VMEM((BOX * PER_CHIP, 128), F32)] * 2,
        compiler_params=params(50),
        cost_estimate=cost(1024, 1024),
        name="yz_planes",
    )(arrived, z_real, jnp.asarray(y_table().astype(BF)))
    by_rows = lax.all_to_all(grids, "dom", 0, 0, tiled=True)
    sums = pl.pallas_call(
        x_rows_kernel,
        out_shape=jax.ShapeDtypeStruct((BOX // DOM, ROT_CLS, BOX, 2 * BOX), F32),
        in_specs=[VMEM, HBM],
        out_specs=VMEM,
        scratch_shapes=[
            pltpu.VMEM((4, ROT_CLS * BOX, ROT_CLS * BOX), BF),
            pltpu.SemaphoreType.DMA,
        ],
        compiler_params=params(50),
        name="x_rows",
    )(by_rows.reshape(DOM, PLANES * PER_CHIP, 2 * BOX), jnp.asarray(x_rows_table()))
    return (scores, sums)


def solution(mesh):
    return jax.shard_map(
        shards,
        mesh=mesh,
        in_specs=(
            P("dom", None, None),
            P("rot", "dom", None),
            P("dom", None),
            P("dom"),
            P("dom"),
            P(),
            P("dom"),
        ),
        out_specs=(P("dom", None), P("dom", "rot", None, None)),
        check_vma=False,
    )
```

```python
import math

import jax
import jax.numpy as jnp
import numpy as np
from jax import lax
from jax.experimental import pallas as pl
from jax.experimental.pallas import tpu as pltpu
from jax.sharding import PartitionSpec as P

BOX = 64
SHIFTS = 8
ROT_CLS = 4
CAP = 4
HALF = 33
KXP = 48
KXV = 40
PAIRS = BOX // 2
DOM = 16
CHIPS = DOM // 2
SAME_CORE = [[2 * chip + core for chip in range(CHIPS)] for core in range(2)]
BF = jnp.bfloat16
F32 = jnp.float32


def grid_cos_sin(rows, cols):
    theta = ((rows[:, None] * cols[None, :]) % BOX).astype(np.float64) * (2.0 * math.pi / BOX)
    return np.cos(theta), np.sin(theta)


def x_half_table():
    c, s = grid_cos_sin(np.arange(BOX), np.arange(BOX))
    out = np.zeros((2, KXP, BOX))
    out[0, :HALF] = c[:HALF]
    out[1, :HALF] = -s[:HALF]
    return out.reshape(2 * KXP, BOX)


def z_complex_table():
    c, s = grid_cos_sin(np.arange(BOX), np.arange(BOX))
    two = np.eye(2)
    return np.block([[np.kron(two, c), np.kron(two, -s)], [np.kron(two, s), np.kron(two, c)]])


def shift_tables():
    c, s = grid_cos_sin(np.arange(SHIFTS) - SHIFTS // 2, np.arange(BOX))
    fold = np.zeros((KXV,))
    fold[:HALF] = 2.0
    fold[0] = fold[HALF - 1] = 1.0
    ex = np.zeros((2 * SHIFTS, KXV))
    ex[:SHIFTS, :HALF] = c[:, :HALF]
    ex[SHIFTS:, :HALF] = s[:, :HALF]
    ex = ex * fold[None, :]
    wz = np.zeros((2, 4 * BOX, 128))
    wz[0, :, :SHIFTS] = np.concatenate([c.T, c.T, -s.T, -s.T], axis=0)
    wz[1, :, :SHIFTS] = np.concatenate([-s.T, -s.T, -c.T, -c.T], axis=0)
    return ex, wz.reshape(8 * BOX, 128)


def z_real_table():
    c, s = grid_cos_sin(np.arange(BOX), np.arange(BOX))
    return np.kron(np.eye(2), np.concatenate([c, -s], axis=1))


def y_table():
    c, s = grid_cos_sin(np.arange(BOX), np.arange(BOX))
    return np.concatenate([c, s], axis=0)


def x_rows_table():
    c, s = grid_cos_sin(np.arange(BOX), np.arange(BOX))
    full = []
    for table in (c, s):
        spread = np.einsum(
            "rq,kdx->rkdqx", np.eye(ROT_CLS), table.reshape(BOX, DOM, BOX // DOM)
        ).reshape(ROT_CLS * BOX, ROT_CLS * BOX)
        high = spread.astype(np.float32).astype(BF)
        low = (spread.astype(np.float32) - high.astype(np.float32)).astype(BF)
        full += [high, low]
    return np.stack(full)


def z_stage(src, table, start, count):
    parts = []
    for j in range(start, start + count):
        lanes = slice(128 * j, 128 * (j + 1))
        parts.append(jnp.concatenate([src[0:KXP, lanes], src[KXP : 2 * KXP, lanes]], axis=1))
    return jnp.dot(jnp.concatenate(parts, axis=0), table, preferred_element_type=F32)


STEP = 8
CHUNK = 4
PLANES = BOX // DOM
PER_CHIP = ROT_CLS * PLANES
SEND = CHIPS * PER_CHIP


LANES = 1024


def slot_copies(flat_hbm, flat_s, sems, rows_of):
    return [
        pltpu.make_async_copy(
            flat_hbm.at[pl.ds(pl.multiple_of(rows_of(slot) * BOX, BOX), BOX)],
            flat_s.at[slot * BOX : (slot + 1) * BOX],
            sems.at[slot],
        )
        for slot in range(CAP)
    ]


def send_kernel(
    class_ref,
    rot_ref,
    bucket_ref,
    live_ref,
    level_ref,
    flat_hbm,
    send_out,
    own_out,
    count_out,
    slot_rot_out,
    slot_row_out,
    flat_s,
    spread_s,
    sems,
):
    owner = lax.axis_index("rot")
    core = lax.axis_index("dom") & 1
    count = jnp.int32(0)
    slot_row = [jnp.int32(0) for _ in range(CAP)]
    slot_rot = [jnp.int32(-1) for _ in range(CAP)]
    slot_bucket = [jnp.int32(-1) for _ in range(CAP)]
    for p in range(class_ref.shape[0]):
        mine = (class_ref[p] == owner) & (p < live_ref[0])
        for slot in range(CAP):
            here = mine & (count == slot)
            slot_row[slot] = jnp.where(here, p, slot_row[slot])
            slot_rot[slot] = jnp.where(here, rot_ref[p], slot_rot[slot])
            slot_bucket[slot] = jnp.where(here, bucket_ref[p], slot_bucket[slot])
        count = count + mine.astype(jnp.int32)
    copies = slot_copies(flat_hbm, flat_s, sems, lambda slot: slot_row[slot])
    for copy in copies:
        copy.start()
    count_out[0] = count
    for slot in range(CAP):
        slot_rot_out[slot] = slot_rot[slot]
        slot_row_out[slot] = slot_row[slot]
    columns = CAP * BOX
    lane = lax.broadcasted_iota(jnp.int32, (1, columns), 1)
    col_slot, col_x = lane >> 6, lane & (BOX - 1)
    col_rot = jnp.full((1, columns), -1, jnp.int32)
    col_bucket = jnp.full((1, columns), -1, jnp.int32)
    for slot in range(CAP):
        col_rot = jnp.where(col_slot == slot, slot_rot[slot], col_rot)
        col_bucket = jnp.where(col_slot == slot, slot_bucket[slot], col_bucket)
    levels = level_ref[...].astype(F32)
    col_weight = jnp.zeros((1, columns), F32)
    for level in range(levels.shape[1]):
        value = jnp.broadcast_to(levels[:, level : level + 1], (1, columns))
        col_weight = jnp.where(col_bucket == level, value, col_weight)
    row = lax.broadcasted_iota(jnp.int32, (SEND, columns), 0)
    dom = lax.axis_index("dom")
    offset = row // PER_CHIP
    to_chip = ((((dom >> 2) + (offset >> 1)) & 3) << 1) + (((dom >> 1) & 1) ^ (offset & 1))
    base = to_chip * (2 * PLANES) + (row & (PLANES - 1))
    right = ((row // PLANES) & (ROT_CLS - 1)) == col_rot
    for half, to_core in enumerate((core, 1 - core)):
        hit = right & (base + to_core * PLANES == col_x)
        spread_s[half * SEND : (half + 1) * SEND] = jnp.where(hit, col_weight, 0.0).astype(BF)
    for copy in copies:
        copy.wait()
    for start in range(0, BOX * BOX, LANES):
        lanes = slice(start, start + LANES)
        part = jnp.dot(spread_s[...], flat_s[:, lanes], preferred_element_type=F32)
        own_out[:, lanes] = part[:SEND].astype(BF)
        send_out[:, lanes] = part[SEND:].astype(BF)


def pair_kernel(own_ref, other_ref, *out_refs):
    for chip, out_ref in enumerate(out_refs):
        rows = slice(chip * PER_CHIP, (chip + 1) * PER_CHIP)
        out_ref[...] = (own_ref[rows].astype(F32) + other_ref[rows].astype(F32)).astype(BF)


def spectra_kernel(slot_row_ref, x_ref, flat_hbm, table_ref, spectra_out, flat_s, sems):
    chunk = pl.program_id(0)

    @pl.when(chunk == 0)
    def _():
        copies = slot_copies(flat_hbm, flat_s, sems, lambda slot: slot_row_ref[slot])
        for copy in copies:
            copy.start()
        for copy in copies:
            copy.wait()

    lanes = pl.ds(pl.multiple_of(chunk * 128 * CHUNK, 128 * CHUNK), 128 * CHUNK)
    along_x = jnp.dot(x_ref[...], flat_s[:, lanes], preferred_element_type=F32).astype(BF)
    table = table_ref[...]
    for slot in range(CAP):
        part = z_stage(along_x[slot * 2 * KXP : (slot + 1) * 2 * KXP], table, 0, CHUNK)
        spectra_out[slot] = part.astype(BF)


def pick_kernel(slot_rot_ref, x_ref, out_ref):
    core = lax.axis_index("dom") & 1
    ref_lane = lax.broadcasted_iota(jnp.int32, (1, SEND), 1)
    ref_rot = (ref_lane // PLANES) & (ROT_CLS - 1)
    for slot in range(CAP):
        rows = slice(slot * 2 * KXP, (slot + 1) * 2 * KXP)
        wanted = ref_rot == slot_rot_ref[slot]
        out_ref[0, rows] = jnp.where(wanted, x_ref[core], 0.0).astype(BF)
        out_ref[1, rows] = jnp.where(wanted, x_ref[1 - core], 0.0).astype(BF)


def score_kernel(
    count_ref,
    zp_ref,
    pick_ref,
    own_ref,
    other_ref,
    table_ref,
    ex_ref,
    wz_ref,
    out_ref,
    x_s,
    p_s,
    r_s,
    a_s,
):
    slot = pl.program_id(0)

    @pl.when((slot == 0) & (count_ref[0] > 0))
    def _():
        for start in range(0, BOX * BOX, 512):
            lanes = slice(start, start + 512)
            part = jnp.dot(pick_ref[0], own_ref[:, lanes], preferred_element_type=F32)
            part = part + jnp.dot(pick_ref[1], other_ref[:, lanes], preferred_element_type=F32)
            x_s[:, :, lanes] = part.astype(BF).reshape(CAP, 2 * KXP, 512)

    @pl.when(slot < count_ref[0])
    def _():
        table = table_ref[...]
        xr = x_s.at[slot]
        for start in range(0, PAIRS, STEP):
            part = z_stage(xr, table, start, STEP)
            part = part.astype(BF).astype(F32).reshape(STEP, KXP, 4 * BOX)
            r_s[start : start + STEP] = part[:, :KXV, :]
            mine = zp_ref[start * KXP : (start + STEP) * KXP, :].astype(F32)
            p_s[start : start + STEP] = mine.reshape(STEP, KXP, 4 * BOX)[:, :KXV, :]
        first = lax.broadcasted_iota(jnp.int32, (8, 128), 1) < BOX

        def column(col, carry):
            rows = pl.ds(pl.multiple_of(col * 8, 8), 8)

            def pair(m):
                return r_s[m % PAIRS, rows, 0:128], r_s[m % PAIRS, rows, 128:256]

            def shifted(before, now):
                return tuple(
                    pltpu.roll(jnp.where(first, n, b), BOX, 1) for b, n in zip(before, now)
                )

            def three(re, im):
                return re, im, re - im

            tiles = {m: pair(m) for m in range(-2, 2)}
            even = {m: three(*tiles[m]) for m in range(-1, 2)}
            odd = {m: three(*shifted(tiles[m - 1], tiles[m])) for m in range(-1, 2)}
            last = tiles[1]
            sums = [[jnp.zeros((8, 128), F32) for _ in range(3)] for _ in range(SHIFTS)]
            for j in range(PAIRS):
                new = pair(j + 2)
                even[j + 2] = three(*new)
                odd[j + 2] = three(*shifted(last, new))
                last = new
                pr = p_s[j, rows, 0:128]
                pi = p_s[j, rows, 128:256]
                both = pr + pi
                for u in range(-2, 2):
                    for parity, held in ((0, even), (1, odd)):
                        t = 2 * u + parity + SHIFTS // 2
                        rr, ri, rd = held[j - u]
                        sums[t][0] = sums[t][0] + pr * rr
                        sums[t][1] = sums[t][1] + pi * ri
                        sums[t][2] = sums[t][2] + both * rd
                del even[j - 1], odd[j - 1]
            for t in range(SHIFTS):
                one, two, mix = sums[t]
                a_s[t, rows, 0:128] = one + two
                a_s[t, rows, 128:256] = mix - one + two
            return carry

        lax.fori_loop(0, KXV // 8, column, 0)
        ex = ex_ref[...]
        along_x = [
            jnp.dot(ex, a_s[t].astype(BF), preferred_element_type=F32) for t in range(SHIFTS)
        ]
        cos_rows = jnp.concatenate([u[:SHIFTS] for u in along_x], axis=0).astype(BF)
        sin_rows = jnp.concatenate([u[SHIFTS:] for u in along_x], axis=0).astype(BF)
        both_rows = jnp.concatenate([cos_rows, sin_rows], axis=1)
        final = jnp.dot(both_rows, wz_ref[...], preferred_element_type=F32)
        out_ref[...] = final * (float(BOX) ** -3.5)

    @pl.when(slot >= count_ref[0])
    def _():
        out_ref[...] = jnp.zeros_like(out_ref)


def yz_kernel(*refs):
    part_refs = refs[:CHIPS]
    z_hbm, y_hbm, out_ref, z_s, g_s, z_ref, y_ref, sems = refs[CHIPS:]
    copies = [
        pltpu.make_async_copy(z_hbm, z_ref, sems.at[0]),
        pltpu.make_async_copy(y_hbm, y_ref, sems.at[1]),
    ]
    for copy in copies:
        copy.start()
    total = part_refs[0][...].astype(F32)
    for part in part_refs[1:]:
        total = total + part[...].astype(F32)
    total = total.astype(BF)
    for copy in copies:
        copy.wait()
    stacked = jnp.concatenate([total[:, 128 * j : 128 * (j + 1)] for j in range(PAIRS)], axis=0)
    z_part = jnp.dot(stacked, z_ref[...], preferred_element_type=F32)
    for j in range(PAIRS):
        for half in range(2):
            start = (2 * j + half) * PER_CHIP
            z_s[start : start + PER_CHIP] = z_part[
                j * PER_CHIP : (j + 1) * PER_CHIP, 128 * half : 128 * (half + 1)
            ]
    by_y = [z_s[pl.ds(n, BOX, stride=PER_CHIP), :].astype(BF) for n in range(PER_CHIP)]
    y_part = jnp.dot(y_ref[...], jnp.concatenate(by_y, axis=1), preferred_element_type=F32)
    first = lax.broadcasted_iota(jnp.int32, (BOX, 128), 1) < BOX
    for n in range(PER_CHIP):
        lanes = slice(128 * n, 128 * (n + 1))
        turned = pltpu.roll(y_part[BOX:, lanes], BOX, 1)
        g_s[pl.ds(n, BOX, stride=PER_CHIP), :] = y_part[:BOX, lanes] + jnp.where(first, turned, -turned)
    out_ref[...] = g_s[...].astype(BF)


def x_rows_kernel(rows_ref, table_hbm, out_ref, table_ref, sem):
    copy = pltpu.make_async_copy(table_hbm, table_ref, sem)
    copy.start()
    copy.wait()
    rows = ROT_CLS * (BOX // DOM)
    first = lax.broadcasted_iota(jnp.int32, (ROT_CLS * BOX, 128), 1) < BOX
    for ky in range(BOX // DOM):
        grid = rows_ref[:, ky * rows : (ky + 1) * rows, :].reshape(ROT_CLS * BOX, 128)
        cos_part = jnp.dot(table_ref[0], grid, preferred_element_type=F32)
        cos_part = cos_part + jnp.dot(table_ref[1], grid, preferred_element_type=F32)
        sin_part = jnp.dot(table_ref[2], grid, preferred_element_type=F32)
        sin_part = sin_part + jnp.dot(table_ref[3], grid, preferred_element_type=F32)
        turned = pltpu.roll(sin_part, BOX, 1)
        total = (cos_part + jnp.where(first, turned, -turned)) * (float(BOX) ** -1.5)
        out_ref[ky] = total.reshape(ROT_CLS, BOX, 128)


VMEM = pl.BlockSpec(memory_space=pltpu.VMEM)
HBM = pl.BlockSpec(memory_space=pltpu.HBM)
SMEM = pl.BlockSpec(memory_space=pltpu.SMEM)


def params(mib):
    return pltpu.CompilerParams(vmem_limit_bytes=mib * 1024 * 1024)


def cost(flops, moved):
    return pl.CostEstimate(flops=flops, bytes_accessed=moved, transcendentals=0)


def shards(particles, references, part_class, part_rot, bucket, bucket_weights, live_count):
    block_size = particles.shape[0]
    voxels = BOX * BOX
    columns = block_size * BOX
    to_other = [(i, i ^ 1) for i in range(DOM)]

    mine_refs = jnp.tile(references.reshape(PER_CHIP, voxels), (CHIPS, 1))

    flat = particles.reshape(columns, voxels)
    classes = part_class.reshape(block_size)
    x_half = x_half_table()
    by_core = x_half.reshape(2 * KXP, CHIPS, 2, 1, PLANES)
    by_core = np.broadcast_to(by_core, (2 * KXP, CHIPS, 2, ROT_CLS, PLANES))
    by_core = by_core.transpose(2, 0, 1, 3, 4).reshape(2, 2 * KXP, SEND)
    held = [
        pltpu.VMEM((CAP * BOX, voxels), BF),
        pltpu.SemaphoreType.DMA((CAP,)),
    ]

    def whole(*shape):
        return pl.BlockSpec(shape, lambda s: (0,) * len(shape))

    to_send, own, count, slot_rot, slot_row = pl.pallas_call(
        send_kernel,
        out_shape=(
            jax.ShapeDtypeStruct((SEND, voxels), BF),
            jax.ShapeDtypeStruct((SEND, voxels), BF),
            jax.ShapeDtypeStruct((1,), jnp.int32),
            jax.ShapeDtypeStruct((CAP,), jnp.int32),
            jax.ShapeDtypeStruct((CAP,), jnp.int32),
        ),
        in_specs=[SMEM, SMEM, SMEM, SMEM, VMEM, HBM],
        out_specs=(VMEM, VMEM, SMEM, SMEM, SMEM),
        scratch_shapes=[held[0], pltpu.VMEM((2 * SEND, CAP * BOX), BF), held[1]],
        compiler_params=params(54),
        cost_estimate=cost(1024, 1024),
        name="send",
    )(
        classes,
        part_rot,
        bucket,
        live_count,
        bucket_weights.reshape(1, -1),
        flat,
    )
    to_send, mine_refs = lax.optimization_barrier((to_send, mine_refs))
    other = lax.ppermute(to_send, "dom", to_other)
    refs_own = lax.all_to_all(
        mine_refs, "dom", 0, 0, tiled=True, axis_index_groups=SAME_CORE
    )
    by_chip = pl.pallas_call(
        pair_kernel,
        out_shape=(jax.ShapeDtypeStruct((PER_CHIP, voxels), BF),) * CHIPS,
        in_specs=[VMEM, VMEM],
        out_specs=(VMEM,) * CHIPS,
        compiler_params=params(50),
        cost_estimate=cost(1024, 1024),
        name="pair",
    )(own, other)
    slot_row, *by_chip = lax.optimization_barrier((slot_row, *by_chip))
    arrived = [by_chip[0]]
    for k in range(1, CHIPS):
        route = []
        for i in range(DOM):
            z, y, c = i // 4, (i // 2) % 2, i % 2
            route.append((i, ((z + k // 2) % 4) * 4 + (y ^ (k % 2)) * 2 + c))
        arrived.append(lax.ppermute(by_chip[k], "dom", route))

    z_table = jnp.asarray(z_complex_table().astype(BF))
    spectra = pl.pallas_call(
        spectra_kernel,
        out_shape=jax.ShapeDtypeStruct((CAP, PAIRS * KXP, 4 * BOX), BF),
        grid=(PAIRS // CHUNK,),
        in_specs=[
            SMEM,
            whole(CAP * 2 * KXP, CAP * BOX),
            HBM,
            whole(4 * BOX, 4 * BOX),
        ],
        out_specs=pl.BlockSpec((CAP, CHUNK * KXP, 4 * BOX), lambda i: (0, i, 0)),
        scratch_shapes=held,
        compiler_params=params(54),
        cost_estimate=cost(1024, 1024),
        name="spectra",
    )(slot_row, jnp.asarray(np.kron(np.eye(CAP), x_half).astype(BF)), flat, z_table)
    pick = pl.pallas_call(
        pick_kernel,
        out_shape=jax.ShapeDtypeStruct((2, CAP * 2 * KXP, SEND), BF),
        in_specs=[SMEM, VMEM],
        out_specs=VMEM,
        compiler_params=params(54),
        cost_estimate=cost(1024, 1024),
        name="pick",
    )(slot_rot, jnp.asarray(by_core, F32))

    refs_own, spectra, *arrived[1:] = lax.optimization_barrier((refs_own, spectra, *arrived[1:]))
    refs_other = lax.ppermute(refs_own, "dom", to_other)
    arrived, pick = lax.optimization_barrier((arrived, pick))
    ex, wz = shift_tables()

    slots = pl.pallas_call(
        score_kernel,
        out_shape=jax.ShapeDtypeStruct((CAP, SHIFTS * SHIFTS, 128), F32),
        grid=(CAP,),
        in_specs=[
            SMEM,
            pl.BlockSpec((None, PAIRS * KXP, 4 * BOX), lambda s: (s, 0, 0)),
            whole(2, CAP * 2 * KXP, SEND),
            whole(SEND, voxels),
            whole(SEND, voxels),
            whole(4 * BOX, 4 * BOX),
            whole(2 * SHIFTS, KXV),
            whole(8 * BOX, 128),
        ],
        out_specs=pl.BlockSpec((None, SHIFTS * SHIFTS, 128), lambda s: (s, 0, 0)),
        scratch_shapes=[
            pltpu.VMEM((CAP, 2 * KXP, voxels), BF),
            pltpu.VMEM((PAIRS, KXV, 4 * BOX), F32),
            pltpu.VMEM((PAIRS, KXV, 4 * BOX), F32),
            pltpu.VMEM((SHIFTS, KXV, 4 * BOX), F32),
        ],
        compiler_params=params(50),
        cost_estimate=cost(1024, 1024),
        name="slot_scores",
    )(
        count,
        spectra,
        pick,
        refs_own,
        refs_other,
        z_table,
        jnp.asarray(ex.astype(BF)),
        jnp.asarray(wz.astype(BF)),
    )
    slot_scores = slots[:, :, :SHIFTS].reshape(CAP, SHIFTS, SHIFTS, SHIFTS)
    slot_scores = slot_scores.transpose(0, 2, 1, 3).reshape(CAP, SHIFTS**3)
    everywhere = slot_scores
    for bit in (1, 2, 4):
        held_there = lax.ppermute(everywhere, "rot", [(i, i ^ bit) for i in range(8)])
        everywhere = jnp.concatenate([everywhere, held_there], axis=0)
    rows_all = jnp.arange(block_size, dtype=jnp.int32)
    alive = rows_all < live_count[0]
    before = (classes[:, None] == classes[None, :]) & (rows_all[None, :] < rows_all[:, None])
    place = (classes ^ lax.axis_index("rot")) * CAP + jnp.sum(before.astype(jnp.int32), axis=1)
    found = (place[:, None] == jnp.arange(8 * CAP, dtype=jnp.int32)[None, :]) & alive[:, None]
    scores = jnp.sum(jnp.where(found[:, :, None], everywhere[None, :, :], 0.0), axis=1)

    z_real = jnp.asarray(z_real_table().astype(BF))
    grids = pl.pallas_call(
        yz_kernel,
        out_shape=jax.ShapeDtypeStruct((BOX * PER_CHIP, 2 * BOX), BF),
        in_specs=[VMEM] * CHIPS + [HBM, HBM],
        out_specs=VMEM,
        scratch_shapes=[
            pltpu.VMEM((BOX * PER_CHIP, 128), F32),
            pltpu.VMEM((BOX * PER_CHIP, 128), F32),
            pltpu.VMEM((2 * BOX, 4 * BOX), BF),
            pltpu.VMEM((2 * BOX, BOX), BF),
            pltpu.SemaphoreType.DMA((2,)),
        ],
        compiler_params=params(50),
        cost_estimate=cost(1024, 1024),
        name="yz_planes",
    )(*arrived, z_real, jnp.asarray(y_table().astype(BF)))
    by_rows = lax.all_to_all(grids, "dom", 0, 0, tiled=True)
    sums = pl.pallas_call(
        x_rows_kernel,
        out_shape=jax.ShapeDtypeStruct((BOX // DOM, ROT_CLS, BOX, 2 * BOX), F32),
        in_specs=[VMEM, HBM],
        out_specs=VMEM,
        scratch_shapes=[
            pltpu.VMEM((4, ROT_CLS * BOX, ROT_CLS * BOX), BF),
            pltpu.SemaphoreType.DMA,
        ],
        compiler_params=params(50),
        name="x_rows",
    )(by_rows.reshape(DOM, PLANES * PER_CHIP, 2 * BOX), jnp.asarray(x_rows_table()))
    return (scores, sums)


def solution(mesh):
    return jax.shard_map(
        shards,
        mesh=mesh,
        in_specs=(
            P("dom", None, None),
            P("rot", "dom", None),
            P("dom", None),
            P("dom"),
            P("dom"),
            P(),
            P("dom"),
        ),
        out_specs=(P("dom", None), P("dom", "rot", None, None)),
        check_vma=False,
    )
```

```python
import math

import jax
import jax.numpy as jnp
import numpy as np
from jax import lax
from jax.experimental import pallas as pl
from jax.experimental.pallas import tpu as pltpu
from jax.sharding import PartitionSpec as P

BOX = 64
SHIFTS = 8
ROT_CLS = 4
CAP = 4
HALF = 33
KXP = 48
KXV = 40
PAIRS = BOX // 2
DOM = 16
CHIPS = DOM // 2
SAME_CORE = [[2 * chip + core for chip in range(CHIPS)] for core in range(2)]
BF = jnp.bfloat16
F32 = jnp.float32


def grid_cos_sin(rows, cols):
    theta = ((rows[:, None] * cols[None, :]) % BOX).astype(np.float64) * (2.0 * math.pi / BOX)
    return np.cos(theta), np.sin(theta)


def x_half_table():
    c, s = grid_cos_sin(np.arange(BOX), np.arange(BOX))
    out = np.zeros((2, KXP, BOX))
    out[0, :HALF] = c[:HALF]
    out[1, :HALF] = -s[:HALF]
    return out.reshape(2 * KXP, BOX)


def z_complex_table():
    c, s = grid_cos_sin(np.arange(BOX), np.arange(BOX))
    two = np.eye(2)
    return np.block([[np.kron(two, c), np.kron(two, -s)], [np.kron(two, s), np.kron(two, c)]])


def shift_tables():
    c, s = grid_cos_sin(np.arange(SHIFTS) - SHIFTS // 2, np.arange(BOX))
    fold = np.zeros((KXV,))
    fold[:HALF] = 2.0
    fold[0] = fold[HALF - 1] = 1.0
    ex = np.zeros((2 * SHIFTS, KXV))
    ex[:SHIFTS, :HALF] = c[:, :HALF]
    ex[SHIFTS:, :HALF] = s[:, :HALF]
    ex = ex * fold[None, :]
    wz = np.zeros((2, 4 * BOX, 128))
    wz[0, :, :SHIFTS] = np.concatenate([c.T, c.T, -s.T, -s.T], axis=0)
    wz[1, :, :SHIFTS] = np.concatenate([-s.T, -s.T, -c.T, -c.T], axis=0)
    return ex, wz.reshape(8 * BOX, 128)


def z_real_table():
    c, s = grid_cos_sin(np.arange(BOX), np.arange(BOX))
    return np.kron(np.eye(2), np.concatenate([c, -s], axis=1))


def y_table():
    c, s = grid_cos_sin(np.arange(BOX), np.arange(BOX))
    return np.concatenate([c, s], axis=0)


def x_rows_table():
    c, s = grid_cos_sin(np.arange(BOX), np.arange(BOX))
    full = []
    for table in (c, s):
        spread = np.einsum(
            "rq,kdx->rkdqx", np.eye(ROT_CLS), table.reshape(BOX, DOM, BOX // DOM)
        ).reshape(ROT_CLS * BOX, ROT_CLS * BOX)
        high = spread.astype(np.float32).astype(BF)
        low = (spread.astype(np.float32) - high.astype(np.float32)).astype(BF)
        full += [high, low]
    return np.stack(full)


def z_stage(src, table, start, count):
    parts = []
    for j in range(start, start + count):
        lanes = slice(128 * j, 128 * (j + 1))
        parts.append(jnp.concatenate([src[0:KXP, lanes], src[KXP : 2 * KXP, lanes]], axis=1))
    return jnp.dot(jnp.concatenate(parts, axis=0), table, preferred_element_type=F32)


STEP = 8
CHUNK = 4
PLANES = BOX // DOM
PER_CHIP = ROT_CLS * PLANES
SEND = CHIPS * PER_CHIP


LANES = 1024


def slot_copies(flat_hbm, flat_s, sems, rows_of):
    return [
        pltpu.make_async_copy(
            flat_hbm.at[pl.ds(pl.multiple_of(rows_of(slot) * BOX, BOX), BOX)],
            flat_s.at[slot * BOX : (slot + 1) * BOX],
            sems.at[slot],
        )
        for slot in range(CAP)
    ]


def send_kernel(
    class_ref,
    rot_ref,
    bucket_ref,
    live_ref,
    level_ref,
    flat_hbm,
    send_out,
    own_out,
    count_out,
    slot_rot_out,
    slot_row_out,
    flat_s,
    spread_s,
    sems,
):
    owner = lax.axis_index("rot")
    core = lax.axis_index("dom") & 1
    count = jnp.int32(0)
    slot_row = [jnp.int32(0) for _ in range(CAP)]
    slot_rot = [jnp.int32(-1) for _ in range(CAP)]
    slot_bucket = [jnp.int32(-1) for _ in range(CAP)]
    for p in range(class_ref.shape[0]):
        mine = (class_ref[p] == owner) & (p < live_ref[0])
        for slot in range(CAP):
            here = mine & (count == slot)
            slot_row[slot] = jnp.where(here, p, slot_row[slot])
            slot_rot[slot] = jnp.where(here, rot_ref[p], slot_rot[slot])
            slot_bucket[slot] = jnp.where(here, bucket_ref[p], slot_bucket[slot])
        count = count + mine.astype(jnp.int32)
    copies = slot_copies(flat_hbm, flat_s, sems, lambda slot: slot_row[slot])
    for copy in copies:
        copy.start()
    count_out[0] = count
    for slot in range(CAP):
        slot_rot_out[slot] = slot_rot[slot]
        slot_row_out[slot] = slot_row[slot]
    columns = CAP * BOX
    lane = lax.broadcasted_iota(jnp.int32, (1, columns), 1)
    col_slot, col_x = lane >> 6, lane & (BOX - 1)
    col_rot = jnp.full((1, columns), -1, jnp.int32)
    col_bucket = jnp.full((1, columns), -1, jnp.int32)
    for slot in range(CAP):
        col_rot = jnp.where(col_slot == slot, slot_rot[slot], col_rot)
        col_bucket = jnp.where(col_slot == slot, slot_bucket[slot], col_bucket)
    levels = level_ref[...].astype(F32)
    col_weight = jnp.zeros((1, columns), F32)
    for level in range(levels.shape[1]):
        value = jnp.broadcast_to(levels[:, level : level + 1], (1, columns))
        col_weight = jnp.where(col_bucket == level, value, col_weight)
    row = lax.broadcasted_iota(jnp.int32, (SEND, columns), 0)
    base = (row // PER_CHIP) * (2 * PLANES) + (row & (PLANES - 1))
    right = ((row // PLANES) & (ROT_CLS - 1)) == col_rot
    for half, to_core in enumerate((core, 1 - core)):
        hit = right & (base + to_core * PLANES == col_x)
        spread_s[half * SEND : (half + 1) * SEND] = jnp.where(hit, col_weight, 0.0).astype(BF)
    for copy in copies:
        copy.wait()
    for start in range(0, BOX * BOX, LANES):
        lanes = slice(start, start + LANES)
        part = jnp.dot(spread_s[...], flat_s[:, lanes], preferred_element_type=F32)
        own_out[:, lanes] = part[:SEND].astype(BF)
        send_out[:, lanes] = part[SEND:].astype(BF)


def pair_kernel(own_ref, other_ref, out_ref):
    out_ref[...] = (own_ref[...].astype(F32) + other_ref[...].astype(F32)).astype(BF)


def spectra_kernel(slot_row_ref, x_ref, flat_hbm, table_ref, spectra_out, flat_s, sems):
    chunk = pl.program_id(0)

    @pl.when(chunk == 0)
    def _():
        copies = slot_copies(flat_hbm, flat_s, sems, lambda slot: slot_row_ref[slot])
        for copy in copies:
            copy.start()
        for copy in copies:
            copy.wait()

    lanes = pl.ds(pl.multiple_of(chunk * 128 * CHUNK, 128 * CHUNK), 128 * CHUNK)
    along_x = jnp.dot(x_ref[...], flat_s[:, lanes], preferred_element_type=F32).astype(BF)
    table = table_ref[...]
    for slot in range(CAP):
        part = z_stage(along_x[slot * 2 * KXP : (slot + 1) * 2 * KXP], table, 0, CHUNK)
        spectra_out[slot] = part.astype(BF)


def score_kernel(
    count_ref,
    slot_rot_ref,
    zp_ref,
    x_ref,
    own_ref,
    other_ref,
    table_ref,
    ex_ref,
    wz_ref,
    out_ref,
    pick_s,
    x_s,
    p_s,
    r_s,
    a_s,
):
    slot = pl.program_id(0)

    @pl.when((slot == 0) & (count_ref[0] > 0))
    def _():
        core = lax.axis_index("dom") & 1
        ref_lane = lax.broadcasted_iota(jnp.int32, (1, SEND), 1)
        ref_rot = (ref_lane // PLANES) & (ROT_CLS - 1)
        for to in range(CAP):
            rows = slice(to * 2 * KXP, (to + 1) * 2 * KXP)
            wanted = ref_rot == slot_rot_ref[to]
            pick_s[0, rows] = jnp.where(wanted, x_ref[core], 0.0).astype(BF)
            pick_s[1, rows] = jnp.where(wanted, x_ref[1 - core], 0.0).astype(BF)
        for start in range(0, BOX * BOX, 512):
            lanes = slice(start, start + 512)
            part = jnp.dot(pick_s[0], own_ref[:, lanes], preferred_element_type=F32)
            part = part + jnp.dot(pick_s[1], other_ref[:, lanes], preferred_element_type=F32)
            x_s[:, :, lanes] = part.astype(BF).reshape(CAP, 2 * KXP, 512)

    @pl.when(slot < count_ref[0])
    def _():
        table = table_ref[...]
        xr = x_s.at[slot]
        for start in range(0, PAIRS, STEP):
            part = z_stage(xr, table, start, STEP)
            part = part.astype(BF).astype(F32).reshape(STEP, KXP, 4 * BOX)
            r_s[start : start + STEP] = part[:, :KXV, :]
            mine = zp_ref[start * KXP : (start + STEP) * KXP, :].astype(F32)
            p_s[start : start + STEP] = mine.reshape(STEP, KXP, 4 * BOX)[:, :KXV, :]
        first = lax.broadcasted_iota(jnp.int32, (8, 128), 1) < BOX

        def column(col, carry):
            rows = pl.ds(pl.multiple_of(col * 8, 8), 8)

            def pair(m):
                return r_s[m % PAIRS, rows, 0:128], r_s[m % PAIRS, rows, 128:256]

            def shifted(before, now):
                return tuple(
                    pltpu.roll(jnp.where(first, n, b), BOX, 1) for b, n in zip(before, now)
                )

            def three(re, im):
                return re, im, re - im

            tiles = {m: pair(m) for m in range(-2, 2)}
            even = {m: three(*tiles[m]) for m in range(-1, 2)}
            odd = {m: three(*shifted(tiles[m - 1], tiles[m])) for m in range(-1, 2)}
            last = tiles[1]
            sums = [[jnp.zeros((8, 128), F32) for _ in range(3)] for _ in range(SHIFTS)]
            for j in range(PAIRS):
                new = pair(j + 2)
                even[j + 2] = three(*new)
                odd[j + 2] = three(*shifted(last, new))
                last = new
                pr = p_s[j, rows, 0:128]
                pi = p_s[j, rows, 128:256]
                both = pr + pi
                for u in range(-2, 2):
                    for parity, held in ((0, even), (1, odd)):
                        t = 2 * u + parity + SHIFTS // 2
                        rr, ri, rd = held[j - u]
                        sums[t][0] = sums[t][0] + pr * rr
                        sums[t][1] = sums[t][1] + pi * ri
                        sums[t][2] = sums[t][2] + both * rd
                del even[j - 1], odd[j - 1]
            for t in range(SHIFTS):
                one, two, mix = sums[t]
                a_s[t, rows, 0:128] = one + two
                a_s[t, rows, 128:256] = mix - one + two
            return carry

        lax.fori_loop(0, KXV // 8, column, 0)
        ex = ex_ref[...]
        along_x = [
            jnp.dot(ex, a_s[t].astype(BF), preferred_element_type=F32) for t in range(SHIFTS)
        ]
        cos_rows = jnp.concatenate([u[:SHIFTS] for u in along_x], axis=0).astype(BF)
        sin_rows = jnp.concatenate([u[SHIFTS:] for u in along_x], axis=0).astype(BF)
        both_rows = jnp.concatenate([cos_rows, sin_rows], axis=1)
        final = jnp.dot(both_rows, wz_ref[...], preferred_element_type=F32)
        out_ref[...] = final * (float(BOX) ** -3.5)

    @pl.when(slot >= count_ref[0])
    def _():
        out_ref[...] = jnp.zeros_like(out_ref)


def yz_kernel(parts_ref, table_hbm, out_ref, z_s, g_s, table_ref, sem):
    copy = pltpu.make_async_copy(table_hbm, table_ref, sem)
    copy.start()
    total = parts_ref[0:PER_CHIP].astype(F32)
    for chip in range(1, CHIPS):
        total = total + parts_ref[chip * PER_CHIP : (chip + 1) * PER_CHIP].astype(F32)
    total = total.astype(BF)
    copy.wait()
    z_ref, y_ref = table_ref[: 2 * BOX], table_ref[2 * BOX :, :BOX]
    stacked = jnp.concatenate([total[:, 128 * j : 128 * (j + 1)] for j in range(PAIRS)], axis=0)
    z_part = jnp.dot(stacked, z_ref, preferred_element_type=F32)
    for j in range(PAIRS):
        for half in range(2):
            start = (2 * j + half) * PER_CHIP
            z_s[start : start + PER_CHIP] = z_part[
                j * PER_CHIP : (j + 1) * PER_CHIP, 128 * half : 128 * (half + 1)
            ]
    by_y = [z_s[pl.ds(n, BOX, stride=PER_CHIP), :].astype(BF) for n in range(PER_CHIP)]
    y_part = jnp.dot(y_ref, jnp.concatenate(by_y, axis=1), preferred_element_type=F32)
    first = lax.broadcasted_iota(jnp.int32, (BOX, 128), 1) < BOX
    for n in range(PER_CHIP):
        lanes = slice(128 * n, 128 * (n + 1))
        turned = pltpu.roll(y_part[BOX:, lanes], BOX, 1)
        g_s[pl.ds(n, BOX, stride=PER_CHIP), :] = y_part[:BOX, lanes] + jnp.where(first, turned, -turned)
    out_ref[...] = g_s[...].astype(BF)


def x_rows_kernel(rows_ref, table_hbm, out_ref, table_ref, sem):
    copy = pltpu.make_async_copy(table_hbm, table_ref, sem)
    copy.start()
    copy.wait()
    rows = ROT_CLS * (BOX // DOM)
    first = lax.broadcasted_iota(jnp.int32, (ROT_CLS * BOX, 128), 1) < BOX
    for ky in range(BOX // DOM):
        grid = rows_ref[:, ky * rows : (ky + 1) * rows, :].reshape(ROT_CLS * BOX, 128)
        cos_part = jnp.dot(table_ref[0], grid, preferred_element_type=F32)
        cos_part = cos_part + jnp.dot(table_ref[1], grid, preferred_element_type=F32)
        sin_part = jnp.dot(table_ref[2], grid, preferred_element_type=F32)
        sin_part = sin_part + jnp.dot(table_ref[3], grid, preferred_element_type=F32)
        turned = pltpu.roll(sin_part, BOX, 1)
        total = (cos_part + jnp.where(first, turned, -turned)) * (float(BOX) ** -1.5)
        out_ref[ky] = total.reshape(ROT_CLS, BOX, 128)


VMEM = pl.BlockSpec(memory_space=pltpu.VMEM)
HBM = pl.BlockSpec(memory_space=pltpu.HBM)
SMEM = pl.BlockSpec(memory_space=pltpu.SMEM)


def params(mib):
    return pltpu.CompilerParams(vmem_limit_bytes=mib * 1024 * 1024)


def cost(flops, moved):
    return pl.CostEstimate(flops=flops, bytes_accessed=moved, transcendentals=0)


def shards(particles, references, part_class, part_rot, bucket, bucket_weights, live_count):
    block_size = particles.shape[0]
    voxels = BOX * BOX
    columns = block_size * BOX
    to_other = [(i, i ^ 1) for i in range(DOM)]

    mine_refs = jnp.tile(references.reshape(PER_CHIP, voxels), (CHIPS, 1))

    flat = particles.reshape(columns, voxels)
    classes = part_class.reshape(block_size)
    x_half = x_half_table()
    by_core = x_half.reshape(2 * KXP, CHIPS, 2, 1, PLANES)
    by_core = np.broadcast_to(by_core, (2 * KXP, CHIPS, 2, ROT_CLS, PLANES))
    by_core = by_core.transpose(2, 0, 1, 3, 4).reshape(2, 2 * KXP, SEND)
    held = [
        pltpu.VMEM((CAP * BOX, voxels), BF),
        pltpu.SemaphoreType.DMA((CAP,)),
    ]

    def whole(*shape):
        return pl.BlockSpec(shape, lambda s: (0,) * len(shape))

    to_send, own, count, slot_rot, slot_row = pl.pallas_call(
        send_kernel,
        out_shape=(
            jax.ShapeDtypeStruct((SEND, voxels), BF),
            jax.ShapeDtypeStruct((SEND, voxels), BF),
            jax.ShapeDtypeStruct((1,), jnp.int32),
            jax.ShapeDtypeStruct((CAP,), jnp.int32),
            jax.ShapeDtypeStruct((CAP,), jnp.int32),
        ),
        in_specs=[SMEM, SMEM, SMEM, SMEM, VMEM, HBM],
        out_specs=(VMEM, VMEM, SMEM, SMEM, SMEM),
        scratch_shapes=[held[0], pltpu.VMEM((2 * SEND, CAP * BOX), BF), held[1]],
        compiler_params=params(54),
        cost_estimate=cost(1024, 1024),
        name="send",
    )(
        classes,
        part_rot,
        bucket,
        live_count,
        bucket_weights.reshape(1, -1),
        flat,
    )
    other = lax.ppermute(to_send, "dom", to_other)
    refs_own = lax.all_to_all(
        mine_refs, "dom", 0, 0, tiled=True, axis_index_groups=SAME_CORE
    )
    pair_sum = pl.pallas_call(
        pair_kernel,
        out_shape=jax.ShapeDtypeStruct((SEND, voxels), BF),
        in_specs=[VMEM, VMEM],
        out_specs=VMEM,
        compiler_params=params(50),
        cost_estimate=cost(1024, 1024),
        name="pair",
    )(own, other)
    arrived = lax.all_to_all(pair_sum, "dom", 0, 0, tiled=True, axis_index_groups=SAME_CORE)

    z_table = jnp.asarray(z_complex_table().astype(BF))
    spectra = pl.pallas_call(
        spectra_kernel,
        out_shape=jax.ShapeDtypeStruct((CAP, PAIRS * KXP, 4 * BOX), BF),
        grid=(PAIRS // CHUNK,),
        in_specs=[
            SMEM,
            whole(CAP * 2 * KXP, CAP * BOX),
            HBM,
            whole(4 * BOX, 4 * BOX),
        ],
        out_specs=pl.BlockSpec((CAP, CHUNK * KXP, 4 * BOX), lambda i: (0, i, 0)),
        scratch_shapes=held,
        compiler_params=params(54),
        cost_estimate=cost(1024, 1024),
        name="spectra",
    )(slot_row, jnp.asarray(np.kron(np.eye(CAP), x_half).astype(BF)), flat, z_table)

    refs_own, spectra = lax.optimization_barrier((refs_own, spectra))
    refs_other = lax.ppermute(refs_own, "dom", to_other)
    ex, wz = shift_tables()

    slots = pl.pallas_call(
        score_kernel,
        out_shape=jax.ShapeDtypeStruct((CAP, SHIFTS * SHIFTS, 128), F32),
        grid=(CAP,),
        in_specs=[
            SMEM,
            SMEM,
            pl.BlockSpec((None, PAIRS * KXP, 4 * BOX), lambda s: (s, 0, 0)),
            whole(2, 2 * KXP, SEND),
            whole(SEND, voxels),
            whole(SEND, voxels),
            whole(4 * BOX, 4 * BOX),
            whole(2 * SHIFTS, KXV),
            whole(8 * BOX, 128),
        ],
        out_specs=pl.BlockSpec((None, SHIFTS * SHIFTS, 128), lambda s: (s, 0, 0)),
        scratch_shapes=[
            pltpu.VMEM((2, CAP * 2 * KXP, SEND), BF),
            pltpu.VMEM((CAP, 2 * KXP, voxels), BF),
            pltpu.VMEM((PAIRS, KXV, 4 * BOX), F32),
            pltpu.VMEM((PAIRS, KXV, 4 * BOX), F32),
            pltpu.VMEM((SHIFTS, KXV, 4 * BOX), F32),
        ],
        compiler_params=params(50),
        cost_estimate=cost(1024, 1024),
        name="slot_scores",
    )(
        count,
        slot_rot,
        spectra,
        jnp.asarray(by_core, F32),
        refs_own,
        refs_other,
        z_table,
        jnp.asarray(ex.astype(BF)),
        jnp.asarray(wz.astype(BF)),
    )
    slot_scores = slots[:, :, :SHIFTS].reshape(CAP, SHIFTS, SHIFTS, SHIFTS)
    slot_scores = slot_scores.transpose(0, 2, 1, 3).reshape(CAP, SHIFTS**3)
    everywhere = slot_scores
    for bit in (1, 2, 4):
        held_there = lax.ppermute(everywhere, "rot", [(i, i ^ bit) for i in range(8)])
        everywhere = jnp.concatenate([everywhere, held_there], axis=0)
    rows_all = jnp.arange(block_size, dtype=jnp.int32)
    alive = rows_all < live_count[0]
    before = (classes[:, None] == classes[None, :]) & (rows_all[None, :] < rows_all[:, None])
    place = (classes ^ lax.axis_index("rot")) * CAP + jnp.sum(before.astype(jnp.int32), axis=1)
    found = (place[:, None] == jnp.arange(8 * CAP, dtype=jnp.int32)[None, :]) & alive[:, None]
    scores = jnp.sum(jnp.where(found[:, :, None], everywhere[None, :, :], 0.0), axis=1)

    yz_table = np.zeros((4 * BOX, 4 * BOX))
    yz_table[: 2 * BOX] = z_real_table()
    yz_table[2 * BOX :, :BOX] = y_table()
    grids = pl.pallas_call(
        yz_kernel,
        out_shape=jax.ShapeDtypeStruct((BOX * PER_CHIP, 2 * BOX), BF),
        in_specs=[VMEM, HBM],
        out_specs=VMEM,
        scratch_shapes=[
            pltpu.VMEM((BOX * PER_CHIP, 128), F32),
            pltpu.VMEM((BOX * PER_CHIP, 128), F32),
            pltpu.VMEM((4 * BOX, 4 * BOX), BF),
            pltpu.SemaphoreType.DMA,
        ],
        compiler_params=params(50),
        cost_estimate=cost(1024, 1024),
        name="yz_planes",
    )(arrived, jnp.asarray(yz_table.astype(BF)))
    by_rows = lax.all_to_all(grids, "dom", 0, 0, tiled=True)
    sums = pl.pallas_call(
        x_rows_kernel,
        out_shape=jax.ShapeDtypeStruct((BOX // DOM, ROT_CLS, BOX, 2 * BOX), F32),
        in_specs=[VMEM, HBM],
        out_specs=VMEM,
        scratch_shapes=[
            pltpu.VMEM((4, ROT_CLS * BOX, ROT_CLS * BOX), BF),
            pltpu.SemaphoreType.DMA,
        ],
        compiler_params=params(50),
        name="x_rows",
    )(by_rows.reshape(DOM, PLANES * PER_CHIP, 2 * BOX), jnp.asarray(x_rows_table()))
    return (scores, sums)


def solution(mesh):
    return jax.shard_map(
        shards,
        mesh=mesh,
        in_specs=(
            P("dom", None, None),
            P("rot", "dom", None),
            P("dom", None),
            P("dom"),
            P("dom"),
            P(),
            P("dom"),
        ),
        out_specs=(P("dom", None), P("dom", "rot", None, None)),
        check_vma=False,
    )
```

```python
import math

import jax
import jax.numpy as jnp
import numpy as np
from jax import lax
from jax.experimental import pallas as pl
from jax.experimental.pallas import tpu as pltpu
from jax.sharding import PartitionSpec as P

BOX = 64
SHIFTS = 8
ROT_CLS = 4
CAP = 4
HALF = 33
KXP = 48
KXV = 40
PAIRS = BOX // 2
DOM = 16
CHIPS = DOM // 2
SAME_CORE = [[2 * chip + core for chip in range(CHIPS)] for core in range(2)]
BF = jnp.bfloat16
F32 = jnp.float32


def grid_cos_sin(rows, cols):
    theta = ((rows[:, None] * cols[None, :]) % BOX).astype(np.float64) * (2.0 * math.pi / BOX)
    return np.cos(theta), np.sin(theta)


def x_half_table():
    c, s = grid_cos_sin(np.arange(BOX), np.arange(BOX))
    out = np.zeros((2, KXP, BOX))
    out[0, :HALF] = c[:HALF]
    out[1, :HALF] = -s[:HALF]
    return out.reshape(2 * KXP, BOX)


def z_complex_table():
    c, s = grid_cos_sin(np.arange(BOX), np.arange(BOX))
    two = np.eye(2)
    return np.block([[np.kron(two, c), np.kron(two, -s)], [np.kron(two, s), np.kron(two, c)]])


def shift_tables():
    c, s = grid_cos_sin(np.arange(SHIFTS) - SHIFTS // 2, np.arange(BOX))
    fold = np.zeros((KXV,))
    fold[:HALF] = 2.0
    fold[0] = fold[HALF - 1] = 1.0
    ex = np.zeros((2 * SHIFTS, KXV))
    ex[:SHIFTS, :HALF] = c[:, :HALF]
    ex[SHIFTS:, :HALF] = s[:, :HALF]
    ex = ex * fold[None, :]
    wz = np.zeros((2, 4 * BOX, 128))
    wz[0, :, :SHIFTS] = np.concatenate([c.T, c.T, -s.T, -s.T], axis=0)
    wz[1, :, :SHIFTS] = np.concatenate([-s.T, -s.T, -c.T, -c.T], axis=0)
    return ex, wz.reshape(8 * BOX, 128)


def z_real_table():
    c, s = grid_cos_sin(np.arange(BOX), np.arange(BOX))
    return np.kron(np.eye(2), np.concatenate([c, -s], axis=1))


def y_table():
    c, s = grid_cos_sin(np.arange(BOX), np.arange(BOX))
    return np.concatenate([c, s], axis=0)


def x_rows_table():
    c, s = grid_cos_sin(np.arange(BOX), np.arange(BOX))
    full = []
    for table in (c, s):
        spread = np.einsum(
            "rq,kdx->rkdqx", np.eye(ROT_CLS), table.reshape(BOX, DOM, BOX // DOM)
        ).reshape(ROT_CLS * BOX, ROT_CLS * BOX)
        high = spread.astype(np.float32).astype(BF)
        low = (spread.astype(np.float32) - high.astype(np.float32)).astype(BF)
        full += [high, low]
    return np.stack(full)


def z_stage(src, table, start, count):
    parts = []
    for j in range(start, start + count):
        lanes = slice(128 * j, 128 * (j + 1))
        parts.append(jnp.concatenate([src[0:KXP, lanes], src[KXP : 2 * KXP, lanes]], axis=1))
    return jnp.dot(jnp.concatenate(parts, axis=0), table, preferred_element_type=F32)


STEP = 8
CHUNK = 4
PLANES = BOX // DOM
PER_CHIP = ROT_CLS * PLANES
SEND = CHIPS * PER_CHIP


LANES = 1024


def slot_copies(flat_hbm, flat_s, sems, rows_of):
    return [
        pltpu.make_async_copy(
            flat_hbm.at[pl.ds(pl.multiple_of(rows_of(slot) * BOX, BOX), BOX)],
            flat_s.at[slot * BOX : (slot + 1) * BOX],
            sems.at[slot],
        )
        for slot in range(CAP)
    ]


def send_kernel(
    class_ref,
    rot_ref,
    bucket_ref,
    live_ref,
    level_ref,
    flat_hbm,
    send_out,
    own_out,
    count_out,
    slot_rot_out,
    slot_row_out,
    flat_s,
    spread_s,
    sems,
):
    owner = lax.axis_index("rot")
    core = lax.axis_index("dom") & 1
    count = jnp.int32(0)
    slot_row = [jnp.int32(0) for _ in range(CAP)]
    slot_rot = [jnp.int32(-1) for _ in range(CAP)]
    slot_bucket = [jnp.int32(-1) for _ in range(CAP)]
    for p in range(class_ref.shape[0]):
        mine = (class_ref[p] == owner) & (p < live_ref[0])
        for slot in range(CAP):
            here = mine & (count == slot)
            slot_row[slot] = jnp.where(here, p, slot_row[slot])
            slot_rot[slot] = jnp.where(here, rot_ref[p], slot_rot[slot])
            slot_bucket[slot] = jnp.where(here, bucket_ref[p], slot_bucket[slot])
        count = count + mine.astype(jnp.int32)
    copies = slot_copies(flat_hbm, flat_s, sems, lambda slot: slot_row[slot])
    for copy in copies:
        copy.start()
    count_out[0] = count
    for slot in range(CAP):
        slot_rot_out[slot] = slot_rot[slot]
        slot_row_out[slot] = slot_row[slot]
    columns = CAP * BOX
    lane = lax.broadcasted_iota(jnp.int32, (1, columns), 1)
    col_slot, col_x = lane >> 6, lane & (BOX - 1)
    col_rot = jnp.full((1, columns), -1, jnp.int32)
    col_bucket = jnp.full((1, columns), -1, jnp.int32)
    for slot in range(CAP):
        col_rot = jnp.where(col_slot == slot, slot_rot[slot], col_rot)
        col_bucket = jnp.where(col_slot == slot, slot_bucket[slot], col_bucket)
    levels = level_ref[...].astype(F32)
    col_weight = jnp.zeros((1, columns), F32)
    for level in range(levels.shape[1]):
        value = jnp.broadcast_to(levels[:, level : level + 1], (1, columns))
        col_weight = jnp.where(col_bucket == level, value, col_weight)
    row = lax.broadcasted_iota(jnp.int32, (SEND, columns), 0)
    base = (row // PER_CHIP) * (2 * PLANES) + (row & (PLANES - 1))
    right = ((row // PLANES) & (ROT_CLS - 1)) == col_rot
    for half, to_core in enumerate((core, 1 - core)):
        hit = right & (base + to_core * PLANES == col_x)
        spread_s[half * SEND : (half + 1) * SEND] = jnp.where(hit, col_weight, 0.0).astype(BF)
    for copy in copies:
        copy.wait()
    for start in range(0, BOX * BOX, LANES):
        lanes = slice(start, start + LANES)
        part = jnp.dot(spread_s[...], flat_s[:, lanes], preferred_element_type=F32)
        own_out[:, lanes] = part[:SEND].astype(BF)
        send_out[:, lanes] = part[SEND:].astype(BF)


def pair_kernel(own_ref, other_ref, out_ref):
    out_ref[...] = (own_ref[...].astype(F32) + other_ref[...].astype(F32)).astype(BF)


def spectra_kernel(slot_row_ref, count_ref, x_ref, flat_hbm, table_ref, spectra_out, flat_s, sems):
    now = pl.program_id(0)
    copies = slot_copies(flat_hbm, flat_s, sems, lambda slot: slot_row_ref[slot])
    for slot, copy in enumerate(copies):

        @pl.when((now == 0) & (slot < count_ref[0]))
        def _():
            copy.start()

    for slot, copy in enumerate(copies):

        @pl.when((now == slot) & (slot < count_ref[0]))
        def _():
            copy.wait()

    @pl.when(now < count_ref[0])
    def _():
        table = table_ref[...]
        rows = pl.ds(pl.multiple_of(now * BOX, BOX), BOX)
        for start in range(0, PAIRS, CHUNK):
            lanes = slice(128 * start, 128 * (start + CHUNK))
            along_x = jnp.dot(x_ref[...], flat_s[rows, lanes], preferred_element_type=F32)
            part = z_stage(along_x.astype(BF), table, 0, CHUNK)
            spectra_out[start * KXP : (start + CHUNK) * KXP, :] = part.astype(BF)

    @pl.when(now >= count_ref[0])
    def _():
        spectra_out[...] = jnp.zeros_like(spectra_out)


def score_kernel(
    count_ref,
    slot_rot_ref,
    zp_ref,
    x_ref,
    own_ref,
    other_ref,
    table_ref,
    ex_ref,
    wz_ref,
    out_ref,
    pick_s,
    x_s,
    p_s,
    r_s,
    a_s,
):
    slot = pl.program_id(0)

    @pl.when((slot == 0) & (count_ref[0] > 0))
    def _():
        core = lax.axis_index("dom") & 1
        ref_lane = lax.broadcasted_iota(jnp.int32, (1, SEND), 1)
        ref_rot = (ref_lane // PLANES) & (ROT_CLS - 1)
        for to in range(CAP):
            rows = slice(to * 2 * KXP, (to + 1) * 2 * KXP)
            wanted = ref_rot == slot_rot_ref[to]
            pick_s[0, rows] = jnp.where(wanted, x_ref[core], 0.0).astype(BF)
            pick_s[1, rows] = jnp.where(wanted, x_ref[1 - core], 0.0).astype(BF)
        for start in range(0, BOX * BOX, 512):
            lanes = slice(start, start + 512)
            part = jnp.dot(pick_s[0], own_ref[:, lanes], preferred_element_type=F32)
            part = part + jnp.dot(pick_s[1], other_ref[:, lanes], preferred_element_type=F32)
            x_s[:, :, lanes] = part.astype(BF).reshape(CAP, 2 * KXP, 512)

    @pl.when(slot < count_ref[0])
    def _():
        table = table_ref[...]
        xr = x_s.at[slot]
        for start in range(0, PAIRS, STEP):
            part = z_stage(xr, table, start, STEP)
            part = part.astype(BF).astype(F32).reshape(STEP, KXP, 4 * BOX)
            r_s[start : start + STEP] = part[:, :KXV, :]
            mine = zp_ref[start * KXP : (start + STEP) * KXP, :].astype(F32)
            p_s[start : start + STEP] = mine.reshape(STEP, KXP, 4 * BOX)[:, :KXV, :]
        first = lax.broadcasted_iota(jnp.int32, (8, 128), 1) < BOX

        def column(col, carry):
            rows = pl.ds(pl.multiple_of(col * 8, 8), 8)

            def pair(m):
                return r_s[m % PAIRS, rows, 0:128], r_s[m % PAIRS, rows, 128:256]

            def shifted(before, now):
                return tuple(
                    pltpu.roll(jnp.where(first, n, b), BOX, 1) for b, n in zip(before, now)
                )

            def three(re, im):
                return re, im, re - im

            tiles = {m: pair(m) for m in range(-2, 2)}
            even = {m: three(*tiles[m]) for m in range(-1, 2)}
            odd = {m: three(*shifted(tiles[m - 1], tiles[m])) for m in range(-1, 2)}
            last = tiles[1]
            sums = [[jnp.zeros((8, 128), F32) for _ in range(3)] for _ in range(SHIFTS)]
            for j in range(PAIRS):
                new = pair(j + 2)
                even[j + 2] = three(*new)
                odd[j + 2] = three(*shifted(last, new))
                last = new
                pr = p_s[j, rows, 0:128]
                pi = p_s[j, rows, 128:256]
                both = pr + pi
                for u in range(-2, 2):
                    for parity, held in ((0, even), (1, odd)):
                        t = 2 * u + parity + SHIFTS // 2
                        rr, ri, rd = held[j - u]
                        sums[t][0] = sums[t][0] + pr * rr
                        sums[t][1] = sums[t][1] + pi * ri
                        sums[t][2] = sums[t][2] + both * rd
                del even[j - 1], odd[j - 1]
            for t in range(SHIFTS):
                one, two, mix = sums[t]
                a_s[t, rows, 0:128] = one + two
                a_s[t, rows, 128:256] = mix - one + two
            return carry

        lax.fori_loop(0, KXV // 8, column, 0)
        ex = ex_ref[...]
        along_x = [
            jnp.dot(ex, a_s[t].astype(BF), preferred_element_type=F32) for t in range(SHIFTS)
        ]
        cos_rows = jnp.concatenate([u[:SHIFTS] for u in along_x], axis=0).astype(BF)
        sin_rows = jnp.concatenate([u[SHIFTS:] for u in along_x], axis=0).astype(BF)
        both_rows = jnp.concatenate([cos_rows, sin_rows], axis=1)
        final = jnp.dot(both_rows, wz_ref[...], preferred_element_type=F32)
        out_ref[...] = final * (float(BOX) ** -3.5)

    @pl.when(slot >= count_ref[0])
    def _():
        out_ref[...] = jnp.zeros_like(out_ref)


def yz_kernel(parts_ref, table_hbm, out_ref, z_s, g_s, table_ref, sem):
    copy = pltpu.make_async_copy(table_hbm, table_ref, sem)
    copy.start()
    total = parts_ref[0:PER_CHIP].astype(F32)
    for chip in range(1, CHIPS):
        total = total + parts_ref[chip * PER_CHIP : (chip + 1) * PER_CHIP].astype(F32)
    total = total.astype(BF)
    copy.wait()
    z_ref, y_ref = table_ref[: 2 * BOX], table_ref[2 * BOX :, :BOX]
    stacked = jnp.concatenate([total[:, 128 * j : 128 * (j + 1)] for j in range(PAIRS)], axis=0)
    z_part = jnp.dot(stacked, z_ref, preferred_element_type=F32)
    for j in range(PAIRS):
        for half in range(2):
            start = (2 * j + half) * PER_CHIP
            z_s[start : start + PER_CHIP] = z_part[
                j * PER_CHIP : (j + 1) * PER_CHIP, 128 * half : 128 * (half + 1)
            ]
    by_y = [z_s[pl.ds(n, BOX, stride=PER_CHIP), :].astype(BF) for n in range(PER_CHIP)]
    y_part = jnp.dot(y_ref, jnp.concatenate(by_y, axis=1), preferred_element_type=F32)
    first = lax.broadcasted_iota(jnp.int32, (BOX, 128), 1) < BOX
    for n in range(PER_CHIP):
        lanes = slice(128 * n, 128 * (n + 1))
        turned = pltpu.roll(y_part[BOX:, lanes], BOX, 1)
        g_s[pl.ds(n, BOX, stride=PER_CHIP), :] = y_part[:BOX, lanes] + jnp.where(first, turned, -turned)
    out_ref[...] = g_s[...].astype(BF)


def x_rows_kernel(rows_ref, table_hbm, out_ref, table_ref, sem):
    copy = pltpu.make_async_copy(table_hbm, table_ref, sem)
    copy.start()
    copy.wait()
    rows = ROT_CLS * (BOX // DOM)
    first = lax.broadcasted_iota(jnp.int32, (ROT_CLS * BOX, 128), 1) < BOX
    for ky in range(BOX // DOM):
        grid = rows_ref[:, ky * rows : (ky + 1) * rows, :].reshape(ROT_CLS * BOX, 128)
        cos_part = jnp.dot(table_ref[0], grid, preferred_element_type=F32)
        cos_part = cos_part + jnp.dot(table_ref[1], grid, preferred_element_type=F32)
        sin_part = jnp.dot(table_ref[2], grid, preferred_element_type=F32)
        sin_part = sin_part + jnp.dot(table_ref[3], grid, preferred_element_type=F32)
        turned = pltpu.roll(sin_part, BOX, 1)
        total = (cos_part + jnp.where(first, turned, -turned)) * (float(BOX) ** -1.5)
        out_ref[ky] = total.reshape(ROT_CLS, BOX, 128)


VMEM = pl.BlockSpec(memory_space=pltpu.VMEM)
HBM = pl.BlockSpec(memory_space=pltpu.HBM)
SMEM = pl.BlockSpec(memory_space=pltpu.SMEM)


def params(mib):
    return pltpu.CompilerParams(vmem_limit_bytes=mib * 1024 * 1024)


def cost(flops, moved):
    return pl.CostEstimate(flops=flops, bytes_accessed=moved, transcendentals=0)


def shards(particles, references, part_class, part_rot, bucket, bucket_weights, live_count):
    block_size = particles.shape[0]
    voxels = BOX * BOX
    columns = block_size * BOX
    to_other = [(i, i ^ 1) for i in range(DOM)]

    mine_refs = jnp.tile(references.reshape(PER_CHIP, voxels), (CHIPS, 1))

    flat = particles.reshape(columns, voxels)
    classes = part_class.reshape(block_size)
    x_half = x_half_table()
    by_core = x_half.reshape(2 * KXP, CHIPS, 2, 1, PLANES)
    by_core = np.broadcast_to(by_core, (2 * KXP, CHIPS, 2, ROT_CLS, PLANES))
    by_core = by_core.transpose(2, 0, 1, 3, 4).reshape(2, 2 * KXP, SEND)
    held = [
        pltpu.VMEM((CAP * BOX, voxels), BF),
        pltpu.SemaphoreType.DMA((CAP,)),
    ]

    def whole(*shape):
        return pl.BlockSpec(shape, lambda s: (0,) * len(shape))

    to_send, own, count, slot_rot, slot_row = pl.pallas_call(
        send_kernel,
        out_shape=(
            jax.ShapeDtypeStruct((SEND, voxels), BF),
            jax.ShapeDtypeStruct((SEND, voxels), BF),
            jax.ShapeDtypeStruct((1,), jnp.int32),
            jax.ShapeDtypeStruct((CAP,), jnp.int32),
            jax.ShapeDtypeStruct((CAP,), jnp.int32),
        ),
        in_specs=[SMEM, SMEM, SMEM, SMEM, VMEM, HBM],
        out_specs=(VMEM, VMEM, SMEM, SMEM, SMEM),
        scratch_shapes=[held[0], pltpu.VMEM((2 * SEND, CAP * BOX), BF), held[1]],
        compiler_params=params(54),
        cost_estimate=cost(1024, 1024),
        name="send",
    )(
        classes,
        part_rot,
        bucket,
        live_count,
        bucket_weights.reshape(1, -1),
        flat,
    )
    other = lax.ppermute(to_send, "dom", to_other)
    refs_own = lax.all_to_all(
        mine_refs, "dom", 0, 0, tiled=True, axis_index_groups=SAME_CORE
    )
    pair_sum = pl.pallas_call(
        pair_kernel,
        out_shape=jax.ShapeDtypeStruct((SEND, voxels), BF),
        in_specs=[VMEM, VMEM],
        out_specs=VMEM,
        compiler_params=params(50),
        cost_estimate=cost(1024, 1024),
        name="pair",
    )(own, other)

    z_table = jnp.asarray(z_complex_table().astype(BF))
    spectra = pl.pallas_call(
        spectra_kernel,
        out_shape=jax.ShapeDtypeStruct((CAP, PAIRS * KXP, 4 * BOX), BF),
        grid=(CAP,),
        in_specs=[SMEM, SMEM, whole(2 * KXP, BOX), HBM, whole(4 * BOX, 4 * BOX)],
        out_specs=pl.BlockSpec((None, PAIRS * KXP, 4 * BOX), lambda i: (i, 0, 0)),
        scratch_shapes=held,
        compiler_params=params(54),
        cost_estimate=cost(20 * 10**9, 1024),
        name="spectra",
    )(slot_row, count, jnp.asarray(x_half.astype(BF)), flat, z_table)

    refs_own, spectra, pair_sum = lax.optimization_barrier((refs_own, spectra, pair_sum))
    arrived = lax.all_to_all(pair_sum, "dom", 0, 0, tiled=True, axis_index_groups=SAME_CORE)
    refs_other = lax.ppermute(refs_own, "dom", to_other)
    ex, wz = shift_tables()

    slots = pl.pallas_call(
        score_kernel,
        out_shape=jax.ShapeDtypeStruct((CAP, SHIFTS * SHIFTS, 128), F32),
        grid=(CAP,),
        in_specs=[
            SMEM,
            SMEM,
            pl.BlockSpec((None, PAIRS * KXP, 4 * BOX), lambda s: (s, 0, 0)),
            whole(2, 2 * KXP, SEND),
            whole(SEND, voxels),
            whole(SEND, voxels),
            whole(4 * BOX, 4 * BOX),
            whole(2 * SHIFTS, KXV),
            whole(8 * BOX, 128),
        ],
        out_specs=pl.BlockSpec((None, SHIFTS * SHIFTS, 128), lambda s: (s, 0, 0)),
        scratch_shapes=[
            pltpu.VMEM((2, CAP * 2 * KXP, SEND), BF),
            pltpu.VMEM((CAP, 2 * KXP, voxels), BF),
            pltpu.VMEM((PAIRS, KXV, 4 * BOX), F32),
            pltpu.VMEM((PAIRS, KXV, 4 * BOX), F32),
            pltpu.VMEM((SHIFTS, KXV, 4 * BOX), F32),
        ],
        compiler_params=params(50),
        cost_estimate=cost(1024, 1024),
        name="slot_scores",
    )(
        count,
        slot_rot,
        spectra,
        jnp.asarray(by_core, F32),
        refs_own,
        refs_other,
        z_table,
        jnp.asarray(ex.astype(BF)),
        jnp.asarray(wz.astype(BF)),
    )
    slot_scores = slots[:, :, :SHIFTS].reshape(CAP, SHIFTS, SHIFTS, SHIFTS)
    slot_scores = slot_scores.transpose(0, 2, 1, 3).reshape(CAP, SHIFTS**3)
    everywhere = slot_scores
    for bit in (1, 2, 4):
        held_there = lax.ppermute(everywhere, "rot", [(i, i ^ bit) for i in range(8)])
        everywhere = jnp.concatenate([everywhere, held_there], axis=0)
    rows_all = jnp.arange(block_size, dtype=jnp.int32)
    alive = rows_all < live_count[0]
    before = (classes[:, None] == classes[None, :]) & (rows_all[None, :] < rows_all[:, None])
    place = (classes ^ lax.axis_index("rot")) * CAP + jnp.sum(before.astype(jnp.int32), axis=1)
    found = (place[:, None] == jnp.arange(8 * CAP, dtype=jnp.int32)[None, :]) & alive[:, None]
    scores = jnp.sum(jnp.where(found[:, :, None], everywhere[None, :, :], 0.0), axis=1)

    yz_table = np.zeros((4 * BOX, 4 * BOX))
    yz_table[: 2 * BOX] = z_real_table()
    yz_table[2 * BOX :, :BOX] = y_table()
    grids = pl.pallas_call(
        yz_kernel,
        out_shape=jax.ShapeDtypeStruct((BOX * PER_CHIP, 2 * BOX), BF),
        in_specs=[VMEM, HBM],
        out_specs=VMEM,
        scratch_shapes=[
            pltpu.VMEM((BOX * PER_CHIP, 128), F32),
            pltpu.VMEM((BOX * PER_CHIP, 128), F32),
            pltpu.VMEM((4 * BOX, 4 * BOX), BF),
            pltpu.SemaphoreType.DMA,
        ],
        compiler_params=params(50),
        cost_estimate=cost(1024, 1024),
        name="yz_planes",
    )(arrived, jnp.asarray(yz_table.astype(BF)))
    by_rows = lax.all_to_all(grids, "dom", 0, 0, tiled=True)
    sums = pl.pallas_call(
        x_rows_kernel,
        out_shape=jax.ShapeDtypeStruct((BOX // DOM, ROT_CLS, BOX, 2 * BOX), F32),
        in_specs=[VMEM, HBM],
        out_specs=VMEM,
        scratch_shapes=[
            pltpu.VMEM((4, ROT_CLS * BOX, ROT_CLS * BOX), BF),
            pltpu.SemaphoreType.DMA,
        ],
        compiler_params=params(50),
        name="x_rows",
    )(by_rows.reshape(DOM, PLANES * PER_CHIP, 2 * BOX), jnp.asarray(x_rows_table()))
    return (scores, sums)


def solution(mesh):
    return jax.shard_map(
        shards,
        mesh=mesh,
        in_specs=(
            P("dom", None, None),
            P("rot", "dom", None),
            P("dom", None),
            P("dom"),
            P("dom"),
            P(),
            P("dom"),
        ),
        out_specs=(P("dom", None), P("dom", "rot", None, None)),
        check_vma=False,
    )
```

```python
import math

import jax
import jax.numpy as jnp
import numpy as np
from jax import lax
from jax.experimental import pallas as pl
from jax.experimental.pallas import tpu as pltpu
from jax.sharding import PartitionSpec as P

BOX = 64
SHIFTS = 8
ROT_CLS = 4
CAP = 4
HALF = 33
KXP = 48
KXV = 40
PAIRS = BOX // 2
DOM = 16
CHIPS = DOM // 2
SAME_CORE = [[2 * chip + core for chip in range(CHIPS)] for core in range(2)]
BF = jnp.bfloat16
F32 = jnp.float32


def grid_cos_sin(rows, cols):
    theta = ((rows[:, None] * cols[None, :]) % BOX).astype(np.float64) * (2.0 * math.pi / BOX)
    return np.cos(theta), np.sin(theta)


def x_half_table():
    c, s = grid_cos_sin(np.arange(BOX), np.arange(BOX))
    out = np.zeros((2, KXP, BOX))
    out[0, :HALF] = c[:HALF]
    out[1, :HALF] = -s[:HALF]
    return out.reshape(2 * KXP, BOX)


def z_complex_table():
    c, s = grid_cos_sin(np.arange(BOX), np.arange(BOX))
    two = np.eye(2)
    return np.block([[np.kron(two, c), np.kron(two, -s)], [np.kron(two, s), np.kron(two, c)]])


def shift_tables():
    c, s = grid_cos_sin(np.arange(SHIFTS) - SHIFTS // 2, np.arange(BOX))
    fold = np.zeros((KXV,))
    fold[:HALF] = 2.0
    fold[0] = fold[HALF - 1] = 1.0
    ex = np.zeros((2 * SHIFTS, KXV))
    ex[:SHIFTS, :HALF] = c[:, :HALF]
    ex[SHIFTS:, :HALF] = s[:, :HALF]
    ex = ex * fold[None, :]
    wz = np.zeros((2, 4 * BOX, 128))
    wz[0, :, :SHIFTS] = np.concatenate([c.T, c.T, -s.T, -s.T], axis=0)
    wz[1, :, :SHIFTS] = np.concatenate([-s.T, -s.T, -c.T, -c.T], axis=0)
    return ex, wz.reshape(8 * BOX, 128)


def z_real_table():
    c, s = grid_cos_sin(np.arange(BOX), np.arange(BOX))
    return np.kron(np.eye(2), np.concatenate([c, -s], axis=1))


def y_table():
    c, s = grid_cos_sin(np.arange(BOX), np.arange(BOX))
    return np.concatenate([c, s], axis=0)


def x_rows_table():
    c, s = grid_cos_sin(np.arange(BOX), np.arange(BOX))
    return np.stack(
        [
            np.einsum(
                "rq,kdx->rkdqx", np.eye(ROT_CLS), table.reshape(BOX, DOM, BOX // DOM)
            ).reshape(ROT_CLS * BOX, ROT_CLS * BOX)
            for table in (c, s)
        ]
    )


def z_stage(src, table, start, count):
    parts = []
    for j in range(start, start + count):
        lanes = slice(128 * j, 128 * (j + 1))
        parts.append(jnp.concatenate([src[0:KXP, lanes], src[KXP : 2 * KXP, lanes]], axis=1))
    return jnp.dot(jnp.concatenate(parts, axis=0), table, preferred_element_type=F32)


STEP = 8
CHUNK = 4
PLANES = BOX // DOM
PER_CHIP = ROT_CLS * PLANES
SEND = CHIPS * PER_CHIP


def fan_kernel(refs_ref, out_hbm, wide_s, block_s, sems):
    for rot in range(ROT_CLS):
        wide_s[rot * PLANES : (rot + 1) * PLANES] = refs_ref[rot].astype(F32)
    block_s[...] = wide_s[...].astype(BF)
    copies = [
        pltpu.make_async_copy(
            block_s, out_hbm.at[chip * PER_CHIP : (chip + 1) * PER_CHIP], sems.at[chip]
        )
        for chip in range(CHIPS)
    ]
    for copy in copies:
        copy.start()
    for copy in copies:
        copy.wait()


LANES = 1024


def slot_copies(flat_hbm, flat_s, sems, rows_of):
    return [
        pltpu.make_async_copy(
            flat_hbm.at[pl.ds(pl.multiple_of(rows_of(slot) * BOX, BOX), BOX)],
            flat_s.at[slot * BOX : (slot + 1) * BOX],
            sems.at[slot],
        )
        for slot in range(CAP)
    ]


def send_kernel(
    class_ref,
    rot_ref,
    bucket_ref,
    live_ref,
    level_ref,
    flat_hbm,
    send_out,
    own_out,
    count_out,
    slot_rot_out,
    slot_row_out,
    flat_s,
    spread_s,
    sems,
):
    owner = lax.axis_index("rot")
    core = lax.axis_index("dom") & 1
    count = jnp.int32(0)
    slot_row = [jnp.int32(0) for _ in range(CAP)]
    slot_rot = [jnp.int32(-1) for _ in range(CAP)]
    slot_bucket = [jnp.int32(-1) for _ in range(CAP)]
    for p in range(class_ref.shape[0]):
        mine = (class_ref[p] == owner) & (p < live_ref[0])
        for slot in range(CAP):
            here = mine & (count == slot)
            slot_row[slot] = jnp.where(here, p, slot_row[slot])
            slot_rot[slot] = jnp.where(here, rot_ref[p], slot_rot[slot])
            slot_bucket[slot] = jnp.where(here, bucket_ref[p], slot_bucket[slot])
        count = count + mine.astype(jnp.int32)
    copies = slot_copies(flat_hbm, flat_s, sems, lambda slot: slot_row[slot])
    for copy in copies:
        copy.start()
    count_out[0] = count
    for slot in range(CAP):
        slot_rot_out[slot] = slot_rot[slot]
        slot_row_out[slot] = slot_row[slot]
    columns = CAP * BOX
    lane = lax.broadcasted_iota(jnp.int32, (1, columns), 1)
    col_slot, col_x = lane >> 6, lane & (BOX - 1)
    col_rot = jnp.full((1, columns), -1, jnp.int32)
    col_bucket = jnp.full((1, columns), -1, jnp.int32)
    for slot in range(CAP):
        col_rot = jnp.where(col_slot == slot, slot_rot[slot], col_rot)
        col_bucket = jnp.where(col_slot == slot, slot_bucket[slot], col_bucket)
    levels = level_ref[...].astype(F32)
    col_weight = jnp.zeros((1, columns), F32)
    for level in range(levels.shape[1]):
        value = jnp.broadcast_to(levels[:, level : level + 1], (1, columns))
        col_weight = jnp.where(col_bucket == level, value, col_weight)
    row = lax.broadcasted_iota(jnp.int32, (SEND, columns), 0)
    base = (row // PER_CHIP) * (2 * PLANES) + (row & (PLANES - 1))
    right = ((row // PLANES) & (ROT_CLS - 1)) == col_rot
    for half, to_core in enumerate((core, 1 - core)):
        hit = right & (base + to_core * PLANES == col_x)
        spread_s[half * SEND : (half + 1) * SEND] = jnp.where(hit, col_weight, 0.0).astype(BF)
    for copy in copies:
        copy.wait()
    for start in range(0, BOX * BOX, LANES):
        lanes = slice(start, start + LANES)
        part = jnp.dot(spread_s[...], flat_s[:, lanes], preferred_element_type=F32)
        own_out[:, lanes] = part[:SEND].astype(BF)
        send_out[:, lanes] = part[SEND:].astype(BF)


def pair_kernel(own_ref, other_ref, out_ref):
    out_ref[...] = (own_ref[...].astype(F32) + other_ref[...].astype(F32)).astype(BF)


def spectra_kernel(slot_row_ref, count_ref, x_ref, flat_hbm, table_ref, spectra_out, flat_s, sems):
    now = pl.program_id(0)
    copies = slot_copies(flat_hbm, flat_s, sems, lambda slot: slot_row_ref[slot])
    for slot, copy in enumerate(copies):

        @pl.when((now == 0) & (slot < count_ref[0]))
        def _():
            copy.start()

    for slot, copy in enumerate(copies):

        @pl.when((now == slot) & (slot < count_ref[0]))
        def _():
            copy.wait()

    @pl.when(now < count_ref[0])
    def _():
        table = table_ref[...]
        rows = pl.ds(pl.multiple_of(now * BOX, BOX), BOX)
        for start in range(0, PAIRS, CHUNK):
            lanes = slice(128 * start, 128 * (start + CHUNK))
            along_x = jnp.dot(x_ref[...], flat_s[rows, lanes], preferred_element_type=F32)
            part = z_stage(along_x.astype(BF), table, 0, CHUNK)
            spectra_out[start * KXP : (start + CHUNK) * KXP, :] = part.astype(BF)

    @pl.when(now >= count_ref[0])
    def _():
        spectra_out[...] = jnp.zeros_like(spectra_out)


def score_kernel(
    count_ref,
    slot_rot_ref,
    zp_ref,
    x_ref,
    own_ref,
    other_ref,
    table_ref,
    ex_ref,
    wz_ref,
    out_ref,
    pick_s,
    x_s,
    p_s,
    r_s,
    a_s,
):
    slot = pl.program_id(0)

    @pl.when((slot == 0) & (count_ref[0] > 0))
    def _():
        core = lax.axis_index("dom") & 1
        ref_lane = lax.broadcasted_iota(jnp.int32, (1, SEND), 1)
        ref_rot = (ref_lane // PLANES) & (ROT_CLS - 1)
        for to in range(CAP):
            rows = slice(to * 2 * KXP, (to + 1) * 2 * KXP)
            wanted = ref_rot == slot_rot_ref[to]
            pick_s[rows, :SEND] = jnp.where(wanted, x_ref[core], 0.0).astype(BF)
            pick_s[rows, SEND:] = jnp.where(wanted, x_ref[1 - core], 0.0).astype(BF)
        for start in range(0, BOX * BOX, 512):
            lanes = slice(start, start + 512)
            planes = jnp.concatenate([own_ref[:, lanes], other_ref[:, lanes]], axis=0)
            part = jnp.dot(pick_s[...], planes, preferred_element_type=F32)
            x_s[:, :, lanes] = part.astype(BF).reshape(CAP, 2 * KXP, 512)

    @pl.when(slot < count_ref[0])
    def _():
        table = table_ref[...]
        xr = x_s.at[slot]
        for start in range(0, PAIRS, STEP):
            part = z_stage(xr, table, start, STEP)
            part = part.astype(BF).astype(F32).reshape(STEP, KXP, 4 * BOX)
            r_s[start : start + STEP] = part[:, :KXV, :]
            mine = zp_ref[start * KXP : (start + STEP) * KXP, :].astype(F32)
            p_s[start : start + STEP] = mine.reshape(STEP, KXP, 4 * BOX)[:, :KXV, :]
        first = lax.broadcasted_iota(jnp.int32, (8, 128), 1) < BOX

        def column(col, carry):
            rows = pl.ds(pl.multiple_of(col * 8, 8), 8)

            def pair(m):
                return r_s[m % PAIRS, rows, 0:128], r_s[m % PAIRS, rows, 128:256]

            def shifted(before, now):
                return tuple(
                    pltpu.roll(jnp.where(first, n, b), BOX, 1) for b, n in zip(before, now)
                )

            def three(re, im):
                return re, im, re - im

            tiles = {m: pair(m) for m in range(-2, 2)}
            even = {m: three(*tiles[m]) for m in range(-1, 2)}
            odd = {m: three(*shifted(tiles[m - 1], tiles[m])) for m in range(-1, 2)}
            last = tiles[1]
            sums = [[jnp.zeros((8, 128), F32) for _ in range(3)] for _ in range(SHIFTS)]
            for j in range(PAIRS):
                new = pair(j + 2)
                even[j + 2] = three(*new)
                odd[j + 2] = three(*shifted(last, new))
                last = new
                pr = p_s[j, rows, 0:128]
                pi = p_s[j, rows, 128:256]
                both = pr + pi
                for u in range(-2, 2):
                    for parity, held in ((0, even), (1, odd)):
                        t = 2 * u + parity + SHIFTS // 2
                        rr, ri, rd = held[j - u]
                        sums[t][0] = sums[t][0] + pr * rr
                        sums[t][1] = sums[t][1] + pi * ri
                        sums[t][2] = sums[t][2] + both * rd
                del even[j - 1], odd[j - 1]
            for t in range(SHIFTS):
                one, two, mix = sums[t]
                a_s[t, rows, 0:128] = one + two
                a_s[t, rows, 128:256] = mix - one + two
            return carry

        lax.fori_loop(0, KXV // 8, column, 0)
        ex = ex_ref[...]
        along_x = [
            jnp.dot(ex, a_s[t].astype(BF), preferred_element_type=F32) for t in range(SHIFTS)
        ]
        cos_rows = jnp.concatenate([u[:SHIFTS] for u in along_x], axis=0).astype(BF)
        sin_rows = jnp.concatenate([u[SHIFTS:] for u in along_x], axis=0).astype(BF)
        both_rows = jnp.concatenate([cos_rows, sin_rows], axis=1)
        final = jnp.dot(both_rows, wz_ref[...], preferred_element_type=F32)
        out_ref[...] = final * (float(BOX) ** -3.5)

    @pl.when(slot >= count_ref[0])
    def _():
        out_ref[...] = jnp.zeros_like(out_ref)


def yz_kernel(parts_ref, table_ref, out_ref, z_s, g_s):
    total = parts_ref[0:PER_CHIP].astype(F32)
    for chip in range(1, CHIPS):
        total = total + parts_ref[chip * PER_CHIP : (chip + 1) * PER_CHIP].astype(F32)
    total = total.astype(BF)
    z_ref, y_ref = table_ref[: 2 * BOX], table_ref[2 * BOX :, :BOX]
    stacked = jnp.concatenate([total[:, 128 * j : 128 * (j + 1)] for j in range(PAIRS)], axis=0)
    z_part = jnp.dot(stacked, z_ref, preferred_element_type=F32)
    for j in range(PAIRS):
        for half in range(2):
            start = (2 * j + half) * PER_CHIP
            z_s[start : start + PER_CHIP] = z_part[
                j * PER_CHIP : (j + 1) * PER_CHIP, 128 * half : 128 * (half + 1)
            ]
    by_y = [z_s[pl.ds(n, BOX, stride=PER_CHIP), :].astype(BF) for n in range(PER_CHIP)]
    y_part = jnp.dot(y_ref, jnp.concatenate(by_y, axis=1), preferred_element_type=F32)
    first = lax.broadcasted_iota(jnp.int32, (BOX, 128), 1) < BOX
    for n in range(PER_CHIP):
        lanes = slice(128 * n, 128 * (n + 1))
        turned = pltpu.roll(y_part[BOX:, lanes], BOX, 1)
        g_s[pl.ds(n, BOX, stride=PER_CHIP), :] = y_part[:BOX, lanes] + jnp.where(first, turned, -turned)
    out_ref[...] = g_s[...].astype(BF)


def x_rows_kernel(rows_ref, table_ref, out_ref):
    rows = ROT_CLS * (BOX // DOM)
    first = lax.broadcasted_iota(jnp.int32, (ROT_CLS * BOX, 128), 1) < BOX
    for ky in range(BOX // DOM):
        grid = rows_ref[:, ky * rows : (ky + 1) * rows, :].reshape(ROT_CLS * BOX, 128)
        cos_part = jnp.dot(table_ref[0], grid, preferred_element_type=F32)
        sin_part = jnp.dot(table_ref[1], grid, preferred_element_type=F32)
        turned = pltpu.roll(sin_part, BOX, 1)
        total = (cos_part + jnp.where(first, turned, -turned)) * (float(BOX) ** -1.5)
        out_ref[ky] = total.reshape(ROT_CLS, BOX, 128)


VMEM = pl.BlockSpec(memory_space=pltpu.VMEM)
HBM = pl.BlockSpec(memory_space=pltpu.HBM)
SMEM = pl.BlockSpec(memory_space=pltpu.SMEM)


def params(mib):
    return pltpu.CompilerParams(vmem_limit_bytes=mib * 1024 * 1024)


def cost(flops, moved):
    return pl.CostEstimate(flops=flops, bytes_accessed=moved, transcendentals=0)


def shards(particles, references, part_class, part_rot, bucket, bucket_weights, live_count):
    block_size = particles.shape[0]
    voxels = BOX * BOX
    columns = block_size * BOX
    to_other = [(i, i ^ 1) for i in range(DOM)]

    mine_refs = pl.pallas_call(
        fan_kernel,
        out_shape=jax.ShapeDtypeStruct((SEND, voxels), BF),
        in_specs=[VMEM],
        out_specs=HBM,
        scratch_shapes=[
            pltpu.VMEM((PER_CHIP, voxels), F32),
            pltpu.VMEM((PER_CHIP, voxels), BF),
            pltpu.SemaphoreType.DMA((CHIPS,)),
        ],
        compiler_params=params(54),
        cost_estimate=cost(1024, 1024),
        name="fan",
    )(references)

    flat = particles.reshape(columns, voxels)
    classes = part_class.reshape(block_size)
    x_half = x_half_table()
    by_core = x_half.reshape(2 * KXP, CHIPS, 2, 1, PLANES)
    by_core = np.broadcast_to(by_core, (2 * KXP, CHIPS, 2, ROT_CLS, PLANES))
    by_core = by_core.transpose(2, 0, 1, 3, 4).reshape(2, 2 * KXP, SEND)
    held = [
        pltpu.VMEM((CAP * BOX, voxels), BF),
        pltpu.SemaphoreType.DMA((CAP,)),
    ]

    def whole(*shape):
        return pl.BlockSpec(shape, lambda s: (0,) * len(shape))

    to_send, own, count, slot_rot, slot_row = pl.pallas_call(
        send_kernel,
        out_shape=(
            jax.ShapeDtypeStruct((SEND, voxels), BF),
            jax.ShapeDtypeStruct((SEND, voxels), BF),
            jax.ShapeDtypeStruct((1,), jnp.int32),
            jax.ShapeDtypeStruct((CAP,), jnp.int32),
            jax.ShapeDtypeStruct((CAP,), jnp.int32),
        ),
        in_specs=[SMEM, SMEM, SMEM, SMEM, VMEM, HBM],
        out_specs=(VMEM, VMEM, SMEM, SMEM, SMEM),
        scratch_shapes=[held[0], pltpu.VMEM((2 * SEND, CAP * BOX), BF), held[1]],
        compiler_params=params(54),
        cost_estimate=cost(1024, 1024),
        name="send",
    )(
        classes,
        part_rot,
        bucket,
        live_count,
        bucket_weights.reshape(1, -1),
        flat,
    )
    other = lax.ppermute(to_send, "dom", to_other)
    refs_own = lax.all_to_all(
        mine_refs, "dom", 0, 0, tiled=True, axis_index_groups=SAME_CORE
    )
    pair_sum = pl.pallas_call(
        pair_kernel,
        out_shape=jax.ShapeDtypeStruct((SEND, voxels), BF),
        in_specs=[VMEM, VMEM],
        out_specs=VMEM,
        compiler_params=params(50),
        cost_estimate=cost(1024, 1024),
        name="pair",
    )(own, other)

    z_table = jnp.asarray(z_complex_table().astype(BF))
    spectra = pl.pallas_call(
        spectra_kernel,
        out_shape=jax.ShapeDtypeStruct((CAP, PAIRS * KXP, 4 * BOX), BF),
        grid=(CAP,),
        in_specs=[SMEM, SMEM, whole(2 * KXP, BOX), HBM, whole(4 * BOX, 4 * BOX)],
        out_specs=pl.BlockSpec((None, PAIRS * KXP, 4 * BOX), lambda i: (i, 0, 0)),
        scratch_shapes=held,
        compiler_params=params(54),
        cost_estimate=cost(20 * 10**9, 1024),
        name="spectra",
    )(slot_row, count, jnp.asarray(x_half.astype(BF)), flat, z_table)

    refs_own, spectra, pair_sum = lax.optimization_barrier((refs_own, spectra, pair_sum))
    arrived = lax.all_to_all(pair_sum, "dom", 0, 0, tiled=True, axis_index_groups=SAME_CORE)
    refs_other = lax.ppermute(refs_own, "dom", to_other)
    ex, wz = shift_tables()

    slots = pl.pallas_call(
        score_kernel,
        out_shape=jax.ShapeDtypeStruct((CAP, SHIFTS * SHIFTS, 128), F32),
        grid=(CAP,),
        in_specs=[
            SMEM,
            SMEM,
            pl.BlockSpec((None, PAIRS * KXP, 4 * BOX), lambda s: (s, 0, 0)),
            whole(2, 2 * KXP, SEND),
            whole(SEND, voxels),
            whole(SEND, voxels),
            whole(4 * BOX, 4 * BOX),
            whole(2 * SHIFTS, KXV),
            whole(8 * BOX, 128),
        ],
        out_specs=pl.BlockSpec((None, SHIFTS * SHIFTS, 128), lambda s: (s, 0, 0)),
        scratch_shapes=[
            pltpu.VMEM((CAP * 2 * KXP, 2 * SEND), BF),
            pltpu.VMEM((CAP, 2 * KXP, voxels), BF),
            pltpu.VMEM((PAIRS, KXV, 4 * BOX), F32),
            pltpu.VMEM((PAIRS, KXV, 4 * BOX), F32),
            pltpu.VMEM((SHIFTS, KXV, 4 * BOX), F32),
        ],
        compiler_params=params(52),
        cost_estimate=cost(1024, 1024),
        name="slot_scores",
    )(
        count,
        slot_rot,
        spectra,
        jnp.asarray(by_core, F32),
        refs_own,
        refs_other,
        z_table,
        jnp.asarray(ex.astype(BF)),
        jnp.asarray(wz.astype(BF)),
    )
    slot_scores = slots[:, :, :SHIFTS].reshape(CAP, SHIFTS, SHIFTS, SHIFTS)
    slot_scores = slot_scores.transpose(0, 2, 1, 3).reshape(CAP, SHIFTS**3)
    everywhere = slot_scores
    for bit in (1, 2, 4):
        held_there = lax.ppermute(everywhere, "rot", [(i, i ^ bit) for i in range(8)])
        everywhere = jnp.concatenate([everywhere, held_there], axis=0)
    rows_all = jnp.arange(block_size, dtype=jnp.int32)
    alive = rows_all < live_count[0]
    before = (classes[:, None] == classes[None, :]) & (rows_all[None, :] < rows_all[:, None])
    place = (classes ^ lax.axis_index("rot")) * CAP + jnp.sum(before.astype(jnp.int32), axis=1)
    found = (place[:, None] == jnp.arange(8 * CAP, dtype=jnp.int32)[None, :]) & alive[:, None]
    scores = jnp.sum(jnp.where(found[:, :, None], everywhere[None, :, :], 0.0), axis=1)

    yz_table = np.zeros((4 * BOX, 4 * BOX))
    yz_table[: 2 * BOX] = z_real_table()
    yz_table[2 * BOX :, :BOX] = y_table()
    grids = pl.pallas_call(
        yz_kernel,
        out_shape=jax.ShapeDtypeStruct((BOX * PER_CHIP, 2 * BOX), BF),
        in_specs=[VMEM, VMEM],
        out_specs=VMEM,
        scratch_shapes=[pltpu.VMEM((BOX * PER_CHIP, 128), F32)] * 2,
        compiler_params=params(50),
        cost_estimate=cost(1024, 1024),
        name="yz_planes",
    )(arrived, jnp.asarray(yz_table.astype(BF)))
    by_rows = lax.all_to_all(grids, "dom", 0, 0, tiled=True)
    sums = pl.pallas_call(
        x_rows_kernel,
        out_shape=jax.ShapeDtypeStruct((BOX // DOM, ROT_CLS, BOX, 2 * BOX), F32),
        in_specs=[VMEM, VMEM],
        out_specs=VMEM,
        compiler_params=params(50),
        name="x_rows",
    )(by_rows.reshape(DOM, PLANES * PER_CHIP, 2 * BOX), jnp.asarray(x_rows_table().astype(BF)))
    return (scores, sums)


def solution(mesh):
    return jax.shard_map(
        shards,
        mesh=mesh,
        in_specs=(
            P("dom", None, None),
            P("rot", "dom", None),
            P("dom", None),
            P("dom"),
            P("dom"),
            P(),
            P("dom"),
        ),
        out_specs=(P("dom", None), P("dom", "rot", None, None)),
        check_vma=False,
    )
```

```python
import math

import jax
import jax.numpy as jnp
import numpy as np
from jax import lax
from jax.experimental import pallas as pl
from jax.experimental.pallas import tpu as pltpu
from jax.sharding import PartitionSpec as P

BOX = 64
SHIFTS = 8
ROT_CLS = 4
CAP = 4
HALF = 33
KXP = 48
KXV = 40
PAIRS = BOX // 2
DOM = 16
CHIPS = DOM // 2
SAME_CORE = [[2 * chip + core for chip in range(CHIPS)] for core in range(2)]
BF = jnp.bfloat16
F32 = jnp.float32


def grid_cos_sin(rows, cols):
    theta = ((rows[:, None] * cols[None, :]) % BOX).astype(np.float64) * (2.0 * math.pi / BOX)
    return np.cos(theta), np.sin(theta)


def x_half_table():
    c, s = grid_cos_sin(np.arange(BOX), np.arange(BOX))
    out = np.zeros((2, KXP, BOX))
    out[0, :HALF] = c[:HALF]
    out[1, :HALF] = -s[:HALF]
    return out.reshape(2 * KXP, BOX)


def z_complex_table():
    c, s = grid_cos_sin(np.arange(BOX), np.arange(BOX))
    two = np.eye(2)
    return np.block([[np.kron(two, c), np.kron(two, -s)], [np.kron(two, s), np.kron(two, c)]])


def shift_tables():
    c, s = grid_cos_sin(np.arange(SHIFTS) - SHIFTS // 2, np.arange(BOX))
    fold = np.zeros((KXV,))
    fold[:HALF] = 2.0
    fold[0] = fold[HALF - 1] = 1.0
    ex = np.zeros((2 * SHIFTS, KXV))
    ex[:SHIFTS, :HALF] = c[:, :HALF]
    ex[SHIFTS:, :HALF] = s[:, :HALF]
    ex = ex * fold[None, :]
    wz = np.zeros((2, 4 * BOX, 128))
    wz[0, :, :SHIFTS] = np.concatenate([c.T, c.T, -s.T, -s.T], axis=0)
    wz[1, :, :SHIFTS] = np.concatenate([-s.T, -s.T, -c.T, -c.T], axis=0)
    return ex, wz.reshape(8 * BOX, 128)


def z_real_table():
    c, s = grid_cos_sin(np.arange(BOX), np.arange(BOX))
    return np.kron(np.eye(2), np.concatenate([c, -s], axis=1))


def y_table():
    c, s = grid_cos_sin(np.arange(BOX), np.arange(BOX))
    return np.concatenate([c, s], axis=0)


def x_rows_table():
    c, s = grid_cos_sin(np.arange(BOX), np.arange(BOX))
    return np.stack(
        [
            np.einsum(
                "rq,kdx->rkdqx", np.eye(ROT_CLS), table.reshape(BOX, DOM, BOX // DOM)
            ).reshape(ROT_CLS * BOX, ROT_CLS * BOX)
            for table in (c, s)
        ]
    )


def z_stage(src, table, start, count):
    parts = []
    for j in range(start, start + count):
        lanes = slice(128 * j, 128 * (j + 1))
        parts.append(jnp.concatenate([src[0:KXP, lanes], src[KXP : 2 * KXP, lanes]], axis=1))
    return jnp.dot(jnp.concatenate(parts, axis=0), table, preferred_element_type=F32)


STEP = 8
CHUNK = 4
PLANES = BOX // DOM
PER_CHIP = ROT_CLS * PLANES
SEND = CHIPS * PER_CHIP


def fan_kernel(refs_ref, out_hbm, wide_s, block_s, sems):
    for rot in range(ROT_CLS):
        wide_s[rot * PLANES : (rot + 1) * PLANES] = refs_ref[rot].astype(F32)
    block_s[...] = wide_s[...].astype(BF)
    copies = [
        pltpu.make_async_copy(
            block_s, out_hbm.at[chip * PER_CHIP : (chip + 1) * PER_CHIP], sems.at[chip]
        )
        for chip in range(CHIPS)
    ]
    for copy in copies:
        copy.start()
    for copy in copies:
        copy.wait()


LANES = 1024


def slot_copies(flat_hbm, flat_s, sems, rows_of):
    return [
        pltpu.make_async_copy(
            flat_hbm.at[pl.ds(pl.multiple_of(rows_of(slot) * BOX, BOX), BOX)],
            flat_s.at[slot * BOX : (slot + 1) * BOX],
            sems.at[slot],
        )
        for slot in range(CAP)
    ]


def send_kernel(
    class_ref,
    rot_ref,
    bucket_ref,
    live_ref,
    level_ref,
    flat_hbm,
    send_out,
    own_out,
    count_out,
    slot_rot_out,
    slot_row_out,
    flat_s,
    spread_s,
    sems,
):
    owner = lax.axis_index("rot")
    core = lax.axis_index("dom") & 1
    count = jnp.int32(0)
    slot_row = [jnp.int32(0) for _ in range(CAP)]
    slot_rot = [jnp.int32(-1) for _ in range(CAP)]
    slot_bucket = [jnp.int32(-1) for _ in range(CAP)]
    for p in range(class_ref.shape[0]):
        mine = (class_ref[p] == owner) & (p < live_ref[0])
        for slot in range(CAP):
            here = mine & (count == slot)
            slot_row[slot] = jnp.where(here, p, slot_row[slot])
            slot_rot[slot] = jnp.where(here, rot_ref[p], slot_rot[slot])
            slot_bucket[slot] = jnp.where(here, bucket_ref[p], slot_bucket[slot])
        count = count + mine.astype(jnp.int32)
    copies = slot_copies(flat_hbm, flat_s, sems, lambda slot: slot_row[slot])
    for copy in copies:
        copy.start()
    count_out[0] = count
    for slot in range(CAP):
        slot_rot_out[slot] = slot_rot[slot]
        slot_row_out[slot] = slot_row[slot]
    columns = CAP * BOX
    lane = lax.broadcasted_iota(jnp.int32, (1, columns), 1)
    col_slot, col_x = lane >> 6, lane & (BOX - 1)
    col_rot = jnp.full((1, columns), -1, jnp.int32)
    col_bucket = jnp.full((1, columns), -1, jnp.int32)
    for slot in range(CAP):
        col_rot = jnp.where(col_slot == slot, slot_rot[slot], col_rot)
        col_bucket = jnp.where(col_slot == slot, slot_bucket[slot], col_bucket)
    levels = level_ref[...].astype(F32)
    col_weight = jnp.zeros((1, columns), F32)
    for level in range(levels.shape[1]):
        value = jnp.broadcast_to(levels[:, level : level + 1], (1, columns))
        col_weight = jnp.where(col_bucket == level, value, col_weight)
    row = lax.broadcasted_iota(jnp.int32, (SEND, columns), 0)
    base = (row // PER_CHIP) * (2 * PLANES) + (row & (PLANES - 1))
    right = ((row // PLANES) & (ROT_CLS - 1)) == col_rot
    for half, to_core in enumerate((core, 1 - core)):
        hit = right & (base + to_core * PLANES == col_x)
        spread_s[half * SEND : (half + 1) * SEND] = jnp.where(hit, col_weight, 0.0).astype(BF)
    for copy in copies:
        copy.wait()
    for start in range(0, BOX * BOX, LANES):
        lanes = slice(start, start + LANES)
        part = jnp.dot(spread_s[...], flat_s[:, lanes], preferred_element_type=F32)
        own_out[:, lanes] = part[:SEND].astype(BF)
        send_out[:, lanes] = part[SEND:].astype(BF)


def pair_kernel(own_ref, other_ref, out_ref):
    out_ref[...] = (own_ref[...].astype(F32) + other_ref[...].astype(F32)).astype(BF)


def spectra_kernel(slot_row_ref, count_ref, x_ref, flat_hbm, table_ref, spectra_out, flat_s, sems):
    now = pl.program_id(0)
    copies = slot_copies(flat_hbm, flat_s, sems, lambda slot: slot_row_ref[slot])
    for slot, copy in enumerate(copies):

        @pl.when((now == 0) & (slot < count_ref[0]))
        def _():
            copy.start()

    for slot, copy in enumerate(copies):

        @pl.when((now == slot) & (slot < count_ref[0]))
        def _():
            copy.wait()

    @pl.when(now < count_ref[0])
    def _():
        table = table_ref[...]
        rows = pl.ds(pl.multiple_of(now * BOX, BOX), BOX)
        for start in range(0, PAIRS, CHUNK):
            lanes = slice(128 * start, 128 * (start + CHUNK))
            along_x = jnp.dot(x_ref[...], flat_s[rows, lanes], preferred_element_type=F32)
            part = z_stage(along_x.astype(BF), table, 0, CHUNK)
            spectra_out[start * KXP : (start + CHUNK) * KXP, :] = part.astype(BF)

    @pl.when(now >= count_ref[0])
    def _():
        spectra_out[...] = jnp.zeros_like(spectra_out)


def score_kernel(
    count_ref,
    slot_rot_ref,
    zp_hbm,
    x_ref,
    own_ref,
    other_ref,
    table_ref,
    ex_ref,
    wz_ref,
    out_ref,
    pick_s,
    x_s,
    zp_s,
    p_s,
    r_s,
    a_s,
    sems,
):
    for slot in range(CAP):

        @pl.when(slot < count_ref[0])
        def _():
            pltpu.make_async_copy(zp_hbm.at[slot], zp_s.at[slot], sems.at[slot]).start()

    out_ref[...] = jnp.zeros_like(out_ref)

    @pl.when(count_ref[0] > 0)
    def _():
        core = lax.axis_index("dom") & 1
        ref_lane = lax.broadcasted_iota(jnp.int32, (1, SEND), 1)
        ref_rot = (ref_lane // PLANES) & (ROT_CLS - 1)
        for to in range(CAP):
            rows = slice(to * 2 * KXP, (to + 1) * 2 * KXP)
            wanted = ref_rot == slot_rot_ref[to]
            pick_s[rows, :SEND] = jnp.where(wanted, x_ref[core], 0.0).astype(BF)
            pick_s[rows, SEND:] = jnp.where(wanted, x_ref[1 - core], 0.0).astype(BF)
        for start in range(0, BOX * BOX, 512):
            lanes = slice(start, start + 512)
            planes = jnp.concatenate([own_ref[:, lanes], other_ref[:, lanes]], axis=0)
            part = jnp.dot(pick_s[...], planes, preferred_element_type=F32)
            x_s[:, :, lanes] = part.astype(BF).reshape(CAP, 2 * KXP, 512)

    def one_slot(slot, carry):
        pltpu.make_async_copy(zp_hbm.at[slot], zp_s.at[slot], sems.at[slot]).wait()
        table = table_ref[...]
        xr = x_s.at[slot]
        for start in range(0, PAIRS, STEP):
            part = z_stage(xr, table, start, STEP)
            part = part.astype(BF).astype(F32).reshape(STEP, KXP, 4 * BOX)
            r_s[start : start + STEP] = part[:, :KXV, :]
            mine = zp_s[slot, start * KXP : (start + STEP) * KXP, :].astype(F32)
            p_s[start : start + STEP] = mine.reshape(STEP, KXP, 4 * BOX)[:, :KXV, :]
        first = lax.broadcasted_iota(jnp.int32, (8, 128), 1) < BOX

        def column(col, carry):
            rows = pl.ds(pl.multiple_of(col * 8, 8), 8)

            def pair(m):
                return r_s[m % PAIRS, rows, 0:128], r_s[m % PAIRS, rows, 128:256]

            def shifted(before, now):
                return tuple(
                    pltpu.roll(jnp.where(first, n, b), BOX, 1) for b, n in zip(before, now)
                )

            def three(re, im):
                return re, im, re - im

            tiles = {m: pair(m) for m in range(-2, 2)}
            even = {m: three(*tiles[m]) for m in range(-1, 2)}
            odd = {m: three(*shifted(tiles[m - 1], tiles[m])) for m in range(-1, 2)}
            last = tiles[1]
            sums = [[jnp.zeros((8, 128), F32) for _ in range(3)] for _ in range(SHIFTS)]
            for j in range(PAIRS):
                new = pair(j + 2)
                even[j + 2] = three(*new)
                odd[j + 2] = three(*shifted(last, new))
                last = new
                pr = p_s[j, rows, 0:128]
                pi = p_s[j, rows, 128:256]
                both = pr + pi
                for u in range(-2, 2):
                    for parity, held in ((0, even), (1, odd)):
                        t = 2 * u + parity + SHIFTS // 2
                        rr, ri, rd = held[j - u]
                        sums[t][0] = sums[t][0] + pr * rr
                        sums[t][1] = sums[t][1] + pi * ri
                        sums[t][2] = sums[t][2] + both * rd
                del even[j - 1], odd[j - 1]
            for t in range(SHIFTS):
                one, two, mix = sums[t]
                a_s[t, rows, 0:128] = one + two
                a_s[t, rows, 128:256] = mix - one + two
            return carry

        lax.fori_loop(0, KXV // 8, column, 0)
        ex = ex_ref[...]
        along_x = [
            jnp.dot(ex, a_s[t].astype(BF), preferred_element_type=F32) for t in range(SHIFTS)
        ]
        cos_rows = jnp.concatenate([u[:SHIFTS] for u in along_x], axis=0).astype(BF)
        sin_rows = jnp.concatenate([u[SHIFTS:] for u in along_x], axis=0).astype(BF)
        both_rows = jnp.concatenate([cos_rows, sin_rows], axis=1)
        final = jnp.dot(both_rows, wz_ref[...], preferred_element_type=F32)
        out_ref[slot] = final * (float(BOX) ** -3.5)
        return carry

    lax.fori_loop(0, count_ref[0], one_slot, 0)


def yz_kernel(parts_ref, table_ref, out_ref, z_s, g_s):
    total = parts_ref[0:PER_CHIP].astype(F32)
    for chip in range(1, CHIPS):
        total = total + parts_ref[chip * PER_CHIP : (chip + 1) * PER_CHIP].astype(F32)
    total = total.astype(BF)
    z_ref, y_ref = table_ref[: 2 * BOX], table_ref[2 * BOX :, :BOX]
    stacked = jnp.concatenate([total[:, 128 * j : 128 * (j + 1)] for j in range(PAIRS)], axis=0)
    z_part = jnp.dot(stacked, z_ref, preferred_element_type=F32)
    for j in range(PAIRS):
        for half in range(2):
            start = (2 * j + half) * PER_CHIP
            z_s[start : start + PER_CHIP] = z_part[
                j * PER_CHIP : (j + 1) * PER_CHIP, 128 * half : 128 * (half + 1)
            ]
    by_y = [z_s[pl.ds(n, BOX, stride=PER_CHIP), :].astype(BF) for n in range(PER_CHIP)]
    y_part = jnp.dot(y_ref, jnp.concatenate(by_y, axis=1), preferred_element_type=F32)
    first = lax.broadcasted_iota(jnp.int32, (BOX, 128), 1) < BOX
    for n in range(PER_CHIP):
        lanes = slice(128 * n, 128 * (n + 1))
        turned = pltpu.roll(y_part[BOX:, lanes], BOX, 1)
        g_s[pl.ds(n, BOX, stride=PER_CHIP), :] = y_part[:BOX, lanes] + jnp.where(first, turned, -turned)
    out_ref[...] = g_s[...].astype(BF)


def x_rows_kernel(rows_ref, table_ref, out_ref):
    rows = ROT_CLS * (BOX // DOM)
    first = lax.broadcasted_iota(jnp.int32, (ROT_CLS * BOX, 128), 1) < BOX
    for ky in range(BOX // DOM):
        grid = rows_ref[:, ky * rows : (ky + 1) * rows, :].reshape(ROT_CLS * BOX, 128)
        cos_part = jnp.dot(table_ref[0], grid, preferred_element_type=F32)
        sin_part = jnp.dot(table_ref[1], grid, preferred_element_type=F32)
        turned = pltpu.roll(sin_part, BOX, 1)
        total = (cos_part + jnp.where(first, turned, -turned)) * (float(BOX) ** -1.5)
        out_ref[ky] = total.reshape(ROT_CLS, BOX, 128)


VMEM = pl.BlockSpec(memory_space=pltpu.VMEM)
HBM = pl.BlockSpec(memory_space=pltpu.HBM)
SMEM = pl.BlockSpec(memory_space=pltpu.SMEM)


def params(mib):
    return pltpu.CompilerParams(vmem_limit_bytes=mib * 1024 * 1024)


def cost(flops, moved):
    return pl.CostEstimate(flops=flops, bytes_accessed=moved, transcendentals=0)


def shards(particles, references, part_class, part_rot, bucket, bucket_weights, live_count):
    block_size = particles.shape[0]
    voxels = BOX * BOX
    columns = block_size * BOX
    to_other = [(i, i ^ 1) for i in range(DOM)]

    mine_refs = pl.pallas_call(
        fan_kernel,
        out_shape=jax.ShapeDtypeStruct((SEND, voxels), BF),
        in_specs=[VMEM],
        out_specs=HBM,
        scratch_shapes=[
            pltpu.VMEM((PER_CHIP, voxels), F32),
            pltpu.VMEM((PER_CHIP, voxels), BF),
            pltpu.SemaphoreType.DMA((CHIPS,)),
        ],
        compiler_params=params(54),
        cost_estimate=cost(1024, 1024),
        name="fan",
    )(references)

    flat = particles.reshape(columns, voxels)
    classes = part_class.reshape(block_size)
    x_half = x_half_table()
    by_core = x_half.reshape(2 * KXP, CHIPS, 2, 1, PLANES)
    by_core = np.broadcast_to(by_core, (2 * KXP, CHIPS, 2, ROT_CLS, PLANES))
    by_core = by_core.transpose(2, 0, 1, 3, 4).reshape(2, 2 * KXP, SEND)
    held = [
        pltpu.VMEM((CAP * BOX, voxels), BF),
        pltpu.SemaphoreType.DMA((CAP,)),
    ]

    def whole(*shape):
        return pl.BlockSpec(shape, lambda s: (0,) * len(shape))

    to_send, own, count, slot_rot, slot_row = pl.pallas_call(
        send_kernel,
        out_shape=(
            jax.ShapeDtypeStruct((SEND, voxels), BF),
            jax.ShapeDtypeStruct((SEND, voxels), BF),
            jax.ShapeDtypeStruct((1,), jnp.int32),
            jax.ShapeDtypeStruct((CAP,), jnp.int32),
            jax.ShapeDtypeStruct((CAP,), jnp.int32),
        ),
        in_specs=[SMEM, SMEM, SMEM, SMEM, VMEM, HBM],
        out_specs=(VMEM, VMEM, SMEM, SMEM, SMEM),
        scratch_shapes=[held[0], pltpu.VMEM((2 * SEND, CAP * BOX), BF), held[1]],
        compiler_params=params(54),
        cost_estimate=cost(1024, 1024),
        name="send",
    )(
        classes,
        part_rot,
        bucket,
        live_count,
        bucket_weights.reshape(1, -1),
        flat,
    )
    other = lax.ppermute(to_send, "dom", to_other)
    refs_own = lax.all_to_all(
        mine_refs, "dom", 0, 0, tiled=True, axis_index_groups=SAME_CORE
    )
    pair_sum = pl.pallas_call(
        pair_kernel,
        out_shape=jax.ShapeDtypeStruct((SEND, voxels), BF),
        in_specs=[VMEM, VMEM],
        out_specs=VMEM,
        compiler_params=params(50),
        cost_estimate=cost(1024, 1024),
        name="pair",
    )(own, other)

    z_table = jnp.asarray(z_complex_table().astype(BF))
    spectra = pl.pallas_call(
        spectra_kernel,
        out_shape=jax.ShapeDtypeStruct((CAP, PAIRS * KXP, 4 * BOX), BF),
        grid=(CAP,),
        in_specs=[SMEM, SMEM, whole(2 * KXP, BOX), HBM, whole(4 * BOX, 4 * BOX)],
        out_specs=pl.BlockSpec((None, PAIRS * KXP, 4 * BOX), lambda i: (i, 0, 0)),
        scratch_shapes=held,
        compiler_params=params(54),
        cost_estimate=cost(20 * 10**9, 1024),
        name="spectra",
    )(slot_row, count, jnp.asarray(x_half.astype(BF)), flat, z_table)

    refs_own, spectra, pair_sum = lax.optimization_barrier((refs_own, spectra, pair_sum))
    arrived = lax.all_to_all(pair_sum, "dom", 0, 0, tiled=True, axis_index_groups=SAME_CORE)
    refs_other = lax.ppermute(refs_own, "dom", to_other)
    ex, wz = shift_tables()

    slots = pl.pallas_call(
        score_kernel,
        out_shape=jax.ShapeDtypeStruct((CAP, SHIFTS * SHIFTS, 128), F32),
        in_specs=[SMEM, SMEM, HBM] + [VMEM] * 6,
        out_specs=VMEM,
        scratch_shapes=[
            pltpu.VMEM((CAP * 2 * KXP, 2 * SEND), BF),
            pltpu.VMEM((CAP, 2 * KXP, voxels), BF),
            pltpu.VMEM((CAP, PAIRS * KXP, 4 * BOX), BF),
            pltpu.VMEM((PAIRS, KXV, 4 * BOX), F32),
            pltpu.VMEM((PAIRS, KXV, 4 * BOX), F32),
            pltpu.VMEM((SHIFTS, KXV, 4 * BOX), F32),
            pltpu.SemaphoreType.DMA((CAP,)),
        ],
        compiler_params=params(52),
        cost_estimate=cost(1024, 1024),
        name="slot_scores",
    )(
        count,
        slot_rot,
        spectra,
        jnp.asarray(by_core, F32),
        refs_own,
        refs_other,
        z_table,
        jnp.asarray(ex.astype(BF)),
        jnp.asarray(wz.astype(BF)),
    )
    slot_scores = slots[:, :, :SHIFTS].reshape(CAP, SHIFTS, SHIFTS, SHIFTS)
    slot_scores = slot_scores.transpose(0, 2, 1, 3).reshape(CAP, SHIFTS**3)
    everywhere = slot_scores
    for bit in (1, 2, 4):
        held_there = lax.ppermute(everywhere, "rot", [(i, i ^ bit) for i in range(8)])
        everywhere = jnp.concatenate([everywhere, held_there], axis=0)
    rows_all = jnp.arange(block_size, dtype=jnp.int32)
    alive = rows_all < live_count[0]
    before = (classes[:, None] == classes[None, :]) & (rows_all[None, :] < rows_all[:, None])
    place = (classes ^ lax.axis_index("rot")) * CAP + jnp.sum(before.astype(jnp.int32), axis=1)
    found = (place[:, None] == jnp.arange(8 * CAP, dtype=jnp.int32)[None, :]) & alive[:, None]
    scores = jnp.sum(jnp.where(found[:, :, None], everywhere[None, :, :], 0.0), axis=1)

    yz_table = np.zeros((4 * BOX, 4 * BOX))
    yz_table[: 2 * BOX] = z_real_table()
    yz_table[2 * BOX :, :BOX] = y_table()
    grids = pl.pallas_call(
        yz_kernel,
        out_shape=jax.ShapeDtypeStruct((BOX * PER_CHIP, 2 * BOX), BF),
        in_specs=[VMEM, VMEM],
        out_specs=VMEM,
        scratch_shapes=[pltpu.VMEM((BOX * PER_CHIP, 128), F32)] * 2,
        compiler_params=params(50),
        cost_estimate=cost(1024, 1024),
        name="yz_planes",
    )(arrived, jnp.asarray(yz_table.astype(BF)))
    by_rows = lax.all_to_all(grids, "dom", 0, 0, tiled=True)
    sums = pl.pallas_call(
        x_rows_kernel,
        out_shape=jax.ShapeDtypeStruct((BOX // DOM, ROT_CLS, BOX, 2 * BOX), F32),
        in_specs=[VMEM, VMEM],
        out_specs=VMEM,
        compiler_params=params(50),
        name="x_rows",
    )(by_rows.reshape(DOM, PLANES * PER_CHIP, 2 * BOX), jnp.asarray(x_rows_table().astype(BF)))
    return (scores, sums)


def solution(mesh):
    return jax.shard_map(
        shards,
        mesh=mesh,
        in_specs=(
            P("dom", None, None),
            P("rot", "dom", None),
            P("dom", None),
            P("dom"),
            P("dom"),
            P(),
            P("dom"),
        ),
        out_specs=(P("dom", None), P("dom", "rot", None, None)),
        check_vma=False,
    )
```

```python
import math

import jax
import jax.numpy as jnp
import numpy as np
from jax import lax
from jax.experimental import pallas as pl
from jax.experimental.pallas import tpu as pltpu
from jax.sharding import PartitionSpec as P

BOX = 64
SHIFTS = 8
ROT_CLS = 4
CAP = 4
HALF = 33
KXP = 48
KXV = 40
PAIRS = BOX // 2
DOM = 16
CHIPS = DOM // 2
LINE = DOM // 4
SAME_LINE = [[LINE * z + i for z in range(LINE)] for i in range(4)]
SAME_CORE = [[2 * chip + core for chip in range(CHIPS)] for core in range(2)]
BF = jnp.bfloat16
F32 = jnp.float32


def grid_cos_sin(rows, cols):
    theta = ((rows[:, None] * cols[None, :]) % BOX).astype(np.float64) * (2.0 * math.pi / BOX)
    return np.cos(theta), np.sin(theta)


def x_half_table():
    c, s = grid_cos_sin(np.arange(BOX), np.arange(BOX))
    out = np.zeros((2, KXP, BOX))
    out[0, :HALF] = c[:HALF]
    out[1, :HALF] = -s[:HALF]
    return out.reshape(2 * KXP, BOX)


def z_complex_table():
    c, s = grid_cos_sin(np.arange(BOX), np.arange(BOX))
    two = np.eye(2)
    return np.block([[np.kron(two, c), np.kron(two, -s)], [np.kron(two, s), np.kron(two, c)]])


def shift_tables():
    c, s = grid_cos_sin(np.arange(SHIFTS) - SHIFTS // 2, np.arange(BOX))
    fold = np.zeros((KXV,))
    fold[:HALF] = 2.0
    fold[0] = fold[HALF - 1] = 1.0
    ex = np.zeros((2 * SHIFTS, KXV))
    ex[:SHIFTS, :HALF] = c[:, :HALF]
    ex[SHIFTS:, :HALF] = s[:, :HALF]
    ex = ex * fold[None, :]
    wz = np.zeros((2, 4 * BOX, 128))
    wz[0, :, :SHIFTS] = np.concatenate([c.T, c.T, -s.T, -s.T], axis=0)
    wz[1, :, :SHIFTS] = np.concatenate([-s.T, -s.T, -c.T, -c.T], axis=0)
    return ex, wz.reshape(8 * BOX, 128)


def z_real_table():
    c, s = grid_cos_sin(np.arange(BOX), np.arange(BOX))
    return np.kron(np.eye(2), np.concatenate([c, -s], axis=1))


def y_table():
    c, s = grid_cos_sin(np.arange(BOX), np.arange(BOX))
    return np.concatenate([c, s], axis=0)


def x_rows_table():
    c, s = grid_cos_sin(np.arange(BOX), np.arange(BOX))
    return np.stack(
        [
            np.einsum(
                "rq,kdx->rkdqx", np.eye(ROT_CLS), table.reshape(BOX, DOM, BOX // DOM)
            ).reshape(ROT_CLS * BOX, ROT_CLS * BOX)
            for table in (c, s)
        ]
    )


def z_stage(src, table, start, count):
    parts = []
    for j in range(start, start + count):
        lanes = slice(128 * j, 128 * (j + 1))
        parts.append(jnp.concatenate([src[0:KXP, lanes], src[KXP : 2 * KXP, lanes]], axis=1))
    return jnp.dot(jnp.concatenate(parts, axis=0), table, preferred_element_type=F32)


STEP = 8
CHUNK = 4
PLANES = BOX // DOM
PER_CHIP = ROT_CLS * PLANES
SEND = CHIPS * PER_CHIP


def fan_kernel(refs_ref, out_hbm, wide_s, block_s, sems):
    for rot in range(ROT_CLS):
        wide_s[rot * PLANES : (rot + 1) * PLANES] = refs_ref[rot].astype(F32)
    block_s[...] = wide_s[...].astype(BF)
    copies = [
        pltpu.make_async_copy(
            block_s, out_hbm.at[chip * PER_CHIP : (chip + 1) * PER_CHIP], sems.at[chip]
        )
        for chip in range(LINE)
    ]
    for copy in copies:
        copy.start()
    for copy in copies:
        copy.wait()


LANES = 1024


def slot_copies(flat_hbm, flat_s, sems, rows_of):
    return [
        pltpu.make_async_copy(
            flat_hbm.at[pl.ds(pl.multiple_of(rows_of(slot) * BOX, BOX), BOX)],
            flat_s.at[slot * BOX : (slot + 1) * BOX],
            sems.at[slot],
        )
        for slot in range(CAP)
    ]


def send_kernel(
    class_ref,
    rot_ref,
    bucket_ref,
    live_ref,
    level_ref,
    flat_hbm,
    send_out,
    own_out,
    count_out,
    slot_rot_out,
    slot_row_out,
    flat_s,
    spread_s,
    sems,
):
    owner = lax.axis_index("rot")
    core = lax.axis_index("dom") & 1
    count = jnp.int32(0)
    slot_row = [jnp.int32(0) for _ in range(CAP)]
    slot_rot = [jnp.int32(-1) for _ in range(CAP)]
    slot_bucket = [jnp.int32(-1) for _ in range(CAP)]
    for p in range(class_ref.shape[0]):
        mine = (class_ref[p] == owner) & (p < live_ref[0])
        for slot in range(CAP):
            here = mine & (count == slot)
            slot_row[slot] = jnp.where(here, p, slot_row[slot])
            slot_rot[slot] = jnp.where(here, rot_ref[p], slot_rot[slot])
            slot_bucket[slot] = jnp.where(here, bucket_ref[p], slot_bucket[slot])
        count = count + mine.astype(jnp.int32)
    copies = slot_copies(flat_hbm, flat_s, sems, lambda slot: slot_row[slot])
    for copy in copies:
        copy.start()
    count_out[0] = count
    for slot in range(CAP):
        slot_rot_out[slot] = slot_rot[slot]
        slot_row_out[slot] = slot_row[slot]
    columns = CAP * BOX
    lane = lax.broadcasted_iota(jnp.int32, (1, columns), 1)
    col_slot, col_x = lane >> 6, lane & (BOX - 1)
    col_rot = jnp.full((1, columns), -1, jnp.int32)
    col_bucket = jnp.full((1, columns), -1, jnp.int32)
    for slot in range(CAP):
        col_rot = jnp.where(col_slot == slot, slot_rot[slot], col_rot)
        col_bucket = jnp.where(col_slot == slot, slot_bucket[slot], col_bucket)
    levels = level_ref[...].astype(F32)
    col_weight = jnp.zeros((1, columns), F32)
    for level in range(levels.shape[1]):
        value = jnp.broadcast_to(levels[:, level : level + 1], (1, columns))
        col_weight = jnp.where(col_bucket == level, value, col_weight)
    row = lax.broadcasted_iota(jnp.int32, (SEND, columns), 0)
    base = (row // PER_CHIP) * (2 * PLANES) + (row & (PLANES - 1))
    right = ((row // PLANES) & (ROT_CLS - 1)) == col_rot
    for half, to_core in enumerate((core, 1 - core)):
        hit = right & (base + to_core * PLANES == col_x)
        spread_s[half * SEND : (half + 1) * SEND] = jnp.where(hit, col_weight, 0.0).astype(BF)
    for copy in copies:
        copy.wait()
    for start in range(0, BOX * BOX, LANES):
        lanes = slice(start, start + LANES)
        part = jnp.dot(spread_s[...], flat_s[:, lanes], preferred_element_type=F32)
        own_out[:, lanes] = part[:SEND].astype(BF)
        send_out[:, lanes] = part[SEND:].astype(BF)


def pair_kernel(own_ref, other_ref, out_ref):
    out_ref[...] = (own_ref[...].astype(F32) + other_ref[...].astype(F32)).astype(BF)


def spectra_kernel(slot_row_ref, count_ref, x_ref, flat_hbm, table_ref, spectra_out, flat_s, sems):
    now = pl.program_id(0)
    copies = slot_copies(flat_hbm, flat_s, sems, lambda slot: slot_row_ref[slot])
    for slot, copy in enumerate(copies):

        @pl.when((now == 0) & (slot < count_ref[0]))
        def _():
            copy.start()

    for slot, copy in enumerate(copies):

        @pl.when((now == slot) & (slot < count_ref[0]))
        def _():
            copy.wait()

    @pl.when(now < count_ref[0])
    def _():
        table = table_ref[...]
        rows = pl.ds(pl.multiple_of(now * BOX, BOX), BOX)
        for start in range(0, PAIRS, CHUNK):
            lanes = slice(128 * start, 128 * (start + CHUNK))
            along_x = jnp.dot(x_ref[...], flat_s[rows, lanes], preferred_element_type=F32)
            part = z_stage(along_x.astype(BF), table, 0, CHUNK)
            spectra_out[start * KXP : (start + CHUNK) * KXP, :] = part.astype(BF)

    @pl.when(now >= count_ref[0])
    def _():
        spectra_out[...] = jnp.zeros_like(spectra_out)


def score_kernel(
    count_ref,
    slot_rot_ref,
    zp_hbm,
    x_ref,
    part_0_ref,
    part_1_ref,
    part_2_ref,
    part_3_ref,
    table_ref,
    ex_ref,
    wz_ref,
    out_ref,
    pick_s,
    x_s,
    zp_s,
    p_s,
    r_s,
    a_s,
    sems,
):
    for slot in range(CAP):

        @pl.when(slot < count_ref[0])
        def _():
            pltpu.make_async_copy(zp_hbm.at[slot], zp_s.at[slot], sems.at[slot]).start()

    out_ref[...] = jnp.zeros_like(out_ref)

    @pl.when(count_ref[0] > 0)
    def _():
        place = lax.axis_index("dom") & 3
        spread = jnp.concatenate([x_ref[place ^ part] for part in (0, 2, 1, 3)], axis=1)
        ref_lane = lax.broadcasted_iota(jnp.int32, (1, ROT_CLS * BOX), 1)
        ref_rot = (ref_lane // PLANES) & (ROT_CLS - 1)
        for to in range(CAP):
            rows = slice(to * 2 * KXP, (to + 1) * 2 * KXP)
            wanted = ref_rot == slot_rot_ref[to]
            pick_s[rows] = jnp.where(wanted, spread, 0.0).astype(BF)
        parts = (part_0_ref, part_1_ref, part_2_ref, part_3_ref)
        for start in range(0, BOX * BOX, 512):
            lanes = slice(start, start + 512)
            planes = jnp.concatenate([part[:, lanes] for part in parts], axis=0)
            part = jnp.dot(pick_s[...], planes, preferred_element_type=F32)
            x_s[:, :, lanes] = part.astype(BF).reshape(CAP, 2 * KXP, 512)

    def one_slot(slot, carry):
        pltpu.make_async_copy(zp_hbm.at[slot], zp_s.at[slot], sems.at[slot]).wait()
        table = table_ref[...]
        xr = x_s.at[slot]
        for start in range(0, PAIRS, STEP):
            part = z_stage(xr, table, start, STEP)
            part = part.astype(BF).astype(F32).reshape(STEP, KXP, 4 * BOX)
            r_s[start : start + STEP] = part[:, :KXV, :]
            mine = zp_s[slot, start * KXP : (start + STEP) * KXP, :].astype(F32)
            p_s[start : start + STEP] = mine.reshape(STEP, KXP, 4 * BOX)[:, :KXV, :]
        first = lax.broadcasted_iota(jnp.int32, (8, 128), 1) < BOX

        def column(col, carry):
            rows = pl.ds(pl.multiple_of(col * 8, 8), 8)

            def pair(m):
                return r_s[m % PAIRS, rows, 0:128], r_s[m % PAIRS, rows, 128:256]

            def shifted(before, now):
                return tuple(
                    pltpu.roll(jnp.where(first, n, b), BOX, 1) for b, n in zip(before, now)
                )

            def three(re, im):
                return re, im, re - im

            tiles = {m: pair(m) for m in range(-2, 2)}
            even = {m: three(*tiles[m]) for m in range(-1, 2)}
            odd = {m: three(*shifted(tiles[m - 1], tiles[m])) for m in range(-1, 2)}
            last = tiles[1]
            sums = [[jnp.zeros((8, 128), F32) for _ in range(3)] for _ in range(SHIFTS)]
            for j in range(PAIRS):
                new = pair(j + 2)
                even[j + 2] = three(*new)
                odd[j + 2] = three(*shifted(last, new))
                last = new
                pr = p_s[j, rows, 0:128]
                pi = p_s[j, rows, 128:256]
                both = pr + pi
                for u in range(-2, 2):
                    for parity, held in ((0, even), (1, odd)):
                        t = 2 * u + parity + SHIFTS // 2
                        rr, ri, rd = held[j - u]
                        sums[t][0] = sums[t][0] + pr * rr
                        sums[t][1] = sums[t][1] + pi * ri
                        sums[t][2] = sums[t][2] + both * rd
                del even[j - 1], odd[j - 1]
            for t in range(SHIFTS):
                one, two, mix = sums[t]
                a_s[t, rows, 0:128] = one + two
                a_s[t, rows, 128:256] = mix - one + two
            return carry

        lax.fori_loop(0, KXV // 8, column, 0)
        ex = ex_ref[...]
        along_x = [
            jnp.dot(ex, a_s[t].astype(BF), preferred_element_type=F32) for t in range(SHIFTS)
        ]
        cos_rows = jnp.concatenate([u[:SHIFTS] for u in along_x], axis=0).astype(BF)
        sin_rows = jnp.concatenate([u[SHIFTS:] for u in along_x], axis=0).astype(BF)
        both_rows = jnp.concatenate([cos_rows, sin_rows], axis=1)
        final = jnp.dot(both_rows, wz_ref[...], preferred_element_type=F32)
        out_ref[slot] = final * (float(BOX) ** -3.5)
        return carry

    lax.fori_loop(0, count_ref[0], one_slot, 0)


def yz_kernel(parts_ref, table_ref, out_ref, z_s, g_s):
    total = parts_ref[0:PER_CHIP].astype(F32)
    for chip in range(1, CHIPS):
        total = total + parts_ref[chip * PER_CHIP : (chip + 1) * PER_CHIP].astype(F32)
    total = total.astype(BF)
    z_ref, y_ref = table_ref[: 2 * BOX], table_ref[2 * BOX :, :BOX]
    stacked = jnp.concatenate([total[:, 128 * j : 128 * (j + 1)] for j in range(PAIRS)], axis=0)
    z_part = jnp.dot(stacked, z_ref, preferred_element_type=F32)
    for j in range(PAIRS):
        for half in range(2):
            start = (2 * j + half) * PER_CHIP
            z_s[start : start + PER_CHIP] = z_part[
                j * PER_CHIP : (j + 1) * PER_CHIP, 128 * half : 128 * (half + 1)
            ]
    by_y = [z_s[pl.ds(n, BOX, stride=PER_CHIP), :].astype(BF) for n in range(PER_CHIP)]
    y_part = jnp.dot(y_ref, jnp.concatenate(by_y, axis=1), preferred_element_type=F32)
    first = lax.broadcasted_iota(jnp.int32, (BOX, 128), 1) < BOX
    for n in range(PER_CHIP):
        lanes = slice(128 * n, 128 * (n + 1))
        turned = pltpu.roll(y_part[BOX:, lanes], BOX, 1)
        g_s[pl.ds(n, BOX, stride=PER_CHIP), :] = y_part[:BOX, lanes] + jnp.where(first, turned, -turned)
    out_ref[...] = g_s[...].astype(BF)


def x_rows_kernel(rows_ref, table_ref, out_ref):
    rows = ROT_CLS * (BOX // DOM)
    first = lax.broadcasted_iota(jnp.int32, (ROT_CLS * BOX, 128), 1) < BOX
    for ky in range(BOX // DOM):
        grid = rows_ref[:, ky * rows : (ky + 1) * rows, :].reshape(ROT_CLS * BOX, 128)
        cos_part = jnp.dot(table_ref[0], grid, preferred_element_type=F32)
        sin_part = jnp.dot(table_ref[1], grid, preferred_element_type=F32)
        turned = pltpu.roll(sin_part, BOX, 1)
        total = (cos_part + jnp.where(first, turned, -turned)) * (float(BOX) ** -1.5)
        out_ref[ky] = total.reshape(ROT_CLS, BOX, 128)


VMEM = pl.BlockSpec(memory_space=pltpu.VMEM)
HBM = pl.BlockSpec(memory_space=pltpu.HBM)
SMEM = pl.BlockSpec(memory_space=pltpu.SMEM)


def params(mib):
    return pltpu.CompilerParams(vmem_limit_bytes=mib * 1024 * 1024)


def cost(flops, moved):
    return pl.CostEstimate(flops=flops, bytes_accessed=moved, transcendentals=0)


def shards(particles, references, part_class, part_rot, bucket, bucket_weights, live_count):
    block_size = particles.shape[0]
    voxels = BOX * BOX
    columns = block_size * BOX
    to_other = [(i, i ^ 1) for i in range(DOM)]

    mine_refs = pl.pallas_call(
        fan_kernel,
        out_shape=jax.ShapeDtypeStruct((LINE * PER_CHIP, voxels), BF),
        in_specs=[VMEM],
        out_specs=HBM,
        scratch_shapes=[
            pltpu.VMEM((PER_CHIP, voxels), F32),
            pltpu.VMEM((PER_CHIP, voxels), BF),
            pltpu.SemaphoreType.DMA((LINE,)),
        ],
        compiler_params=params(54),
        cost_estimate=cost(1024, 1024),
        name="fan",
    )(references)

    flat = particles.reshape(columns, voxels)
    classes = part_class.reshape(block_size)
    x_half = x_half_table()
    by_place = x_half.reshape(2 * KXP, LINE, 4, 1, PLANES)
    by_place = np.broadcast_to(by_place, (2 * KXP, LINE, 4, ROT_CLS, PLANES))
    by_place = by_place.transpose(2, 0, 1, 3, 4).reshape(4, 2 * KXP, BOX)
    held = [
        pltpu.VMEM((CAP * BOX, voxels), BF),
        pltpu.SemaphoreType.DMA((CAP,)),
    ]

    def whole(*shape):
        return pl.BlockSpec(shape, lambda s: (0,) * len(shape))

    to_send, own, count, slot_rot, slot_row = pl.pallas_call(
        send_kernel,
        out_shape=(
            jax.ShapeDtypeStruct((SEND, voxels), BF),
            jax.ShapeDtypeStruct((SEND, voxels), BF),
            jax.ShapeDtypeStruct((1,), jnp.int32),
            jax.ShapeDtypeStruct((CAP,), jnp.int32),
            jax.ShapeDtypeStruct((CAP,), jnp.int32),
        ),
        in_specs=[SMEM, SMEM, SMEM, SMEM, VMEM, HBM],
        out_specs=(VMEM, VMEM, SMEM, SMEM, SMEM),
        scratch_shapes=[held[0], pltpu.VMEM((2 * SEND, CAP * BOX), BF), held[1]],
        compiler_params=params(54),
        cost_estimate=cost(1024, 1024),
        name="send",
    )(
        classes,
        part_rot,
        bucket,
        live_count,
        bucket_weights.reshape(1, -1),
        flat,
    )
    other = lax.ppermute(to_send, "dom", to_other)
    refs_line = lax.all_to_all(
        mine_refs, "dom", 0, 0, tiled=True, axis_index_groups=SAME_LINE
    )
    pair_sum = pl.pallas_call(
        pair_kernel,
        out_shape=jax.ShapeDtypeStruct((SEND, voxels), BF),
        in_specs=[VMEM, VMEM],
        out_specs=VMEM,
        compiler_params=params(50),
        cost_estimate=cost(1024, 1024),
        name="pair",
    )(own, other)

    refs_line, slot_row, pair_sum = lax.optimization_barrier((refs_line, slot_row, pair_sum))
    refs_y = lax.ppermute(refs_line, "dom", [(i, i ^ 2) for i in range(DOM)])
    arrived = lax.all_to_all(pair_sum, "dom", 0, 0, tiled=True, axis_index_groups=SAME_CORE)

    z_table = jnp.asarray(z_complex_table().astype(BF))
    spectra = pl.pallas_call(
        spectra_kernel,
        out_shape=jax.ShapeDtypeStruct((CAP, PAIRS * KXP, 4 * BOX), BF),
        grid=(CAP,),
        in_specs=[SMEM, SMEM, whole(2 * KXP, BOX), HBM, whole(4 * BOX, 4 * BOX)],
        out_specs=pl.BlockSpec((None, PAIRS * KXP, 4 * BOX), lambda i: (i, 0, 0)),
        scratch_shapes=held,
        compiler_params=params(54),
        cost_estimate=cost(20 * 10**9, 1024),
        name="spectra",
    )(slot_row, count, jnp.asarray(x_half.astype(BF)), flat, z_table)

    parts = (
        refs_line,
        refs_y,
        lax.ppermute(refs_line, "dom", to_other),
        lax.ppermute(refs_y, "dom", to_other),
    )
    ex, wz = shift_tables()

    slots = pl.pallas_call(
        score_kernel,
        out_shape=jax.ShapeDtypeStruct((CAP, SHIFTS * SHIFTS, 128), F32),
        in_specs=[SMEM, SMEM, HBM] + [VMEM] * 8,
        out_specs=VMEM,
        scratch_shapes=[
            pltpu.VMEM((CAP * 2 * KXP, 2 * SEND), BF),
            pltpu.VMEM((CAP, 2 * KXP, voxels), BF),
            pltpu.VMEM((CAP, PAIRS * KXP, 4 * BOX), BF),
            pltpu.VMEM((PAIRS, KXV, 4 * BOX), F32),
            pltpu.VMEM((PAIRS, KXV, 4 * BOX), F32),
            pltpu.VMEM((SHIFTS, KXV, 4 * BOX), F32),
            pltpu.SemaphoreType.DMA((CAP,)),
        ],
        compiler_params=params(51),
        cost_estimate=cost(1024, 1024),
        name="slot_scores",
    )(
        count,
        slot_rot,
        spectra,
        jnp.asarray(by_place, F32),
        *parts,
        z_table,
        jnp.asarray(ex.astype(BF)),
        jnp.asarray(wz.astype(BF)),
    )
    slot_scores = slots[:, :, :SHIFTS].reshape(CAP, SHIFTS, SHIFTS, SHIFTS)
    slot_scores = slot_scores.transpose(0, 2, 1, 3).reshape(CAP, SHIFTS**3)
    everywhere = slot_scores
    for bit in (1, 2, 4):
        held_there = lax.ppermute(everywhere, "rot", [(i, i ^ bit) for i in range(8)])
        everywhere = jnp.concatenate([everywhere, held_there], axis=0)
    rows_all = jnp.arange(block_size, dtype=jnp.int32)
    alive = rows_all < live_count[0]
    before = (classes[:, None] == classes[None, :]) & (rows_all[None, :] < rows_all[:, None])
    place = (classes ^ lax.axis_index("rot")) * CAP + jnp.sum(before.astype(jnp.int32), axis=1)
    found = (place[:, None] == jnp.arange(8 * CAP, dtype=jnp.int32)[None, :]) & alive[:, None]
    scores = jnp.sum(jnp.where(found[:, :, None], everywhere[None, :, :], 0.0), axis=1)

    yz_table = np.zeros((4 * BOX, 4 * BOX))
    yz_table[: 2 * BOX] = z_real_table()
    yz_table[2 * BOX :, :BOX] = y_table()
    grids = pl.pallas_call(
        yz_kernel,
        out_shape=jax.ShapeDtypeStruct((BOX * PER_CHIP, 2 * BOX), BF),
        in_specs=[VMEM, VMEM],
        out_specs=VMEM,
        scratch_shapes=[pltpu.VMEM((BOX * PER_CHIP, 128), F32)] * 2,
        compiler_params=params(50),
        cost_estimate=cost(1024, 1024),
        name="yz_planes",
    )(arrived, jnp.asarray(yz_table.astype(BF)))
    by_rows = lax.all_to_all(grids, "dom", 0, 0, tiled=True)
    sums = pl.pallas_call(
        x_rows_kernel,
        out_shape=jax.ShapeDtypeStruct((BOX // DOM, ROT_CLS, BOX, 2 * BOX), F32),
        in_specs=[VMEM, VMEM],
        out_specs=VMEM,
        compiler_params=params(50),
        name="x_rows",
    )(by_rows.reshape(DOM, PLANES * PER_CHIP, 2 * BOX), jnp.asarray(x_rows_table().astype(BF)))
    return (scores, sums)


def solution(mesh):
    return jax.shard_map(
        shards,
        mesh=mesh,
        in_specs=(
            P("dom", None, None),
            P("rot", "dom", None),
            P("dom", None),
            P("dom"),
            P("dom"),
            P(),
            P("dom"),
        ),
        out_specs=(P("dom", None), P("dom", "rot", None, None)),
        check_vma=False,
    )
```

```python
import math

import jax
import jax.numpy as jnp
import numpy as np
from jax import lax
from jax.experimental import pallas as pl
from jax.experimental.pallas import tpu as pltpu
from jax.sharding import PartitionSpec as P

BOX = 64
SHIFTS = 8
ROT_CLS = 4
CAP = 4
HALF = 33
KXP = 48
KXV = 40
PAIRS = BOX // 2
DOM = 16
CHIPS = DOM // 2
SAME_CORE = [[2 * chip + core for chip in range(CHIPS)] for core in range(2)]
BF = jnp.bfloat16
F32 = jnp.float32


def grid_cos_sin(rows, cols):
    theta = ((rows[:, None] * cols[None, :]) % BOX).astype(np.float64) * (2.0 * math.pi / BOX)
    return np.cos(theta), np.sin(theta)


def x_half_table():
    c, s = grid_cos_sin(np.arange(BOX), np.arange(BOX))
    out = np.zeros((2, KXP, BOX))
    out[0, :HALF] = c[:HALF]
    out[1, :HALF] = -s[:HALF]
    return out.reshape(2 * KXP, BOX)


def z_complex_table():
    c, s = grid_cos_sin(np.arange(BOX), np.arange(BOX))
    two = np.eye(2)
    return np.block([[np.kron(two, c), np.kron(two, -s)], [np.kron(two, s), np.kron(two, c)]])


def shift_tables():
    c, s = grid_cos_sin(np.arange(SHIFTS) - SHIFTS // 2, np.arange(BOX))
    fold = np.zeros((KXV,))
    fold[:HALF] = 2.0
    fold[0] = fold[HALF - 1] = 1.0
    ex = np.zeros((2 * SHIFTS, KXV))
    ex[:SHIFTS, :HALF] = c[:, :HALF]
    ex[SHIFTS:, :HALF] = s[:, :HALF]
    ex = ex * fold[None, :]
    wz = np.zeros((2, 4 * BOX, 128))
    wz[0, :, :SHIFTS] = np.concatenate([c.T, c.T, -s.T, -s.T], axis=0)
    wz[1, :, :SHIFTS] = np.concatenate([-s.T, -s.T, -c.T, -c.T], axis=0)
    return ex, wz.reshape(8 * BOX, 128)


def z_real_table():
    c, s = grid_cos_sin(np.arange(BOX), np.arange(BOX))
    return np.kron(np.eye(2), np.concatenate([c, -s], axis=1))


def y_table():
    c, s = grid_cos_sin(np.arange(BOX), np.arange(BOX))
    return np.concatenate([c, s], axis=0)


def x_rows_table():
    c, s = grid_cos_sin(np.arange(BOX), np.arange(BOX))
    return np.stack(
        [
            np.einsum(
                "rq,kdx->rkdqx", np.eye(ROT_CLS), table.reshape(BOX, DOM, BOX // DOM)
            ).reshape(ROT_CLS * BOX, ROT_CLS * BOX)
            for table in (c, s)
        ]
    )


def z_stage(src, table, start, count):
    parts = []
    for j in range(start, start + count):
        lanes = slice(128 * j, 128 * (j + 1))
        parts.append(jnp.concatenate([src[0:KXP, lanes], src[KXP : 2 * KXP, lanes]], axis=1))
    return jnp.dot(jnp.concatenate(parts, axis=0), table, preferred_element_type=F32)


STEP = 8
CHUNK = 4
PLANES = BOX // DOM
PER_CHIP = ROT_CLS * PLANES
SEND = CHIPS * PER_CHIP


def fan_kernel(refs_ref, out_hbm, wide_s, block_s, sems):
    copies = []
    for half in range(2):
        lanes = slice(half * BOX * PAIRS, (half + 1) * BOX * PAIRS)
        for rot in range(ROT_CLS):
            wide_s[rot * PLANES : (rot + 1) * PLANES, lanes] = refs_ref[rot, :, lanes].astype(F32)
        block_s[:, lanes] = wide_s[:, lanes].astype(BF)
        for chip in range(CHIPS):
            copies.append(
                pltpu.make_async_copy(
                    block_s.at[:, lanes],
                    out_hbm.at[chip * PER_CHIP : (chip + 1) * PER_CHIP, lanes],
                    sems.at[half, chip],
                )
            )
            copies[-1].start()
    for copy in copies:
        copy.wait()


LANES = 1024


def slot_copies(flat_hbm, flat_s, sems, rows_of):
    return [
        pltpu.make_async_copy(
            flat_hbm.at[pl.ds(pl.multiple_of(rows_of(slot) * BOX, BOX), BOX)],
            flat_s.at[slot * BOX : (slot + 1) * BOX],
            sems.at[slot],
        )
        for slot in range(CAP)
    ]


def send_kernel(
    class_ref,
    rot_ref,
    bucket_ref,
    live_ref,
    level_ref,
    flat_hbm,
    send_out,
    own_out,
    count_out,
    slot_rot_out,
    slot_row_out,
    flat_s,
    spread_s,
    sems,
):
    owner = lax.axis_index("rot")
    core = lax.axis_index("dom") & 1
    count = jnp.int32(0)
    slot_row = [jnp.int32(0) for _ in range(CAP)]
    slot_rot = [jnp.int32(-1) for _ in range(CAP)]
    slot_bucket = [jnp.int32(-1) for _ in range(CAP)]
    for p in range(class_ref.shape[0]):
        mine = (class_ref[p] == owner) & (p < live_ref[0])
        for slot in range(CAP):
            here = mine & (count == slot)
            slot_row[slot] = jnp.where(here, p, slot_row[slot])
            slot_rot[slot] = jnp.where(here, rot_ref[p], slot_rot[slot])
            slot_bucket[slot] = jnp.where(here, bucket_ref[p], slot_bucket[slot])
        count = count + mine.astype(jnp.int32)
    copies = slot_copies(flat_hbm, flat_s, sems, lambda slot: slot_row[slot])
    for copy in copies:
        copy.start()
    count_out[0] = count
    for slot in range(CAP):
        slot_rot_out[slot] = slot_rot[slot]
        slot_row_out[slot] = slot_row[slot]
    columns = CAP * BOX
    lane = lax.broadcasted_iota(jnp.int32, (1, columns), 1)
    col_slot, col_x = lane >> 6, lane & (BOX - 1)
    col_rot = jnp.full((1, columns), -1, jnp.int32)
    col_bucket = jnp.full((1, columns), -1, jnp.int32)
    for slot in range(CAP):
        col_rot = jnp.where(col_slot == slot, slot_rot[slot], col_rot)
        col_bucket = jnp.where(col_slot == slot, slot_bucket[slot], col_bucket)
    levels = level_ref[...].astype(F32)
    col_weight = jnp.zeros((1, columns), F32)
    for level in range(levels.shape[1]):
        value = jnp.broadcast_to(levels[:, level : level + 1], (1, columns))
        col_weight = jnp.where(col_bucket == level, value, col_weight)
    row = lax.broadcasted_iota(jnp.int32, (SEND, columns), 0)
    base = (row // PER_CHIP) * (2 * PLANES) + (row & (PLANES - 1))
    right = ((row // PLANES) & (ROT_CLS - 1)) == col_rot
    for half, to_core in enumerate((core, 1 - core)):
        hit = right & (base + to_core * PLANES == col_x)
        spread_s[half * SEND : (half + 1) * SEND] = jnp.where(hit, col_weight, 0.0).astype(BF)
    for copy in copies:
        copy.wait()
    for start in range(0, BOX * BOX, LANES):
        lanes = slice(start, start + LANES)
        part = jnp.dot(spread_s[...], flat_s[:, lanes], preferred_element_type=F32)
        own_out[:, lanes] = part[:SEND].astype(BF)
        send_out[:, lanes] = part[SEND:].astype(BF)


def pair_kernel(own_ref, other_ref, out_ref):
    out_ref[...] = (own_ref[...].astype(F32) + other_ref[...].astype(F32)).astype(BF)


def spectra_kernel(slot_row_ref, count_ref, x_ref, flat_hbm, table_ref, spectra_out, flat_s, sems):
    now = pl.program_id(0)
    copies = slot_copies(flat_hbm, flat_s, sems, lambda slot: slot_row_ref[slot])
    for slot, copy in enumerate(copies):

        @pl.when((now == 0) & (slot < count_ref[0]))
        def _():
            copy.start()

    for slot, copy in enumerate(copies):

        @pl.when((now == slot) & (slot < count_ref[0]))
        def _():
            copy.wait()

    @pl.when(now < count_ref[0])
    def _():
        table = table_ref[...]
        rows = pl.ds(pl.multiple_of(now * BOX, BOX), BOX)
        for start in range(0, PAIRS, CHUNK):
            lanes = slice(128 * start, 128 * (start + CHUNK))
            along_x = jnp.dot(x_ref[...], flat_s[rows, lanes], preferred_element_type=F32)
            part = z_stage(along_x.astype(BF), table, 0, CHUNK)
            spectra_out[start * KXP : (start + CHUNK) * KXP, :] = part.astype(BF)

    @pl.when(now >= count_ref[0])
    def _():
        spectra_out[...] = jnp.zeros_like(spectra_out)


def score_kernel(
    count_ref,
    slot_rot_ref,
    zp_hbm,
    x_ref,
    own_ref,
    other_ref,
    table_ref,
    ex_ref,
    wz_ref,
    out_ref,
    pick_s,
    x_s,
    zp_s,
    p_s,
    r_s,
    a_s,
    sems,
):
    for slot in range(CAP):

        @pl.when(slot < count_ref[0])
        def _():
            pltpu.make_async_copy(zp_hbm.at[slot], zp_s.at[slot], sems.at[slot]).start()

    out_ref[...] = jnp.zeros_like(out_ref)

    @pl.when(count_ref[0] > 0)
    def _():
        core = lax.axis_index("dom") & 1
        ref_lane = lax.broadcasted_iota(jnp.int32, (1, SEND), 1)
        ref_rot = (ref_lane // PLANES) & (ROT_CLS - 1)
        for to in range(CAP):
            rows = slice(to * 2 * KXP, (to + 1) * 2 * KXP)
            wanted = ref_rot == slot_rot_ref[to]
            pick_s[rows, :SEND] = jnp.where(wanted, x_ref[core], 0.0).astype(BF)
            pick_s[rows, SEND:] = jnp.where(wanted, x_ref[1 - core], 0.0).astype(BF)
        for start in range(0, BOX * BOX, 512):
            lanes = slice(start, start + 512)
            planes = jnp.concatenate([own_ref[:, lanes], other_ref[:, lanes]], axis=0)
            part = jnp.dot(pick_s[...], planes, preferred_element_type=F32)
            x_s[:, :, lanes] = part.astype(BF).reshape(CAP, 2 * KXP, 512)

    def one_slot(slot, carry):
        pltpu.make_async_copy(zp_hbm.at[slot], zp_s.at[slot], sems.at[slot]).wait()
        table = table_ref[...]
        xr = x_s.at[slot]
        for start in range(0, PAIRS, STEP):
            part = z_stage(xr, table, start, STEP)
            part = part.astype(BF).astype(F32).reshape(STEP, KXP, 4 * BOX)
            r_s[start : start + STEP] = part[:, :KXV, :]
            mine = zp_s[slot, start * KXP : (start + STEP) * KXP, :].astype(F32)
            p_s[start : start + STEP] = mine.reshape(STEP, KXP, 4 * BOX)[:, :KXV, :]
        first = lax.broadcasted_iota(jnp.int32, (8, 128), 1) < BOX

        def column(col, carry):
            rows = pl.ds(pl.multiple_of(col * 8, 8), 8)

            def pair(m):
                return r_s[m % PAIRS, rows, 0:128], r_s[m % PAIRS, rows, 128:256]

            def shifted(before, now):
                return tuple(
                    pltpu.roll(jnp.where(first, n, b), BOX, 1) for b, n in zip(before, now)
                )

            def three(re, im):
                return re, im, re - im

            tiles = {m: pair(m) for m in range(-2, 2)}
            even = {m: three(*tiles[m]) for m in range(-1, 2)}
            odd = {m: three(*shifted(tiles[m - 1], tiles[m])) for m in range(-1, 2)}
            last = tiles[1]
            sums = [[jnp.zeros((8, 128), F32) for _ in range(3)] for _ in range(SHIFTS)]
            for j in range(PAIRS):
                new = pair(j + 2)
                even[j + 2] = three(*new)
                odd[j + 2] = three(*shifted(last, new))
                last = new
                pr = p_s[j, rows, 0:128]
                pi = p_s[j, rows, 128:256]
                both = pr + pi
                for u in range(-2, 2):
                    for parity, held in ((0, even), (1, odd)):
                        t = 2 * u + parity + SHIFTS // 2
                        rr, ri, rd = held[j - u]
                        sums[t][0] = sums[t][0] + pr * rr
                        sums[t][1] = sums[t][1] + pi * ri
                        sums[t][2] = sums[t][2] + both * rd
                del even[j - 1], odd[j - 1]
            for t in range(SHIFTS):
                one, two, mix = sums[t]
                a_s[t, rows, 0:128] = one + two
                a_s[t, rows, 128:256] = mix - one + two
            return carry

        lax.fori_loop(0, KXV // 8, column, 0)
        ex = ex_ref[...]
        along_x = [
            jnp.dot(ex, a_s[t].astype(BF), preferred_element_type=F32) for t in range(SHIFTS)
        ]
        cos_rows = jnp.concatenate([u[:SHIFTS] for u in along_x], axis=0).astype(BF)
        sin_rows = jnp.concatenate([u[SHIFTS:] for u in along_x], axis=0).astype(BF)
        both_rows = jnp.concatenate([cos_rows, sin_rows], axis=1)
        final = jnp.dot(both_rows, wz_ref[...], preferred_element_type=F32)
        out_ref[slot] = final * (float(BOX) ** -3.5)
        return carry

    lax.fori_loop(0, count_ref[0], one_slot, 0)


def yz_kernel(parts_ref, table_ref, out_ref, z_s, g_s):
    total = parts_ref[0:PER_CHIP].astype(F32)
    for chip in range(1, CHIPS):
        total = total + parts_ref[chip * PER_CHIP : (chip + 1) * PER_CHIP].astype(F32)
    total = total.astype(BF)
    z_ref, y_ref = table_ref[: 2 * BOX], table_ref[2 * BOX :, :BOX]
    stacked = jnp.concatenate([total[:, 128 * j : 128 * (j + 1)] for j in range(PAIRS)], axis=0)
    z_part = jnp.dot(stacked, z_ref, preferred_element_type=F32)
    for j in range(PAIRS):
        for half in range(2):
            start = (2 * j + half) * PER_CHIP
            z_s[start : start + PER_CHIP] = z_part[
                j * PER_CHIP : (j + 1) * PER_CHIP, 128 * half : 128 * (half + 1)
            ]
    by_y = [z_s[pl.ds(n, BOX, stride=PER_CHIP), :].astype(BF) for n in range(PER_CHIP)]
    y_part = jnp.dot(y_ref, jnp.concatenate(by_y, axis=1), preferred_element_type=F32)
    first = lax.broadcasted_iota(jnp.int32, (BOX, 128), 1) < BOX
    for n in range(PER_CHIP):
        lanes = slice(128 * n, 128 * (n + 1))
        turned = pltpu.roll(y_part[BOX:, lanes], BOX, 1)
        g_s[pl.ds(n, BOX, stride=PER_CHIP), :] = y_part[:BOX, lanes] + jnp.where(first, turned, -turned)
    out_ref[...] = g_s[...].astype(BF)


def x_rows_kernel(rows_ref, table_ref, out_hbm, out_s, sems):
    copies = []
    rows = ROT_CLS * (BOX // DOM)
    first = lax.broadcasted_iota(jnp.int32, (ROT_CLS * BOX, 128), 1) < BOX
    for ky in range(BOX // DOM):
        grid = rows_ref[:, ky * rows : (ky + 1) * rows, :].reshape(ROT_CLS * BOX, 128)
        cos_part = jnp.dot(table_ref[0], grid, preferred_element_type=F32)
        sin_part = jnp.dot(table_ref[1], grid, preferred_element_type=F32)
        turned = pltpu.roll(sin_part, BOX, 1)
        total = (cos_part + jnp.where(first, turned, -turned)) * (float(BOX) ** -1.5)
        out_s[ky] = total.reshape(ROT_CLS, BOX, 128)
        copies.append(pltpu.make_async_copy(out_s.at[ky], out_hbm.at[ky], sems.at[ky]))
        copies[-1].start()
    for copy in copies:
        copy.wait()


VMEM = pl.BlockSpec(memory_space=pltpu.VMEM)
HBM = pl.BlockSpec(memory_space=pltpu.HBM)
SMEM = pl.BlockSpec(memory_space=pltpu.SMEM)


def params(mib):
    return pltpu.CompilerParams(vmem_limit_bytes=mib * 1024 * 1024)


def cost(flops, moved):
    return pl.CostEstimate(flops=flops, bytes_accessed=moved, transcendentals=0)


def shards(particles, references, part_class, part_rot, bucket, bucket_weights, live_count):
    block_size = particles.shape[0]
    voxels = BOX * BOX
    columns = block_size * BOX
    to_other = [(i, i ^ 1) for i in range(DOM)]

    mine_refs = pl.pallas_call(
        fan_kernel,
        out_shape=jax.ShapeDtypeStruct((SEND, voxels), BF),
        in_specs=[VMEM],
        out_specs=HBM,
        scratch_shapes=[
            pltpu.VMEM((PER_CHIP, voxels), F32),
            pltpu.VMEM((PER_CHIP, voxels), BF),
            pltpu.SemaphoreType.DMA((2, CHIPS)),
        ],
        compiler_params=params(54),
        cost_estimate=cost(1024, 1024),
        name="fan",
    )(references)

    flat = particles.reshape(columns, voxels)
    classes = part_class.reshape(block_size)
    x_half = x_half_table()
    by_core = x_half.reshape(2 * KXP, CHIPS, 2, 1, PLANES)
    by_core = np.broadcast_to(by_core, (2 * KXP, CHIPS, 2, ROT_CLS, PLANES))
    by_core = by_core.transpose(2, 0, 1, 3, 4).reshape(2, 2 * KXP, SEND)
    held = [
        pltpu.VMEM((CAP * BOX, voxels), BF),
        pltpu.SemaphoreType.DMA((CAP,)),
    ]

    def whole(*shape):
        return pl.BlockSpec(shape, lambda s: (0,) * len(shape))

    to_send, own, count, slot_rot, slot_row = pl.pallas_call(
        send_kernel,
        out_shape=(
            jax.ShapeDtypeStruct((SEND, voxels), BF),
            jax.ShapeDtypeStruct((SEND, voxels), BF),
            jax.ShapeDtypeStruct((1,), jnp.int32),
            jax.ShapeDtypeStruct((CAP,), jnp.int32),
            jax.ShapeDtypeStruct((CAP,), jnp.int32),
        ),
        in_specs=[SMEM, SMEM, SMEM, SMEM, VMEM, HBM],
        out_specs=(VMEM, VMEM, SMEM, SMEM, SMEM),
        scratch_shapes=[held[0], pltpu.VMEM((2 * SEND, CAP * BOX), BF), held[1]],
        compiler_params=params(54),
        cost_estimate=cost(1024, 1024),
        name="send",
    )(
        classes,
        part_rot,
        bucket,
        live_count,
        bucket_weights.reshape(1, -1),
        flat,
    )
    other = lax.ppermute(to_send, "dom", to_other)
    refs_own = lax.all_to_all(
        mine_refs, "dom", 0, 0, tiled=True, axis_index_groups=SAME_CORE
    )
    pair_sum = pl.pallas_call(
        pair_kernel,
        out_shape=jax.ShapeDtypeStruct((SEND, voxels), BF),
        in_specs=[VMEM, VMEM],
        out_specs=VMEM,
        compiler_params=params(50),
        cost_estimate=cost(1024, 1024),
        name="pair",
    )(own, other)

    z_table = jnp.asarray(z_complex_table().astype(BF))
    spectra = pl.pallas_call(
        spectra_kernel,
        out_shape=jax.ShapeDtypeStruct((CAP, PAIRS * KXP, 4 * BOX), BF),
        grid=(CAP,),
        in_specs=[SMEM, SMEM, whole(2 * KXP, BOX), HBM, whole(4 * BOX, 4 * BOX)],
        out_specs=pl.BlockSpec((None, PAIRS * KXP, 4 * BOX), lambda i: (i, 0, 0)),
        scratch_shapes=held,
        compiler_params=params(54),
        cost_estimate=cost(20 * 10**9, 1024),
        name="spectra",
    )(slot_row, count, jnp.asarray(x_half.astype(BF)), flat, z_table)

    refs_own, spectra, pair_sum = lax.optimization_barrier((refs_own, spectra, pair_sum))
    arrived = lax.all_to_all(pair_sum, "dom", 0, 0, tiled=True, axis_index_groups=SAME_CORE)
    refs_other = lax.ppermute(refs_own, "dom", to_other)
    ex, wz = shift_tables()

    slots = pl.pallas_call(
        score_kernel,
        out_shape=jax.ShapeDtypeStruct((CAP, SHIFTS * SHIFTS, 128), F32),
        in_specs=[SMEM, SMEM, HBM] + [VMEM] * 6,
        out_specs=VMEM,
        scratch_shapes=[
            pltpu.VMEM((CAP * 2 * KXP, 2 * SEND), BF),
            pltpu.VMEM((CAP, 2 * KXP, voxels), BF),
            pltpu.VMEM((CAP, PAIRS * KXP, 4 * BOX), BF),
            pltpu.VMEM((PAIRS, KXV, 4 * BOX), F32),
            pltpu.VMEM((PAIRS, KXV, 4 * BOX), F32),
            pltpu.VMEM((SHIFTS, KXV, 4 * BOX), F32),
            pltpu.SemaphoreType.DMA((CAP,)),
        ],
        compiler_params=params(52),
        cost_estimate=cost(1024, 1024),
        name="slot_scores",
    )(
        count,
        slot_rot,
        spectra,
        jnp.asarray(by_core, F32),
        refs_own,
        refs_other,
        z_table,
        jnp.asarray(ex.astype(BF)),
        jnp.asarray(wz.astype(BF)),
    )
    slot_scores = slots[:, :, :SHIFTS].reshape(CAP, SHIFTS, SHIFTS, SHIFTS)
    slot_scores = slot_scores.transpose(0, 2, 1, 3).reshape(CAP, SHIFTS**3)
    everywhere = slot_scores
    for bit in (1, 2, 4):
        held_there = lax.ppermute(everywhere, "rot", [(i, i ^ bit) for i in range(8)])
        everywhere = jnp.concatenate([everywhere, held_there], axis=0)
    rows_all = jnp.arange(block_size, dtype=jnp.int32)
    alive = rows_all < live_count[0]
    before = (classes[:, None] == classes[None, :]) & (rows_all[None, :] < rows_all[:, None])
    place = (classes ^ lax.axis_index("rot")) * CAP + jnp.sum(before.astype(jnp.int32), axis=1)
    found = (place[:, None] == jnp.arange(8 * CAP, dtype=jnp.int32)[None, :]) & alive[:, None]
    scores = jnp.sum(jnp.where(found[:, :, None], everywhere[None, :, :], 0.0), axis=1)

    yz_table = np.zeros((4 * BOX, 4 * BOX))
    yz_table[: 2 * BOX] = z_real_table()
    yz_table[2 * BOX :, :BOX] = y_table()
    grids = pl.pallas_call(
        yz_kernel,
        out_shape=jax.ShapeDtypeStruct((BOX * PER_CHIP, 2 * BOX), BF),
        in_specs=[VMEM, VMEM],
        out_specs=VMEM,
        scratch_shapes=[pltpu.VMEM((BOX * PER_CHIP, 128), F32)] * 2,
        compiler_params=params(50),
        cost_estimate=cost(1024, 1024),
        name="yz_planes",
    )(arrived, jnp.asarray(yz_table.astype(BF)))
    by_rows = lax.all_to_all(grids, "dom", 0, 0, tiled=True)
    sums = pl.pallas_call(
        x_rows_kernel,
        out_shape=jax.ShapeDtypeStruct((BOX // DOM, ROT_CLS, BOX, 2 * BOX), F32),
        in_specs=[VMEM, VMEM],
        out_specs=HBM,
        scratch_shapes=[
            pltpu.VMEM((BOX // DOM, ROT_CLS, BOX, 2 * BOX), F32),
            pltpu.SemaphoreType.DMA((BOX // DOM,)),
        ],
        compiler_params=params(50),
        name="x_rows",
    )(by_rows.reshape(DOM, PLANES * PER_CHIP, 2 * BOX), jnp.asarray(x_rows_table().astype(BF)))
    return (scores, sums)


def solution(mesh):
    return jax.shard_map(
        shards,
        mesh=mesh,
        in_specs=(
            P("dom", None, None),
            P("rot", "dom", None),
            P("dom", None),
            P("dom"),
            P("dom"),
            P(),
            P("dom"),
        ),
        out_specs=(P("dom", None), P("dom", "rot", None, None)),
        check_vma=False,
    )
```

```python
import math

import jax
import jax.numpy as jnp
import numpy as np
from jax import lax
from jax.experimental import pallas as pl
from jax.experimental.pallas import tpu as pltpu
from jax.sharding import PartitionSpec as P

BOX = 64
SHIFTS = 8
ROT_CLS = 4
CAP = 4
HALF = 33
KXP = 48
KXV = 40
PAIRS = BOX // 2
DOM = 16
CHIPS = DOM // 2
SAME_CORE = [[2 * chip + core for chip in range(CHIPS)] for core in range(2)]
BF = jnp.bfloat16
F32 = jnp.float32


def grid_cos_sin(rows, cols):
    theta = ((rows[:, None] * cols[None, :]) % BOX).astype(np.float64) * (2.0 * math.pi / BOX)
    return np.cos(theta), np.sin(theta)


def x_half_table():
    c, s = grid_cos_sin(np.arange(BOX), np.arange(BOX))
    out = np.zeros((2, KXP, BOX))
    out[0, :HALF] = c[:HALF]
    out[1, :HALF] = -s[:HALF]
    return out.reshape(2 * KXP, BOX)


def z_complex_table():
    c, s = grid_cos_sin(np.arange(BOX), np.arange(BOX))
    two = np.eye(2)
    return np.block([[np.kron(two, c), np.kron(two, -s)], [np.kron(two, s), np.kron(two, c)]])


def shift_tables():
    c, s = grid_cos_sin(np.arange(SHIFTS) - SHIFTS // 2, np.arange(BOX))
    fold = np.zeros((KXV,))
    fold[:HALF] = 2.0
    fold[0] = fold[HALF - 1] = 1.0
    ex = np.zeros((2 * SHIFTS, KXV))
    ex[:SHIFTS, :HALF] = c[:, :HALF]
    ex[SHIFTS:, :HALF] = s[:, :HALF]
    ex = ex * fold[None, :]
    wz = np.zeros((2, 4 * BOX, 128))
    wz[0, :, :SHIFTS] = np.concatenate([c.T, c.T, -s.T, -s.T], axis=0)
    wz[1, :, :SHIFTS] = np.concatenate([-s.T, -s.T, -c.T, -c.T], axis=0)
    return ex, wz.reshape(8 * BOX, 128)


def z_real_table():
    c, s = grid_cos_sin(np.arange(BOX), np.arange(BOX))
    return np.kron(np.eye(2), np.concatenate([c, -s], axis=1))


def y_table():
    c, s = grid_cos_sin(np.arange(BOX), np.arange(BOX))
    return np.concatenate([c, s], axis=0)


def x_rows_table():
    c, s = grid_cos_sin(np.arange(BOX), np.arange(BOX))
    return np.stack(
        [
            np.einsum(
                "rq,kdx->rkdqx", np.eye(ROT_CLS), table.reshape(BOX, DOM, BOX // DOM)
            ).reshape(ROT_CLS * BOX, ROT_CLS * BOX)
            for table in (c, s)
        ]
    )


def z_stage(src, table, start, count):
    parts = []
    for j in range(start, start + count):
        lanes = slice(128 * j, 128 * (j + 1))
        parts.append(jnp.concatenate([src[0:KXP, lanes], src[KXP : 2 * KXP, lanes]], axis=1))
    return jnp.dot(jnp.concatenate(parts, axis=0), table, preferred_element_type=F32)


STEP = 8
CHUNK = 4
PLANES = BOX // DOM
PER_CHIP = ROT_CLS * PLANES
SEND = CHIPS * PER_CHIP


def fan_kernel(refs_ref, out_hbm, wide_s, block_s, sems):
    copies = []
    for half in range(2):
        lanes = slice(half * BOX * PAIRS, (half + 1) * BOX * PAIRS)
        for rot in range(ROT_CLS):
            wide_s[rot * PLANES : (rot + 1) * PLANES, lanes] = refs_ref[rot, :, lanes].astype(F32)
        block_s[:, lanes] = wide_s[:, lanes].astype(BF)
        for chip in range(CHIPS):
            copies.append(
                pltpu.make_async_copy(
                    block_s.at[:, lanes],
                    out_hbm.at[chip * PER_CHIP : (chip + 1) * PER_CHIP, lanes],
                    sems.at[half, chip],
                )
            )
            copies[-1].start()
    for copy in copies:
        copy.wait()


LANES = 1024


def slot_copies(flat_hbm, flat_s, sems, rows_of):
    return [
        pltpu.make_async_copy(
            flat_hbm.at[pl.ds(pl.multiple_of(rows_of(slot) * BOX, BOX), BOX)],
            flat_s.at[slot * BOX : (slot + 1) * BOX],
            sems.at[slot],
        )
        for slot in range(CAP)
    ]


def send_kernel(
    class_ref,
    rot_ref,
    bucket_ref,
    live_ref,
    level_ref,
    flat_hbm,
    send_out,
    own_out,
    count_out,
    slot_rot_out,
    slot_row_out,
    flat_s,
    spread_s,
    sems,
):
    owner = lax.axis_index("rot")
    core = lax.axis_index("dom") & 1
    count = jnp.int32(0)
    slot_row = [jnp.int32(0) for _ in range(CAP)]
    slot_rot = [jnp.int32(-1) for _ in range(CAP)]
    slot_bucket = [jnp.int32(-1) for _ in range(CAP)]
    for p in range(class_ref.shape[0]):
        mine = (class_ref[p] == owner) & (p < live_ref[0])
        for slot in range(CAP):
            here = mine & (count == slot)
            slot_row[slot] = jnp.where(here, p, slot_row[slot])
            slot_rot[slot] = jnp.where(here, rot_ref[p], slot_rot[slot])
            slot_bucket[slot] = jnp.where(here, bucket_ref[p], slot_bucket[slot])
        count = count + mine.astype(jnp.int32)
    copies = slot_copies(flat_hbm, flat_s, sems, lambda slot: slot_row[slot])
    for copy in copies:
        copy.start()
    count_out[0] = count
    for slot in range(CAP):
        slot_rot_out[slot] = slot_rot[slot]
        slot_row_out[slot] = slot_row[slot]
    columns = CAP * BOX
    lane = lax.broadcasted_iota(jnp.int32, (1, columns), 1)
    col_slot, col_x = lane >> 6, lane & (BOX - 1)
    col_rot = jnp.full((1, columns), -1, jnp.int32)
    col_bucket = jnp.full((1, columns), -1, jnp.int32)
    for slot in range(CAP):
        col_rot = jnp.where(col_slot == slot, slot_rot[slot], col_rot)
        col_bucket = jnp.where(col_slot == slot, slot_bucket[slot], col_bucket)
    levels = level_ref[...].astype(F32)
    col_weight = jnp.zeros((1, columns), F32)
    for level in range(levels.shape[1]):
        value = jnp.broadcast_to(levels[:, level : level + 1], (1, columns))
        col_weight = jnp.where(col_bucket == level, value, col_weight)
    row = lax.broadcasted_iota(jnp.int32, (SEND, columns), 0)
    base = (row // PER_CHIP) * (2 * PLANES) + (row & (PLANES - 1))
    right = ((row // PLANES) & (ROT_CLS - 1)) == col_rot
    for half, to_core in enumerate((core, 1 - core)):
        hit = right & (base + to_core * PLANES == col_x)
        spread_s[half * SEND : (half + 1) * SEND] = jnp.where(hit, col_weight, 0.0).astype(BF)
    for copy in copies:
        copy.wait()
    for start in range(0, BOX * BOX, LANES):
        lanes = slice(start, start + LANES)
        part = jnp.dot(spread_s[...], flat_s[:, lanes], preferred_element_type=F32)
        own_out[:, lanes] = part[:SEND].astype(BF)
        send_out[:, lanes] = part[SEND:].astype(BF)


def pair_kernel(own_ref, other_ref, out_ref):
    out_ref[...] = (own_ref[...].astype(F32) + other_ref[...].astype(F32)).astype(BF)


def spectra_kernel(slot_row_ref, count_ref, x_ref, flat_hbm, table_ref, spectra_out, flat_s, sems):
    now = pl.program_id(0)
    copies = slot_copies(flat_hbm, flat_s, sems, lambda slot: slot_row_ref[slot])
    for slot, copy in enumerate(copies):

        @pl.when((now == 0) & (slot < count_ref[0]))
        def _():
            copy.start()

    for slot, copy in enumerate(copies):

        @pl.when((now == slot) & (slot < count_ref[0]))
        def _():
            copy.wait()

    @pl.when(now < count_ref[0])
    def _():
        table = table_ref[...]
        rows = pl.ds(pl.multiple_of(now * BOX, BOX), BOX)
        for start in range(0, PAIRS, CHUNK):
            lanes = slice(128 * start, 128 * (start + CHUNK))
            along_x = jnp.dot(x_ref[...], flat_s[rows, lanes], preferred_element_type=F32)
            part = z_stage(along_x.astype(BF), table, 0, CHUNK)
            spectra_out[start * KXP : (start + CHUNK) * KXP, :] = part.astype(BF)

    @pl.when(now >= count_ref[0])
    def _():
        spectra_out[...] = jnp.zeros_like(spectra_out)


def pick_kernel(slot_rot_ref, x_ref, out_ref):
    core = lax.axis_index("dom") & 1
    ref_lane = lax.broadcasted_iota(jnp.int32, (1, SEND), 1)
    ref_rot = (ref_lane // PLANES) & (ROT_CLS - 1)
    for to in range(CAP):
        rows = slice(to * 2 * KXP, (to + 1) * 2 * KXP)
        wanted = ref_rot == slot_rot_ref[to]
        out_ref[rows, :SEND] = jnp.where(wanted, x_ref[core], 0.0).astype(BF)
        out_ref[rows, SEND:] = jnp.where(wanted, x_ref[1 - core], 0.0).astype(BF)


def score_kernel(
    count_ref,
    zp_hbm,
    pick_ref,
    own_ref,
    other_ref,
    table_ref,
    ex_ref,
    wz_ref,
    out_ref,
    x_s,
    zp_s,
    p_s,
    r_s,
    a_s,
    sems,
):
    for slot in range(CAP):

        @pl.when(slot < count_ref[0])
        def _():
            pltpu.make_async_copy(zp_hbm.at[slot], zp_s.at[slot], sems.at[slot]).start()

    out_ref[...] = jnp.zeros_like(out_ref)

    @pl.when(count_ref[0] > 0)
    def _():
        for start in range(0, BOX * BOX, 512):
            lanes = slice(start, start + 512)
            planes = jnp.concatenate([own_ref[:, lanes], other_ref[:, lanes]], axis=0)
            part = jnp.dot(pick_ref[...], planes, preferred_element_type=F32)
            x_s[:, :, lanes] = part.astype(BF).reshape(CAP, 2 * KXP, 512)

    def one_slot(slot, carry):
        pltpu.make_async_copy(zp_hbm.at[slot], zp_s.at[slot], sems.at[slot]).wait()
        table = table_ref[...]
        xr = x_s.at[slot]
        for start in range(0, PAIRS, STEP):
            part = z_stage(xr, table, start, STEP)
            part = part.astype(BF).astype(F32).reshape(STEP, KXP, 4 * BOX)
            r_s[start : start + STEP] = part[:, :KXV, :]
            mine = zp_s[slot, start * KXP : (start + STEP) * KXP, :].astype(F32)
            p_s[start : start + STEP] = mine.reshape(STEP, KXP, 4 * BOX)[:, :KXV, :]
        first = lax.broadcasted_iota(jnp.int32, (8, 128), 1) < BOX

        def column(col, carry):
            rows = pl.ds(pl.multiple_of(col * 8, 8), 8)

            def pair(m):
                return r_s[m % PAIRS, rows, 0:128], r_s[m % PAIRS, rows, 128:256]

            def shifted(before, now):
                return tuple(
                    pltpu.roll(jnp.where(first, n, b), BOX, 1) for b, n in zip(before, now)
                )

            def three(re, im):
                return re, im, re - im

            tiles = {m: pair(m) for m in range(-2, 2)}
            even = {m: three(*tiles[m]) for m in range(-1, 2)}
            odd = {m: three(*shifted(tiles[m - 1], tiles[m])) for m in range(-1, 2)}
            last = tiles[1]
            sums = [[jnp.zeros((8, 128), F32) for _ in range(3)] for _ in range(SHIFTS)]
            for j in range(PAIRS):
                new = pair(j + 2)
                even[j + 2] = three(*new)
                odd[j + 2] = three(*shifted(last, new))
                last = new
                pr = p_s[j, rows, 0:128]
                pi = p_s[j, rows, 128:256]
                both = pr + pi
                for u in range(-2, 2):
                    for parity, held in ((0, even), (1, odd)):
                        t = 2 * u + parity + SHIFTS // 2
                        rr, ri, rd = held[j - u]
                        sums[t][0] = sums[t][0] + pr * rr
                        sums[t][1] = sums[t][1] + pi * ri
                        sums[t][2] = sums[t][2] + both * rd
                del even[j - 1], odd[j - 1]
            for t in range(SHIFTS):
                one, two, mix = sums[t]
                a_s[t, rows, 0:128] = one + two
                a_s[t, rows, 128:256] = mix - one + two
            return carry

        lax.fori_loop(0, KXV // 8, column, 0)
        ex = ex_ref[...]
        along_x = [
            jnp.dot(ex, a_s[t].astype(BF), preferred_element_type=F32) for t in range(SHIFTS)
        ]
        cos_rows = jnp.concatenate([u[:SHIFTS] for u in along_x], axis=0).astype(BF)
        sin_rows = jnp.concatenate([u[SHIFTS:] for u in along_x], axis=0).astype(BF)
        both_rows = jnp.concatenate([cos_rows, sin_rows], axis=1)
        final = jnp.dot(both_rows, wz_ref[...], preferred_element_type=F32)
        out_ref[slot] = final * (float(BOX) ** -3.5)
        return carry

    lax.fori_loop(0, count_ref[0], one_slot, 0)


def yz_kernel(parts_ref, table_ref, out_ref, z_s, g_s):
    total = parts_ref[0:PER_CHIP].astype(F32)
    for chip in range(1, CHIPS):
        total = total + parts_ref[chip * PER_CHIP : (chip + 1) * PER_CHIP].astype(F32)
    total = total.astype(BF)
    z_ref, y_ref = table_ref[: 2 * BOX], table_ref[2 * BOX :, :BOX]
    stacked = jnp.concatenate([total[:, 128 * j : 128 * (j + 1)] for j in range(PAIRS)], axis=0)
    z_part = jnp.dot(stacked, z_ref, preferred_element_type=F32)
    for j in range(PAIRS):
        for half in range(2):
            start = (2 * j + half) * PER_CHIP
            z_s[start : start + PER_CHIP] = z_part[
                j * PER_CHIP : (j + 1) * PER_CHIP, 128 * half : 128 * (half + 1)
            ]
    by_y = [z_s[pl.ds(n, BOX, stride=PER_CHIP), :].astype(BF) for n in range(PER_CHIP)]
    y_part = jnp.dot(y_ref, jnp.concatenate(by_y, axis=1), preferred_element_type=F32)
    first = lax.broadcasted_iota(jnp.int32, (BOX, 128), 1) < BOX
    for n in range(PER_CHIP):
        lanes = slice(128 * n, 128 * (n + 1))
        turned = pltpu.roll(y_part[BOX:, lanes], BOX, 1)
        g_s[pl.ds(n, BOX, stride=PER_CHIP), :] = y_part[:BOX, lanes] + jnp.where(first, turned, -turned)
    out_ref[...] = g_s[...].astype(BF)


def x_rows_kernel(rows_ref, table_ref, out_hbm, out_s, sems):
    copies = []
    rows = ROT_CLS * (BOX // DOM)
    first = lax.broadcasted_iota(jnp.int32, (ROT_CLS * BOX, 128), 1) < BOX
    for ky in range(BOX // DOM):
        grid = rows_ref[:, ky * rows : (ky + 1) * rows, :].reshape(ROT_CLS * BOX, 128)
        cos_part = jnp.dot(table_ref[0], grid, preferred_element_type=F32)
        sin_part = jnp.dot(table_ref[1], grid, preferred_element_type=F32)
        turned = pltpu.roll(sin_part, BOX, 1)
        total = (cos_part + jnp.where(first, turned, -turned)) * (float(BOX) ** -1.5)
        out_s[ky] = total.reshape(ROT_CLS, BOX, 128)
        copies.append(pltpu.make_async_copy(out_s.at[ky], out_hbm.at[ky], sems.at[ky]))
        copies[-1].start()
    for copy in copies:
        copy.wait()


VMEM = pl.BlockSpec(memory_space=pltpu.VMEM)
HBM = pl.BlockSpec(memory_space=pltpu.HBM)
SMEM = pl.BlockSpec(memory_space=pltpu.SMEM)


def params(mib):
    return pltpu.CompilerParams(vmem_limit_bytes=mib * 1024 * 1024)


def cost(flops, moved):
    return pl.CostEstimate(flops=flops, bytes_accessed=moved, transcendentals=0)


def shards(particles, references, part_class, part_rot, bucket, bucket_weights, live_count):
    block_size = particles.shape[0]
    voxels = BOX * BOX
    columns = block_size * BOX
    to_other = [(i, i ^ 1) for i in range(DOM)]

    mine_refs = pl.pallas_call(
        fan_kernel,
        out_shape=jax.ShapeDtypeStruct((SEND, voxels), BF),
        in_specs=[VMEM],
        out_specs=HBM,
        scratch_shapes=[
            pltpu.VMEM((PER_CHIP, voxels), F32),
            pltpu.VMEM((PER_CHIP, voxels), BF),
            pltpu.SemaphoreType.DMA((2, CHIPS)),
        ],
        compiler_params=params(54),
        cost_estimate=cost(1024, 1024),
        name="fan",
    )(references)

    flat = particles.reshape(columns, voxels)
    classes = part_class.reshape(block_size)
    x_half = x_half_table()
    by_core = x_half.reshape(2 * KXP, CHIPS, 2, 1, PLANES)
    by_core = np.broadcast_to(by_core, (2 * KXP, CHIPS, 2, ROT_CLS, PLANES))
    by_core = by_core.transpose(2, 0, 1, 3, 4).reshape(2, 2 * KXP, SEND)
    held = [
        pltpu.VMEM((CAP * BOX, voxels), BF),
        pltpu.SemaphoreType.DMA((CAP,)),
    ]

    def whole(*shape):
        return pl.BlockSpec(shape, lambda s: (0,) * len(shape))

    to_send, own, count, slot_rot, slot_row = pl.pallas_call(
        send_kernel,
        out_shape=(
            jax.ShapeDtypeStruct((SEND, voxels), BF),
            jax.ShapeDtypeStruct((SEND, voxels), BF),
            jax.ShapeDtypeStruct((1,), jnp.int32),
            jax.ShapeDtypeStruct((CAP,), jnp.int32),
            jax.ShapeDtypeStruct((CAP,), jnp.int32),
        ),
        in_specs=[SMEM, SMEM, SMEM, SMEM, VMEM, HBM],
        out_specs=(VMEM, VMEM, SMEM, SMEM, SMEM),
        scratch_shapes=[held[0], pltpu.VMEM((2 * SEND, CAP * BOX), BF), held[1]],
        compiler_params=params(54),
        cost_estimate=cost(1024, 1024),
        name="send",
    )(
        classes,
        part_rot,
        bucket,
        live_count,
        bucket_weights.reshape(1, -1),
        flat,
    )
    other = lax.ppermute(to_send, "dom", to_other)
    refs_own = lax.all_to_all(
        mine_refs, "dom", 0, 0, tiled=True, axis_index_groups=SAME_CORE
    )
    pair_sum = pl.pallas_call(
        pair_kernel,
        out_shape=jax.ShapeDtypeStruct((SEND, voxels), BF),
        in_specs=[VMEM, VMEM],
        out_specs=VMEM,
        compiler_params=params(50),
        cost_estimate=cost(1024, 1024),
        name="pair",
    )(own, other)

    z_table = jnp.asarray(z_complex_table().astype(BF))
    spectra = pl.pallas_call(
        spectra_kernel,
        out_shape=jax.ShapeDtypeStruct((CAP, PAIRS * KXP, 4 * BOX), BF),
        grid=(CAP,),
        in_specs=[SMEM, SMEM, whole(2 * KXP, BOX), HBM, whole(4 * BOX, 4 * BOX)],
        out_specs=pl.BlockSpec((None, PAIRS * KXP, 4 * BOX), lambda i: (i, 0, 0)),
        scratch_shapes=held,
        compiler_params=params(54),
        cost_estimate=cost(20 * 10**9, 1024),
        name="spectra",
    )(slot_row, count, jnp.asarray(x_half.astype(BF)), flat, z_table)

    refs_own, spectra, pair_sum = lax.optimization_barrier((refs_own, spectra, pair_sum))
    arrived = lax.all_to_all(pair_sum, "dom", 0, 0, tiled=True, axis_index_groups=SAME_CORE)
    refs_other = lax.ppermute(refs_own, "dom", to_other)
    pick = pl.pallas_call(
        pick_kernel,
        out_shape=jax.ShapeDtypeStruct((CAP * 2 * KXP, 2 * SEND), BF),
        in_specs=[SMEM, VMEM],
        out_specs=VMEM,
        compiler_params=params(52),
        cost_estimate=cost(20 * 10**9, 1024),
        name="pick",
    )(slot_rot, jnp.asarray(by_core, F32))
    ex, wz = shift_tables()

    slots = pl.pallas_call(
        score_kernel,
        out_shape=jax.ShapeDtypeStruct((CAP, SHIFTS * SHIFTS, 128), F32),
        in_specs=[SMEM, HBM] + [VMEM] * 6,
        out_specs=VMEM,
        scratch_shapes=[
            pltpu.VMEM((CAP, 2 * KXP, voxels), BF),
            pltpu.VMEM((CAP, PAIRS * KXP, 4 * BOX), BF),
            pltpu.VMEM((PAIRS, KXV, 4 * BOX), F32),
            pltpu.VMEM((PAIRS, KXV, 4 * BOX), F32),
            pltpu.VMEM((SHIFTS, KXV, 4 * BOX), F32),
            pltpu.SemaphoreType.DMA((CAP,)),
        ],
        compiler_params=params(52),
        cost_estimate=cost(1024, 1024),
        name="slot_scores",
    )(
        count,
        spectra,
        pick,
        refs_own,
        refs_other,
        z_table,
        jnp.asarray(ex.astype(BF)),
        jnp.asarray(wz.astype(BF)),
    )
    slot_scores = slots[:, :, :SHIFTS].reshape(CAP, SHIFTS, SHIFTS, SHIFTS)
    slot_scores = slot_scores.transpose(0, 2, 1, 3).reshape(CAP, SHIFTS**3)
    everywhere = slot_scores
    for bit in (1, 2, 4):
        held_there = lax.ppermute(everywhere, "rot", [(i, i ^ bit) for i in range(8)])
        everywhere = jnp.concatenate([everywhere, held_there], axis=0)
    rows_all = jnp.arange(block_size, dtype=jnp.int32)
    alive = rows_all < live_count[0]
    before = (classes[:, None] == classes[None, :]) & (rows_all[None, :] < rows_all[:, None])
    place = (classes ^ lax.axis_index("rot")) * CAP + jnp.sum(before.astype(jnp.int32), axis=1)
    found = (place[:, None] == jnp.arange(8 * CAP, dtype=jnp.int32)[None, :]) & alive[:, None]
    scores = jnp.sum(jnp.where(found[:, :, None], everywhere[None, :, :], 0.0), axis=1)

    yz_table = np.zeros((4 * BOX, 4 * BOX))
    yz_table[: 2 * BOX] = z_real_table()
    yz_table[2 * BOX :, :BOX] = y_table()
    grids = pl.pallas_call(
        yz_kernel,
        out_shape=jax.ShapeDtypeStruct((BOX * PER_CHIP, 2 * BOX), BF),
        in_specs=[VMEM, VMEM],
        out_specs=VMEM,
        scratch_shapes=[pltpu.VMEM((BOX * PER_CHIP, 128), F32)] * 2,
        compiler_params=params(50),
        cost_estimate=cost(1024, 1024),
        name="yz_planes",
    )(arrived, jnp.asarray(yz_table.astype(BF)))
    by_rows = lax.all_to_all(grids, "dom", 0, 0, tiled=True)
    sums = pl.pallas_call(
        x_rows_kernel,
        out_shape=jax.ShapeDtypeStruct((BOX // DOM, ROT_CLS, BOX, 2 * BOX), F32),
        in_specs=[VMEM, VMEM],
        out_specs=HBM,
        scratch_shapes=[
            pltpu.VMEM((BOX // DOM, ROT_CLS, BOX, 2 * BOX), F32),
            pltpu.SemaphoreType.DMA((BOX // DOM,)),
        ],
        compiler_params=params(50),
        name="x_rows",
    )(by_rows.reshape(DOM, PLANES * PER_CHIP, 2 * BOX), jnp.asarray(x_rows_table().astype(BF)))
    return (scores, sums)


def solution(mesh):
    return jax.shard_map(
        shards,
        mesh=mesh,
        in_specs=(
            P("dom", None, None),
            P("rot", "dom", None),
            P("dom", None),
            P("dom"),
            P("dom"),
            P(),
            P("dom"),
        ),
        out_specs=(P("dom", None), P("dom", "rot", None, None)),
        check_vma=False,
    )
```

```python
import math

import jax
import jax.numpy as jnp
import numpy as np
from jax import lax
from jax.experimental import pallas as pl
from jax.experimental.pallas import tpu as pltpu
from jax.sharding import PartitionSpec as P

BOX = 64
SHIFTS = 8
ROT_CLS = 4
CAP = 4
HALF = 33
KXP = 48
KXV = 40
PAIRS = BOX // 2
DOM = 16
CHIPS = DOM // 2
SAME_CORE = [[2 * chip + core for chip in range(CHIPS)] for core in range(2)]
BF = jnp.bfloat16
F32 = jnp.float32


def grid_cos_sin(rows, cols):
    theta = ((rows[:, None] * cols[None, :]) % BOX).astype(np.float64) * (2.0 * math.pi / BOX)
    return np.cos(theta), np.sin(theta)


def x_half_table():
    c, s = grid_cos_sin(np.arange(BOX), np.arange(BOX))
    out = np.zeros((2, KXP, BOX))
    out[0, :HALF] = c[:HALF]
    out[1, :HALF] = -s[:HALF]
    return out.reshape(2 * KXP, BOX)


def z_complex_table():
    c, s = grid_cos_sin(np.arange(BOX), np.arange(BOX))
    two = np.eye(2)
    return np.block([[np.kron(two, c), np.kron(two, -s)], [np.kron(two, s), np.kron(two, c)]])


def shift_tables():
    c, s = grid_cos_sin(np.arange(SHIFTS) - SHIFTS // 2, np.arange(BOX))
    fold = np.zeros((KXV,))
    fold[:HALF] = 2.0
    fold[0] = fold[HALF - 1] = 1.0
    ex = np.zeros((2 * SHIFTS, KXV))
    ex[:SHIFTS, :HALF] = c[:, :HALF]
    ex[SHIFTS:, :HALF] = s[:, :HALF]
    ex = ex * fold[None, :]
    wz = np.zeros((2, 4 * BOX, 128))
    wz[0, :, :SHIFTS] = np.concatenate([c.T, c.T, -s.T, -s.T], axis=0)
    wz[1, :, :SHIFTS] = np.concatenate([-s.T, -s.T, -c.T, -c.T], axis=0)
    return ex, wz.reshape(8 * BOX, 128)


def z_real_table():
    c, s = grid_cos_sin(np.arange(BOX), np.arange(BOX))
    return np.kron(np.eye(2), np.concatenate([c, -s], axis=1))


def y_table():
    c, s = grid_cos_sin(np.arange(BOX), np.arange(BOX))
    return np.concatenate([c, s], axis=0)


def x_rows_table():
    c, s = grid_cos_sin(np.arange(BOX), np.arange(BOX))
    return np.stack(
        [
            np.einsum(
                "rq,kdx->rkdqx", np.eye(ROT_CLS), table.reshape(BOX, DOM, BOX // DOM)
            ).reshape(ROT_CLS * BOX, ROT_CLS * BOX)
            for table in (c, s)
        ]
    )


def z_stage(src, table, start, count):
    parts = []
    for j in range(start, start + count):
        lanes = slice(128 * j, 128 * (j + 1))
        parts.append(jnp.concatenate([src[0:KXP, lanes], src[KXP : 2 * KXP, lanes]], axis=1))
    return jnp.dot(jnp.concatenate(parts, axis=0), table, preferred_element_type=F32)


STEP = 8
CHUNK = 4
PLANES = BOX // DOM
PER_CHIP = ROT_CLS * PLANES
SEND = CHIPS * PER_CHIP


def fan_kernel(refs_ref, out_hbm, wide_s, block_s, sems):
    copies = []
    for half in range(2):
        lanes = slice(half * BOX * PAIRS, (half + 1) * BOX * PAIRS)
        for rot in range(ROT_CLS):
            wide_s[rot * PLANES : (rot + 1) * PLANES, lanes] = refs_ref[rot, :, lanes].astype(F32)
        block_s[:, lanes] = wide_s[:, lanes].astype(BF)
        for chip in range(CHIPS):
            copies.append(
                pltpu.make_async_copy(
                    block_s.at[:, lanes],
                    out_hbm.at[chip * PER_CHIP : (chip + 1) * PER_CHIP, lanes],
                    sems.at[half, chip],
                )
            )
            copies[-1].start()
    for copy in copies:
        copy.wait()


LANES = 1024


def slot_copies(flat_hbm, flat_s, sems, rows_of):
    return [
        pltpu.make_async_copy(
            flat_hbm.at[pl.ds(pl.multiple_of(rows_of(slot) * BOX, BOX), BOX)],
            flat_s.at[slot * BOX : (slot + 1) * BOX],
            sems.at[slot],
        )
        for slot in range(CAP)
    ]


def send_kernel(
    class_ref,
    rot_ref,
    bucket_ref,
    live_ref,
    level_ref,
    flat_hbm,
    send_out,
    own_out,
    count_out,
    slot_rot_out,
    slot_row_out,
    flat_s,
    spread_s,
    sems,
):
    owner = lax.axis_index("rot")
    core = lax.axis_index("dom") & 1
    count = jnp.int32(0)
    slot_row = [jnp.int32(0) for _ in range(CAP)]
    slot_rot = [jnp.int32(-1) for _ in range(CAP)]
    slot_bucket = [jnp.int32(-1) for _ in range(CAP)]
    for p in range(class_ref.shape[0]):
        mine = (class_ref[p] == owner) & (p < live_ref[0])
        for slot in range(CAP):
            here = mine & (count == slot)
            slot_row[slot] = jnp.where(here, p, slot_row[slot])
            slot_rot[slot] = jnp.where(here, rot_ref[p], slot_rot[slot])
            slot_bucket[slot] = jnp.where(here, bucket_ref[p], slot_bucket[slot])
        count = count + mine.astype(jnp.int32)
    copies = slot_copies(flat_hbm, flat_s, sems, lambda slot: slot_row[slot])
    for copy in copies:
        copy.start()
    count_out[0] = count
    for slot in range(CAP):
        slot_rot_out[slot] = slot_rot[slot]
        slot_row_out[slot] = slot_row[slot]
    columns = CAP * BOX
    lane = lax.broadcasted_iota(jnp.int32, (1, columns), 1)
    col_slot, col_x = lane >> 6, lane & (BOX - 1)
    col_rot = jnp.full((1, columns), -1, jnp.int32)
    col_bucket = jnp.full((1, columns), -1, jnp.int32)
    for slot in range(CAP):
        col_rot = jnp.where(col_slot == slot, slot_rot[slot], col_rot)
        col_bucket = jnp.where(col_slot == slot, slot_bucket[slot], col_bucket)
    levels = level_ref[...].astype(F32)
    col_weight = jnp.zeros((1, columns), F32)
    for level in range(levels.shape[1]):
        value = jnp.broadcast_to(levels[:, level : level + 1], (1, columns))
        col_weight = jnp.where(col_bucket == level, value, col_weight)
    row = lax.broadcasted_iota(jnp.int32, (SEND, columns), 0)
    base = (row // PER_CHIP) * (2 * PLANES) + (row & (PLANES - 1))
    right = ((row // PLANES) & (ROT_CLS - 1)) == col_rot
    for half, to_core in enumerate((core, 1 - core)):
        hit = right & (base + to_core * PLANES == col_x)
        spread_s[half * SEND : (half + 1) * SEND] = jnp.where(hit, col_weight, 0.0).astype(BF)
    for copy in copies:
        copy.wait()
    for start in range(0, BOX * BOX, LANES):
        lanes = slice(start, start + LANES)
        part = jnp.dot(spread_s[...], flat_s[:, lanes], preferred_element_type=F32)
        own_out[:, lanes] = part[:SEND].astype(BF)
        send_out[:, lanes] = part[SEND:].astype(BF)


def pair_kernel(own_ref, other_ref, out_ref):
    out_ref[...] = (own_ref[...].astype(F32) + other_ref[...].astype(F32)).astype(BF)


def spectra_kernel(slot_row_ref, count_ref, x_ref, flat_hbm, table_ref, spectra_out, flat_s, sems):
    now = pl.program_id(0)
    copies = slot_copies(flat_hbm, flat_s, sems, lambda slot: slot_row_ref[slot])
    for slot, copy in enumerate(copies):

        @pl.when((now == 0) & (slot < count_ref[0]))
        def _():
            copy.start()

    for slot, copy in enumerate(copies):

        @pl.when((now == slot) & (slot < count_ref[0]))
        def _():
            copy.wait()

    @pl.when(now < count_ref[0])
    def _():
        table = table_ref[...]
        rows = pl.ds(pl.multiple_of(now * BOX, BOX), BOX)
        for start in range(0, PAIRS, CHUNK):
            lanes = slice(128 * start, 128 * (start + CHUNK))
            along_x = jnp.dot(x_ref[...], flat_s[rows, lanes], preferred_element_type=F32)
            part = z_stage(along_x.astype(BF), table, 0, CHUNK)
            spectra_out[start * KXP : (start + CHUNK) * KXP, :] = part.astype(BF)

    @pl.when(now >= count_ref[0])
    def _():
        spectra_out[...] = jnp.zeros_like(spectra_out)


def pick_kernel(slot_rot_ref, x_ref, out_ref):
    core = lax.axis_index("dom") & 1
    ref_lane = lax.broadcasted_iota(jnp.int32, (1, SEND), 1)
    ref_rot = (ref_lane // PLANES) & (ROT_CLS - 1)
    for to in range(CAP):
        rows = slice(to * 2 * KXP, (to + 1) * 2 * KXP)
        wanted = ref_rot == slot_rot_ref[to]
        out_ref[rows, :SEND] = jnp.where(wanted, x_ref[core], 0.0).astype(BF)
        out_ref[rows, SEND:] = jnp.where(wanted, x_ref[1 - core], 0.0).astype(BF)


def score_kernel(
    count_ref,
    zp_hbm,
    pick_ref,
    own_ref,
    other_ref,
    table_ref,
    ex_ref,
    wz_ref,
    out_ref,
    x_s,
    zp_s,
    p_s,
    r_s,
    a_s,
    sems,
):
    for slot in range(CAP):

        @pl.when(slot < count_ref[0])
        def _():
            pltpu.make_async_copy(zp_hbm.at[slot], zp_s.at[slot], sems.at[slot]).start()

    out_ref[...] = jnp.zeros_like(out_ref)

    @pl.when(count_ref[0] > 0)
    def _():
        for start in range(0, BOX * BOX, 512):
            lanes = slice(start, start + 512)
            planes = jnp.concatenate([own_ref[:, lanes], other_ref[:, lanes]], axis=0)
            part = jnp.dot(pick_ref[...], planes, preferred_element_type=F32)
            x_s[:, :, lanes] = part.astype(BF).reshape(CAP, 2 * KXP, 512)

    def one_slot(slot, carry):
        pltpu.make_async_copy(zp_hbm.at[slot], zp_s.at[slot], sems.at[slot]).wait()
        table = table_ref[...]
        xr = x_s.at[slot]
        for start in range(0, PAIRS, STEP):
            part = z_stage(xr, table, start, STEP)
            part = part.astype(BF).astype(F32).reshape(STEP, KXP, 4 * BOX)
            r_s[start : start + STEP] = part[:, :KXV, :]
            mine = zp_s[slot, start * KXP : (start + STEP) * KXP, :].astype(F32)
            p_s[start : start + STEP] = mine.reshape(STEP, KXP, 4 * BOX)[:, :KXV, :]
        first = lax.broadcasted_iota(jnp.int32, (8, 128), 1) < BOX

        def column(col, carry):
            rows = pl.ds(pl.multiple_of(col * 8, 8), 8)

            def pair(m):
                return r_s[m % PAIRS, rows, 0:128], r_s[m % PAIRS, rows, 128:256]

            def shifted(before, now):
                return tuple(
                    pltpu.roll(jnp.where(first, n, b), BOX, 1) for b, n in zip(before, now)
                )

            def three(re, im):
                return re, im, re - im

            tiles = {m: pair(m) for m in range(-2, 2)}
            even = {m: three(*tiles[m]) for m in range(-1, 2)}
            odd = {m: three(*shifted(tiles[m - 1], tiles[m])) for m in range(-1, 2)}
            last = tiles[1]
            sums = [[jnp.zeros((8, 128), F32) for _ in range(3)] for _ in range(SHIFTS)]
            for j in range(PAIRS):
                new = pair(j + 2)
                even[j + 2] = three(*new)
                odd[j + 2] = three(*shifted(last, new))
                last = new
                pr = p_s[j, rows, 0:128]
                pi = p_s[j, rows, 128:256]
                both = pr + pi
                for u in range(-2, 2):
                    for parity, held in ((0, even), (1, odd)):
                        t = 2 * u + parity + SHIFTS // 2
                        rr, ri, rd = held[j - u]
                        sums[t][0] = sums[t][0] + pr * rr
                        sums[t][1] = sums[t][1] + pi * ri
                        sums[t][2] = sums[t][2] + both * rd
                del even[j - 1], odd[j - 1]
            for t in range(SHIFTS):
                one, two, mix = sums[t]
                a_s[t, rows, 0:128] = one + two
                a_s[t, rows, 128:256] = mix - one + two
            return carry

        lax.fori_loop(0, KXV // 8, column, 0)
        ex = ex_ref[...]
        along_x = [
            jnp.dot(ex, a_s[t].astype(BF), preferred_element_type=F32) for t in range(SHIFTS)
        ]
        cos_rows = jnp.concatenate([u[:SHIFTS] for u in along_x], axis=0).astype(BF)
        sin_rows = jnp.concatenate([u[SHIFTS:] for u in along_x], axis=0).astype(BF)
        both_rows = jnp.concatenate([cos_rows, sin_rows], axis=1)
        final = jnp.dot(both_rows, wz_ref[...], preferred_element_type=F32)
        out_ref[slot] = final * (float(BOX) ** -3.5)
        return carry

    lax.fori_loop(0, count_ref[0], one_slot, 0)


def yz_kernel(parts_ref, table_ref, out_ref, z_s, g_s):
    total = parts_ref[0:PER_CHIP].astype(F32)
    for chip in range(1, CHIPS):
        total = total + parts_ref[chip * PER_CHIP : (chip + 1) * PER_CHIP].astype(F32)
    total = total.astype(BF)
    z_ref, y_ref = table_ref[: 2 * BOX], table_ref[2 * BOX :, :BOX]
    stacked = jnp.concatenate([total[:, 128 * j : 128 * (j + 1)] for j in range(PAIRS)], axis=0)
    z_part = jnp.dot(stacked, z_ref, preferred_element_type=F32)
    for j in range(PAIRS):
        for half in range(2):
            start = (2 * j + half) * PER_CHIP
            z_s[start : start + PER_CHIP] = z_part[
                j * PER_CHIP : (j + 1) * PER_CHIP, 128 * half : 128 * (half + 1)
            ]
    by_y = [z_s[pl.ds(n, BOX, stride=PER_CHIP), :].astype(BF) for n in range(PER_CHIP)]
    y_part = jnp.dot(y_ref, jnp.concatenate(by_y, axis=1), preferred_element_type=F32)
    first = lax.broadcasted_iota(jnp.int32, (BOX, 128), 1) < BOX
    for n in range(PER_CHIP):
        lanes = slice(128 * n, 128 * (n + 1))
        turned = pltpu.roll(y_part[BOX:, lanes], BOX, 1)
        g_s[pl.ds(n, BOX, stride=PER_CHIP), :] = y_part[:BOX, lanes] + jnp.where(first, turned, -turned)
    out_ref[...] = g_s[...].astype(BF)


def x_rows_kernel(rows_ref, table_ref, out_hbm, out_s, sems):
    copies = []
    rows = ROT_CLS * (BOX // DOM)
    first = lax.broadcasted_iota(jnp.int32, (ROT_CLS * BOX, 128), 1) < BOX
    for ky in range(BOX // DOM):
        grid = rows_ref[:, ky * rows : (ky + 1) * rows, :].reshape(ROT_CLS * BOX, 128)
        cos_part = jnp.dot(table_ref[0], grid, preferred_element_type=F32)
        sin_part = jnp.dot(table_ref[1], grid, preferred_element_type=F32)
        turned = pltpu.roll(sin_part, BOX, 1)
        total = (cos_part + jnp.where(first, turned, -turned)) * (float(BOX) ** -1.5)
        out_s[ky] = total.reshape(ROT_CLS, BOX, 128)
        copies.append(pltpu.make_async_copy(out_s.at[ky], out_hbm.at[ky], sems.at[ky]))
        copies[-1].start()
    for copy in copies:
        copy.wait()


VMEM = pl.BlockSpec(memory_space=pltpu.VMEM)
HBM = pl.BlockSpec(memory_space=pltpu.HBM)
SMEM = pl.BlockSpec(memory_space=pltpu.SMEM)


def params(mib):
    return pltpu.CompilerParams(vmem_limit_bytes=mib * 1024 * 1024)


def cost(flops, moved):
    return pl.CostEstimate(flops=flops, bytes_accessed=moved, transcendentals=0)


def shards(particles, references, part_class, part_rot, bucket, bucket_weights, live_count):
    block_size = particles.shape[0]
    voxels = BOX * BOX
    columns = block_size * BOX
    to_other = [(i, i ^ 1) for i in range(DOM)]

    mine_refs = pl.pallas_call(
        fan_kernel,
        out_shape=jax.ShapeDtypeStruct((SEND, voxels), BF),
        in_specs=[VMEM],
        out_specs=HBM,
        scratch_shapes=[
            pltpu.VMEM((PER_CHIP, voxels), F32),
            pltpu.VMEM((PER_CHIP, voxels), BF),
            pltpu.SemaphoreType.DMA((2, CHIPS)),
        ],
        compiler_params=params(54),
        cost_estimate=cost(1024, 1024),
        name="fan",
    )(references)

    flat = particles.reshape(columns, voxels)
    classes = part_class.reshape(block_size)
    x_half = x_half_table()
    by_core = x_half.reshape(2 * KXP, CHIPS, 2, 1, PLANES)
    by_core = np.broadcast_to(by_core, (2 * KXP, CHIPS, 2, ROT_CLS, PLANES))
    by_core = by_core.transpose(2, 0, 1, 3, 4).reshape(2, 2 * KXP, SEND)
    held = [
        pltpu.VMEM((CAP * BOX, voxels), BF),
        pltpu.SemaphoreType.DMA((CAP,)),
    ]

    def whole(*shape):
        return pl.BlockSpec(shape, lambda s: (0,) * len(shape))

    to_send, own, count, slot_rot, slot_row = pl.pallas_call(
        send_kernel,
        out_shape=(
            jax.ShapeDtypeStruct((SEND, voxels), BF),
            jax.ShapeDtypeStruct((SEND, voxels), BF),
            jax.ShapeDtypeStruct((1,), jnp.int32),
            jax.ShapeDtypeStruct((CAP,), jnp.int32),
            jax.ShapeDtypeStruct((CAP,), jnp.int32),
        ),
        in_specs=[SMEM, SMEM, SMEM, SMEM, VMEM, HBM],
        out_specs=(VMEM, VMEM, SMEM, SMEM, SMEM),
        scratch_shapes=[held[0], pltpu.VMEM((2 * SEND, CAP * BOX), BF), held[1]],
        compiler_params=params(54),
        cost_estimate=cost(1024, 1024),
        name="send",
    )(
        classes,
        part_rot,
        bucket,
        live_count,
        bucket_weights.reshape(1, -1),
        flat,
    )
    other = lax.ppermute(to_send, "dom", to_other)
    refs_own = lax.all_to_all(
        mine_refs, "dom", 0, 0, tiled=True, axis_index_groups=SAME_CORE
    )
    pair_sum = pl.pallas_call(
        pair_kernel,
        out_shape=jax.ShapeDtypeStruct((SEND, voxels), BF),
        in_specs=[VMEM, VMEM],
        out_specs=VMEM,
        compiler_params=params(50),
        cost_estimate=cost(1024, 1024),
        name="pair",
    )(own, other)

    z_table = jnp.asarray(z_complex_table().astype(BF))
    spectra = pl.pallas_call(
        spectra_kernel,
        out_shape=jax.ShapeDtypeStruct((CAP, PAIRS * KXP, 4 * BOX), BF),
        grid=(CAP,),
        in_specs=[SMEM, SMEM, whole(2 * KXP, BOX), HBM, whole(4 * BOX, 4 * BOX)],
        out_specs=pl.BlockSpec((None, PAIRS * KXP, 4 * BOX), lambda i: (i, 0, 0)),
        scratch_shapes=held,
        compiler_params=params(54),
        cost_estimate=cost(20 * 10**9, 1024),
        name="spectra",
    )(slot_row, count, jnp.asarray(x_half.astype(BF)), flat, z_table)

    refs_own, spectra, pair_sum = lax.optimization_barrier((refs_own, spectra, pair_sum))
    arrived = lax.all_to_all(pair_sum, "dom", 0, 0, tiled=True, axis_index_groups=SAME_CORE)
    refs_other = lax.ppermute(refs_own, "dom", to_other)
    pick = pl.pallas_call(
        pick_kernel,
        out_shape=jax.ShapeDtypeStruct((CAP * 2 * KXP, 2 * SEND), BF),
        in_specs=[SMEM, VMEM],
        out_specs=VMEM,
        compiler_params=params(52),
        cost_estimate=cost(20 * 10**9, 1024),
        name="pick",
    )(slot_rot, jnp.asarray(by_core, F32))
    ex, wz = shift_tables()

    slots = pl.pallas_call(
        score_kernel,
        out_shape=jax.ShapeDtypeStruct((CAP, SHIFTS * SHIFTS, 128), F32),
        in_specs=[SMEM, HBM] + [VMEM] * 6,
        out_specs=VMEM,
        scratch_shapes=[
            pltpu.VMEM((CAP, 2 * KXP, voxels), BF),
            pltpu.VMEM((CAP, PAIRS * KXP, 4 * BOX), BF),
            pltpu.VMEM((PAIRS, KXV, 4 * BOX), F32),
            pltpu.VMEM((PAIRS, KXV, 4 * BOX), F32),
            pltpu.VMEM((SHIFTS, KXV, 4 * BOX), F32),
            pltpu.SemaphoreType.DMA((CAP,)),
        ],
        compiler_params=params(52),
        cost_estimate=cost(1024, 1024),
        name="slot_scores",
    )(
        count,
        spectra,
        pick,
        refs_own,
        refs_other,
        z_table,
        jnp.asarray(ex.astype(BF)),
        jnp.asarray(wz.astype(BF)),
    )
    yz_table = np.zeros((4 * BOX, 4 * BOX))
    yz_table[: 2 * BOX] = z_real_table()
    yz_table[2 * BOX :, :BOX] = y_table()
    grids = pl.pallas_call(
        yz_kernel,
        out_shape=jax.ShapeDtypeStruct((BOX * PER_CHIP, 2 * BOX), BF),
        in_specs=[VMEM, VMEM],
        out_specs=VMEM,
        scratch_shapes=[pltpu.VMEM((BOX * PER_CHIP, 128), F32)] * 2,
        compiler_params=params(50),
        cost_estimate=cost(1024, 1024),
        name="yz_planes",
    )(arrived, jnp.asarray(yz_table.astype(BF)))
    slot_scores = slots[:, :, :SHIFTS].reshape(CAP, SHIFTS, SHIFTS, SHIFTS)
    slot_scores = slot_scores.transpose(0, 2, 1, 3).reshape(CAP, SHIFTS**3)
    everywhere = slot_scores
    for bit in (1, 2, 4):
        if bit == 2:
            everywhere, grids = lax.optimization_barrier((everywhere, grids))
        held_there = lax.ppermute(everywhere, "rot", [(i, i ^ bit) for i in range(8)])
        everywhere = jnp.concatenate([everywhere, held_there], axis=0)
    rows_all = jnp.arange(block_size, dtype=jnp.int32)
    alive = rows_all < live_count[0]
    before = (classes[:, None] == classes[None, :]) & (rows_all[None, :] < rows_all[:, None])
    place = (classes ^ lax.axis_index("rot")) * CAP + jnp.sum(before.astype(jnp.int32), axis=1)
    found = (place[:, None] == jnp.arange(8 * CAP, dtype=jnp.int32)[None, :]) & alive[:, None]
    scores = jnp.sum(jnp.where(found[:, :, None], everywhere[None, :, :], 0.0), axis=1)

    by_rows = lax.all_to_all(grids, "dom", 0, 0, tiled=True)
    sums = pl.pallas_call(
        x_rows_kernel,
        out_shape=jax.ShapeDtypeStruct((BOX // DOM, ROT_CLS, BOX, 2 * BOX), F32),
        in_specs=[VMEM, VMEM],
        out_specs=HBM,
        scratch_shapes=[
            pltpu.VMEM((BOX // DOM, ROT_CLS, BOX, 2 * BOX), F32),
            pltpu.SemaphoreType.DMA((BOX // DOM,)),
        ],
        compiler_params=params(50),
        name="x_rows",
    )(by_rows.reshape(DOM, PLANES * PER_CHIP, 2 * BOX), jnp.asarray(x_rows_table().astype(BF)))
    return (scores, sums)


def solution(mesh):
    return jax.shard_map(
        shards,
        mesh=mesh,
        in_specs=(
            P("dom", None, None),
            P("rot", "dom", None),
            P("dom", None),
            P("dom"),
            P("dom"),
            P(),
            P("dom"),
        ),
        out_specs=(P("dom", None), P("dom", "rot", None, None)),
        check_vma=False,
    )
```

```python
import math

import jax
import jax.numpy as jnp
import numpy as np
from jax import lax
from jax.experimental import pallas as pl
from jax.experimental.pallas import tpu as pltpu
from jax.sharding import PartitionSpec as P

BOX = 64
SHIFTS = 8
ROT_CLS = 4
CAP = 4
HALF = 33
KXP = 48
KXV = 40
PAIRS = BOX // 2
DOM = 16
CHIPS = DOM // 2
SAME_CORE = [[2 * chip + core for chip in range(CHIPS)] for core in range(2)]
BF = jnp.bfloat16
F32 = jnp.float32


def grid_cos_sin(rows, cols):
    theta = ((rows[:, None] * cols[None, :]) % BOX).astype(np.float64) * (2.0 * math.pi / BOX)
    return np.cos(theta), np.sin(theta)


def x_half_table():
    c, s = grid_cos_sin(np.arange(BOX), np.arange(BOX))
    out = np.zeros((2, KXP, BOX))
    out[0, :HALF] = c[:HALF]
    out[1, :HALF] = -s[:HALF]
    return out.reshape(2 * KXP, BOX)


def z_complex_table():
    c, s = grid_cos_sin(np.arange(BOX), np.arange(BOX))
    two = np.eye(2)
    return np.block([[np.kron(two, c), np.kron(two, -s)], [np.kron(two, s), np.kron(two, c)]])


def shift_tables():
    c, s = grid_cos_sin(np.arange(SHIFTS) - SHIFTS // 2, np.arange(BOX))
    fold = np.zeros((KXV,))
    fold[:HALF] = 2.0
    fold[0] = fold[HALF - 1] = 1.0
    ex = np.zeros((2 * SHIFTS, KXV))
    ex[:SHIFTS, :HALF] = c[:, :HALF]
    ex[SHIFTS:, :HALF] = s[:, :HALF]
    ex = ex * fold[None, :]
    wz = np.zeros((2, 4 * BOX, 128))
    wz[0, :, :SHIFTS] = np.concatenate([c.T, c.T, -s.T, -s.T], axis=0)
    wz[1, :, :SHIFTS] = np.concatenate([-s.T, -s.T, -c.T, -c.T], axis=0)
    return ex, wz.reshape(8 * BOX, 128)


def z_real_table():
    c, s = grid_cos_sin(np.arange(BOX), np.arange(BOX))
    return np.kron(np.eye(2), np.concatenate([c, -s], axis=1))


def y_table():
    c, s = grid_cos_sin(np.arange(BOX), np.arange(BOX))
    return np.concatenate([c, s], axis=0)


def x_rows_table():
    c, s = grid_cos_sin(np.arange(BOX), np.arange(BOX))
    return np.stack(
        [
            np.einsum(
                "rq,kdx->rkdqx", np.eye(ROT_CLS), table.reshape(BOX, DOM, BOX // DOM)
            ).reshape(ROT_CLS * BOX, ROT_CLS * BOX)
            for table in (c, s)
        ]
    )


def z_stage(src, table, start, count):
    parts = []
    for j in range(start, start + count):
        lanes = slice(128 * j, 128 * (j + 1))
        parts.append(jnp.concatenate([src[0:KXP, lanes], src[KXP : 2 * KXP, lanes]], axis=1))
    return jnp.dot(jnp.concatenate(parts, axis=0), table, preferred_element_type=F32)


STEP = 8
CHUNK = 4
PLANES = BOX // DOM
PER_CHIP = ROT_CLS * PLANES
SEND = CHIPS * PER_CHIP


def fan_kernel(refs_ref, out_hbm, wide_s, block_s, sems):
    copies = []
    for half in range(2):
        lanes = slice(half * BOX * PAIRS, (half + 1) * BOX * PAIRS)
        for rot in range(ROT_CLS):
            wide_s[rot * PLANES : (rot + 1) * PLANES, lanes] = refs_ref[rot, :, lanes].astype(F32)
        block_s[:, lanes] = wide_s[:, lanes].astype(BF)
        for chip in range(CHIPS):
            copies.append(
                pltpu.make_async_copy(
                    block_s.at[:, lanes],
                    out_hbm.at[chip * PER_CHIP : (chip + 1) * PER_CHIP, lanes],
                    sems.at[half, chip],
                )
            )
            copies[-1].start()
    for copy in copies:
        copy.wait()


LANES = 1024


def slot_copies(flat_hbm, flat_s, sems, rows_of):
    return [
        pltpu.make_async_copy(
            flat_hbm.at[pl.ds(pl.multiple_of(rows_of(slot) * BOX, BOX), BOX)],
            flat_s.at[slot * BOX : (slot + 1) * BOX],
            sems.at[slot],
        )
        for slot in range(CAP)
    ]


def send_kernel(
    class_ref,
    rot_ref,
    bucket_ref,
    live_ref,
    level_ref,
    flat_hbm,
    send_out,
    own_out,
    count_out,
    slot_rot_out,
    slot_row_out,
    flat_s,
    spread_s,
    sems,
):
    owner = lax.axis_index("rot")
    core = lax.axis_index("dom") & 1
    count = jnp.int32(0)
    slot_row = [jnp.int32(0) for _ in range(CAP)]
    slot_rot = [jnp.int32(-1) for _ in range(CAP)]
    slot_bucket = [jnp.int32(-1) for _ in range(CAP)]
    for p in range(class_ref.shape[0]):
        mine = (class_ref[p] == owner) & (p < live_ref[0])
        for slot in range(CAP):
            here = mine & (count == slot)
            slot_row[slot] = jnp.where(here, p, slot_row[slot])
            slot_rot[slot] = jnp.where(here, rot_ref[p], slot_rot[slot])
            slot_bucket[slot] = jnp.where(here, bucket_ref[p], slot_bucket[slot])
        count = count + mine.astype(jnp.int32)
    copies = slot_copies(flat_hbm, flat_s, sems, lambda slot: slot_row[slot])
    for copy in copies:
        copy.start()
    count_out[0] = count
    for slot in range(CAP):
        slot_rot_out[slot] = slot_rot[slot]
        slot_row_out[slot] = slot_row[slot]
    columns = CAP * BOX
    lane = lax.broadcasted_iota(jnp.int32, (1, columns), 1)
    col_slot, col_x = lane >> 6, lane & (BOX - 1)
    col_rot = jnp.full((1, columns), -1, jnp.int32)
    col_bucket = jnp.full((1, columns), -1, jnp.int32)
    for slot in range(CAP):
        col_rot = jnp.where(col_slot == slot, slot_rot[slot], col_rot)
        col_bucket = jnp.where(col_slot == slot, slot_bucket[slot], col_bucket)
    levels = level_ref[...].astype(F32)
    col_weight = jnp.zeros((1, columns), F32)
    for level in range(levels.shape[1]):
        value = jnp.broadcast_to(levels[:, level : level + 1], (1, columns))
        col_weight = jnp.where(col_bucket == level, value, col_weight)
    row = lax.broadcasted_iota(jnp.int32, (SEND, columns), 0)
    base = (row // PER_CHIP) * (2 * PLANES) + (row & (PLANES - 1))
    right = ((row // PLANES) & (ROT_CLS - 1)) == col_rot
    for half, to_core in enumerate((core, 1 - core)):
        hit = right & (base + to_core * PLANES == col_x)
        spread_s[half * SEND : (half + 1) * SEND] = jnp.where(hit, col_weight, 0.0).astype(BF)
    for copy in copies:
        copy.wait()
    for start in range(0, BOX * BOX, LANES):
        lanes = slice(start, start + LANES)
        part = jnp.dot(spread_s[...], flat_s[:, lanes], preferred_element_type=F32)
        own_out[:, lanes] = part[:SEND].astype(BF)
        send_out[:, lanes] = part[SEND:].astype(BF)


def pair_kernel(own_ref, other_ref, out_ref):
    out_ref[...] = (own_ref[...].astype(F32) + other_ref[...].astype(F32)).astype(BF)


def spectra_kernel(slot_row_ref, count_ref, x_ref, flat_hbm, table_ref, spectra_out, flat_s, sems):
    now = pl.program_id(0)
    copies = slot_copies(flat_hbm, flat_s, sems, lambda slot: slot_row_ref[slot])
    for slot, copy in enumerate(copies):

        @pl.when((now == 0) & (slot < count_ref[0]))
        def _():
            copy.start()

    for slot, copy in enumerate(copies):

        @pl.when((now == slot) & (slot < count_ref[0]))
        def _():
            copy.wait()

    @pl.when(now < count_ref[0])
    def _():
        table = table_ref[...]
        rows = pl.ds(pl.multiple_of(now * BOX, BOX), BOX)
        for start in range(0, PAIRS, CHUNK):
            lanes = slice(128 * start, 128 * (start + CHUNK))
            along_x = jnp.dot(x_ref[...], flat_s[rows, lanes], preferred_element_type=F32)
            part = z_stage(along_x.astype(BF), table, 0, CHUNK)
            spectra_out[start * KXP : (start + CHUNK) * KXP, :] = part.astype(BF)

    @pl.when(now >= count_ref[0])
    def _():
        spectra_out[...] = jnp.zeros_like(spectra_out)


def score_kernel(
    count_ref,
    slot_rot_ref,
    zp_hbm,
    x_ref,
    own_ref,
    other_ref,
    table_ref,
    ex_ref,
    wz_ref,
    out_ref,
    pick_s,
    x_s,
    zp_s,
    p_s,
    r_s,
    a_s,
    sems,
):
    for slot in range(CAP):

        @pl.when(slot < count_ref[0])
        def _():
            pltpu.make_async_copy(zp_hbm.at[slot], zp_s.at[slot], sems.at[slot]).start()

    out_ref[...] = jnp.zeros_like(out_ref)

    @pl.when(count_ref[0] > 0)
    def _():
        core = lax.axis_index("dom") & 1
        ref_lane = lax.broadcasted_iota(jnp.int32, (1, SEND), 1)
        ref_rot = (ref_lane // PLANES) & (ROT_CLS - 1)
        for to in range(CAP):
            rows = slice(to * 2 * KXP, (to + 1) * 2 * KXP)
            wanted = ref_rot == slot_rot_ref[to]
            pick_s[rows, :SEND] = jnp.where(wanted, x_ref[core], 0.0).astype(BF)
            pick_s[rows, SEND:] = jnp.where(wanted, x_ref[1 - core], 0.0).astype(BF)
        for start in range(0, BOX * BOX, 512):
            lanes = slice(start, start + 512)
            planes = jnp.concatenate([own_ref[:, lanes], other_ref[:, lanes]], axis=0)
            part = jnp.dot(pick_s[...], planes, preferred_element_type=F32)
            x_s[:, :, lanes] = part.astype(BF).reshape(CAP, 2 * KXP, 512)

    def one_slot(slot, carry):
        pltpu.make_async_copy(zp_hbm.at[slot], zp_s.at[slot], sems.at[slot]).wait()
        table = table_ref[...]
        xr = x_s.at[slot]
        for start in range(0, PAIRS, STEP):
            part = z_stage(xr, table, start, STEP)
            r_s[start : start + STEP] = part.reshape(STEP, KXP, 4 * BOX)[:, :KXV, :]
            mine = zp_s[slot, start * KXP : (start + STEP) * KXP, :].astype(F32)
            p_s[start : start + STEP] = mine.reshape(STEP, KXP, 4 * BOX)[:, :KXV, :]
        first = lax.broadcasted_iota(jnp.int32, (8, 128), 1) < BOX

        def column(col, carry):
            rows = pl.ds(pl.multiple_of(col * 8, 8), 8)

            def pair(m):
                return r_s[m % PAIRS, rows, 0:128], r_s[m % PAIRS, rows, 128:256]

            def shifted(before, now):
                return tuple(
                    pltpu.roll(jnp.where(first, n, b), BOX, 1) for b, n in zip(before, now)
                )

            def three(re, im):
                return re, im, re - im

            tiles = {m: pair(m) for m in range(-2, 2)}
            even = {m: three(*tiles[m]) for m in range(-1, 2)}
            odd = {m: three(*shifted(tiles[m - 1], tiles[m])) for m in range(-1, 2)}
            last = tiles[1]
            sums = [[jnp.zeros((8, 128), F32) for _ in range(3)] for _ in range(SHIFTS)]
            for j in range(PAIRS):
                new = pair(j + 2)
                even[j + 2] = three(*new)
                odd[j + 2] = three(*shifted(last, new))
                last = new
                pr = p_s[j, rows, 0:128]
                pi = p_s[j, rows, 128:256]
                both = pr + pi
                for u in range(-2, 2):
                    for parity, held in ((0, even), (1, odd)):
                        t = 2 * u + parity + SHIFTS // 2
                        rr, ri, rd = held[j - u]
                        sums[t][0] = sums[t][0] + pr * rr
                        sums[t][1] = sums[t][1] + pi * ri
                        sums[t][2] = sums[t][2] + both * rd
                del even[j - 1], odd[j - 1]
            for t in range(SHIFTS):
                one, two, mix = sums[t]
                a_s[t, rows, 0:128] = one + two
                a_s[t, rows, 128:256] = mix - one + two
            return carry

        lax.fori_loop(0, KXV // 8, column, 0)
        ex = ex_ref[...]
        along_x = [
            jnp.dot(ex, a_s[t].astype(BF), preferred_element_type=F32) for t in range(SHIFTS)
        ]
        cos_rows = jnp.concatenate([u[:SHIFTS] for u in along_x], axis=0).astype(BF)
        sin_rows = jnp.concatenate([u[SHIFTS:] for u in along_x], axis=0).astype(BF)
        both_rows = jnp.concatenate([cos_rows, sin_rows], axis=1)
        final = jnp.dot(both_rows, wz_ref[...], preferred_element_type=F32)
        out_ref[slot] = final * (float(BOX) ** -3.5)
        return carry

    lax.fori_loop(0, count_ref[0], one_slot, 0)


def yz_kernel(parts_ref, table_ref, out_ref, z_s, g_s):
    total = parts_ref[0:PER_CHIP].astype(F32)
    for chip in range(1, CHIPS):
        total = total + parts_ref[chip * PER_CHIP : (chip + 1) * PER_CHIP].astype(F32)
    total = total.astype(BF)
    z_ref, y_ref = table_ref[: 2 * BOX], table_ref[2 * BOX :, :BOX]
    stacked = jnp.concatenate([total[:, 128 * j : 128 * (j + 1)] for j in range(PAIRS)], axis=0)
    z_part = jnp.dot(stacked, z_ref, preferred_element_type=F32)
    for j in range(PAIRS):
        for half in range(2):
            start = (2 * j + half) * PER_CHIP
            z_s[start : start + PER_CHIP] = z_part[
                j * PER_CHIP : (j + 1) * PER_CHIP, 128 * half : 128 * (half + 1)
            ]
    by_y = [z_s[pl.ds(n, BOX, stride=PER_CHIP), :].astype(BF) for n in range(PER_CHIP)]
    y_part = jnp.dot(y_ref, jnp.concatenate(by_y, axis=1), preferred_element_type=F32)
    first = lax.broadcasted_iota(jnp.int32, (BOX, 128), 1) < BOX
    for n in range(PER_CHIP):
        lanes = slice(128 * n, 128 * (n + 1))
        turned = pltpu.roll(y_part[BOX:, lanes], BOX, 1)
        g_s[pl.ds(n, BOX, stride=PER_CHIP), :] = y_part[:BOX, lanes] + jnp.where(first, turned, -turned)
    out_ref[...] = g_s[...].astype(BF)


def x_rows_kernel(rows_ref, table_ref, out_hbm, out_s, sems):
    copies = []
    rows = ROT_CLS * (BOX // DOM)
    first = lax.broadcasted_iota(jnp.int32, (ROT_CLS * BOX, 128), 1) < BOX
    for ky in range(BOX // DOM):
        grid = rows_ref[:, ky * rows : (ky + 1) * rows, :].reshape(ROT_CLS * BOX, 128)
        cos_part = jnp.dot(table_ref[0], grid, preferred_element_type=F32)
        sin_part = jnp.dot(table_ref[1], grid, preferred_element_type=F32)
        turned = pltpu.roll(sin_part, BOX, 1)
        total = (cos_part + jnp.where(first, turned, -turned)) * (float(BOX) ** -1.5)
        out_s[ky] = total.reshape(ROT_CLS, BOX, 128)
        copies.append(pltpu.make_async_copy(out_s.at[ky], out_hbm.at[ky], sems.at[ky]))
        copies[-1].start()
    for copy in copies:
        copy.wait()


VMEM = pl.BlockSpec(memory_space=pltpu.VMEM)
HBM = pl.BlockSpec(memory_space=pltpu.HBM)
SMEM = pl.BlockSpec(memory_space=pltpu.SMEM)


def params(mib):
    return pltpu.CompilerParams(vmem_limit_bytes=mib * 1024 * 1024)


def cost(flops, moved):
    return pl.CostEstimate(flops=flops, bytes_accessed=moved, transcendentals=0)


def shards(particles, references, part_class, part_rot, bucket, bucket_weights, live_count):
    block_size = particles.shape[0]
    voxels = BOX * BOX
    columns = block_size * BOX
    to_other = [(i, i ^ 1) for i in range(DOM)]

    mine_refs = pl.pallas_call(
        fan_kernel,
        out_shape=jax.ShapeDtypeStruct((SEND, voxels), BF),
        in_specs=[VMEM],
        out_specs=HBM,
        scratch_shapes=[
            pltpu.VMEM((PER_CHIP, voxels), F32),
            pltpu.VMEM((PER_CHIP, voxels), BF),
            pltpu.SemaphoreType.DMA((2, CHIPS)),
        ],
        compiler_params=params(54),
        cost_estimate=cost(1024, 1024),
        name="fan",
    )(references)

    flat = particles.reshape(columns, voxels)
    classes = part_class.reshape(block_size)
    x_half = x_half_table()
    by_core = x_half.reshape(2 * KXP, CHIPS, 2, 1, PLANES)
    by_core = np.broadcast_to(by_core, (2 * KXP, CHIPS, 2, ROT_CLS, PLANES))
    by_core = by_core.transpose(2, 0, 1, 3, 4).reshape(2, 2 * KXP, SEND)
    held = [
        pltpu.VMEM((CAP * BOX, voxels), BF),
        pltpu.SemaphoreType.DMA((CAP,)),
    ]

    def whole(*shape):
        return pl.BlockSpec(shape, lambda s: (0,) * len(shape))

    to_send, own, count, slot_rot, slot_row = pl.pallas_call(
        send_kernel,
        out_shape=(
            jax.ShapeDtypeStruct((SEND, voxels), BF),
            jax.ShapeDtypeStruct((SEND, voxels), BF),
            jax.ShapeDtypeStruct((1,), jnp.int32),
            jax.ShapeDtypeStruct((CAP,), jnp.int32),
            jax.ShapeDtypeStruct((CAP,), jnp.int32),
        ),
        in_specs=[SMEM, SMEM, SMEM, SMEM, VMEM, HBM],
        out_specs=(VMEM, VMEM, SMEM, SMEM, SMEM),
        scratch_shapes=[held[0], pltpu.VMEM((2 * SEND, CAP * BOX), BF), held[1]],
        compiler_params=params(54),
        cost_estimate=cost(1024, 1024),
        name="send",
    )(
        classes,
        part_rot,
        bucket,
        live_count,
        bucket_weights.reshape(1, -1),
        flat,
    )
    other = lax.ppermute(to_send, "dom", to_other)
    refs_own = lax.all_to_all(
        mine_refs, "dom", 0, 0, tiled=True, axis_index_groups=SAME_CORE
    )
    pair_sum = pl.pallas_call(
        pair_kernel,
        out_shape=jax.ShapeDtypeStruct((SEND, voxels), BF),
        in_specs=[VMEM, VMEM],
        out_specs=VMEM,
        compiler_params=params(50),
        cost_estimate=cost(1024, 1024),
        name="pair",
    )(own, other)

    z_table = jnp.asarray(z_complex_table().astype(BF))
    spectra = pl.pallas_call(
        spectra_kernel,
        out_shape=jax.ShapeDtypeStruct((CAP, PAIRS * KXP, 4 * BOX), BF),
        grid=(CAP,),
        in_specs=[SMEM, SMEM, whole(2 * KXP, BOX), HBM, whole(4 * BOX, 4 * BOX)],
        out_specs=pl.BlockSpec((None, PAIRS * KXP, 4 * BOX), lambda i: (i, 0, 0)),
        scratch_shapes=held,
        compiler_params=params(54),
        cost_estimate=cost(20 * 10**9, 1024),
        name="spectra",
    )(slot_row, count, jnp.asarray(x_half.astype(BF)), flat, z_table)

    refs_own, spectra, pair_sum = lax.optimization_barrier((refs_own, spectra, pair_sum))
    arrived = lax.all_to_all(pair_sum, "dom", 0, 0, tiled=True, axis_index_groups=SAME_CORE)
    refs_other = lax.ppermute(refs_own, "dom", to_other)
    ex, wz = shift_tables()

    slots = pl.pallas_call(
        score_kernel,
        out_shape=jax.ShapeDtypeStruct((CAP, SHIFTS * SHIFTS, 128), F32),
        in_specs=[SMEM, SMEM, HBM] + [VMEM] * 6,
        out_specs=VMEM,
        scratch_shapes=[
            pltpu.VMEM((CAP * 2 * KXP, 2 * SEND), BF),
            pltpu.VMEM((CAP, 2 * KXP, voxels), BF),
            pltpu.VMEM((CAP, PAIRS * KXP, 4 * BOX), BF),
            pltpu.VMEM((PAIRS, KXV, 4 * BOX), F32),
            pltpu.VMEM((PAIRS, KXV, 4 * BOX), F32),
            pltpu.VMEM((SHIFTS, KXV, 4 * BOX), F32),
            pltpu.SemaphoreType.DMA((CAP,)),
        ],
        compiler_params=params(52),
        cost_estimate=cost(1024, 1024),
        name="slot_scores",
    )(
        count,
        slot_rot,
        spectra,
        jnp.asarray(by_core, F32),
        refs_own,
        refs_other,
        z_table,
        jnp.asarray(ex.astype(BF)),
        jnp.asarray(wz.astype(BF)),
    )
    slot_scores = slots[:, :, :SHIFTS].reshape(CAP, SHIFTS, SHIFTS, SHIFTS)
    slot_scores = slot_scores.transpose(0, 2, 1, 3).reshape(CAP, SHIFTS**3)
    everywhere = slot_scores
    for bit in (1, 2, 4):
        held_there = lax.ppermute(everywhere, "rot", [(i, i ^ bit) for i in range(8)])
        everywhere = jnp.concatenate([everywhere, held_there], axis=0)
    rows_all = jnp.arange(block_size, dtype=jnp.int32)
    alive = rows_all < live_count[0]
    before = (classes[:, None] == classes[None, :]) & (rows_all[None, :] < rows_all[:, None])
    place = (classes ^ lax.axis_index("rot")) * CAP + jnp.sum(before.astype(jnp.int32), axis=1)
    found = (place[:, None] == jnp.arange(8 * CAP, dtype=jnp.int32)[None, :]) & alive[:, None]
    scores = jnp.sum(jnp.where(found[:, :, None], everywhere[None, :, :], 0.0), axis=1)

    yz_table = np.zeros((4 * BOX, 4 * BOX))
    yz_table[: 2 * BOX] = z_real_table()
    yz_table[2 * BOX :, :BOX] = y_table()
    grids = pl.pallas_call(
        yz_kernel,
        out_shape=jax.ShapeDtypeStruct((BOX * PER_CHIP, 2 * BOX), BF),
        in_specs=[VMEM, VMEM],
        out_specs=VMEM,
        scratch_shapes=[pltpu.VMEM((BOX * PER_CHIP, 128), F32)] * 2,
        compiler_params=params(50),
        cost_estimate=cost(1024, 1024),
        name="yz_planes",
    )(arrived, jnp.asarray(yz_table.astype(BF)))
    by_rows = lax.all_to_all(grids, "dom", 0, 0, tiled=True)
    sums = pl.pallas_call(
        x_rows_kernel,
        out_shape=jax.ShapeDtypeStruct((BOX // DOM, ROT_CLS, BOX, 2 * BOX), F32),
        in_specs=[VMEM, VMEM],
        out_specs=HBM,
        scratch_shapes=[
            pltpu.VMEM((BOX // DOM, ROT_CLS, BOX, 2 * BOX), F32),
            pltpu.SemaphoreType.DMA((BOX // DOM,)),
        ],
        compiler_params=params(50),
        name="x_rows",
    )(by_rows.reshape(DOM, PLANES * PER_CHIP, 2 * BOX), jnp.asarray(x_rows_table().astype(BF)))
    return (scores, sums)


def solution(mesh):
    return jax.shard_map(
        shards,
        mesh=mesh,
        in_specs=(
            P("dom", None, None),
            P("rot", "dom", None),
            P("dom", None),
            P("dom"),
            P("dom"),
            P(),
            P("dom"),
        ),
        out_specs=(P("dom", None), P("dom", "rot", None, None)),
        check_vma=False,
    )
```

```python
import math

import jax
import jax.numpy as jnp
import numpy as np
from jax import lax
from jax.experimental import pallas as pl
from jax.experimental.pallas import tpu as pltpu
from jax.sharding import PartitionSpec as P

BOX = 64
SHIFTS = 8
ROT_CLS = 4
CAP = 4
HALF = 33
KXP = 48
KXV = 40
PAIRS = BOX // 2
DOM = 16
CHIPS = DOM // 2
SAME_CORE = [[2 * chip + core for chip in range(CHIPS)] for core in range(2)]
BF = jnp.bfloat16
F32 = jnp.float32


def grid_cos_sin(rows, cols):
    theta = ((rows[:, None] * cols[None, :]) % BOX).astype(np.float64) * (2.0 * math.pi / BOX)
    return np.cos(theta), np.sin(theta)


def x_half_table():
    c, s = grid_cos_sin(np.arange(BOX), np.arange(BOX))
    out = np.zeros((2, KXP, BOX))
    out[0, :HALF] = c[:HALF]
    out[1, :HALF] = -s[:HALF]
    return out.reshape(2 * KXP, BOX)


def z_complex_table():
    c, s = grid_cos_sin(np.arange(BOX), np.arange(BOX))
    two = np.eye(2)
    return np.block([[np.kron(two, c), np.kron(two, -s)], [np.kron(two, s), np.kron(two, c)]])


def shift_tables():
    c, s = grid_cos_sin(np.arange(SHIFTS) - SHIFTS // 2, np.arange(BOX))
    fold = np.zeros((KXV,))
    fold[:HALF] = 2.0
    fold[0] = fold[HALF - 1] = 1.0
    ex = np.zeros((2 * SHIFTS, KXV))
    ex[:SHIFTS, :HALF] = c[:, :HALF]
    ex[SHIFTS:, :HALF] = s[:, :HALF]
    ex = ex * fold[None, :]
    wz = np.zeros((2, 4 * BOX, 128))
    wz[0, :, :SHIFTS] = np.concatenate([c.T, c.T, -s.T, -s.T], axis=0)
    wz[1, :, :SHIFTS] = np.concatenate([-s.T, -s.T, -c.T, -c.T], axis=0)
    return ex, wz.reshape(8 * BOX, 128)


def z_real_table():
    c, s = grid_cos_sin(np.arange(BOX), np.arange(BOX))
    return np.kron(np.eye(2), np.concatenate([c, -s], axis=1))


def y_table():
    c, s = grid_cos_sin(np.arange(BOX), np.arange(BOX))
    return np.concatenate([c, s], axis=0)


def x_rows_table():
    c, s = grid_cos_sin(np.arange(BOX), np.arange(BOX))
    return np.stack(
        [
            np.einsum(
                "rq,kdx->rkdqx", np.eye(ROT_CLS), table.reshape(BOX, DOM, BOX // DOM)
            ).reshape(ROT_CLS * BOX, ROT_CLS * BOX)
            for table in (c, s)
        ]
    )


def z_stage(src, table, start, count):
    parts = []
    for j in range(start, start + count):
        lanes = slice(128 * j, 128 * (j + 1))
        parts.append(jnp.concatenate([src[0:KXP, lanes], src[KXP : 2 * KXP, lanes]], axis=1))
    return jnp.dot(jnp.concatenate(parts, axis=0), table, preferred_element_type=F32)


STEP = 8
CHUNK = 4
PLANES = BOX // DOM
PER_CHIP = ROT_CLS * PLANES
SEND = CHIPS * PER_CHIP


def fan_kernel(refs_ref, out_hbm, wide_s, block_s, sems):
    copies = []
    for half in range(2):
        lanes = slice(half * BOX * PAIRS, (half + 1) * BOX * PAIRS)
        for rot in range(ROT_CLS):
            wide_s[rot * PLANES : (rot + 1) * PLANES, lanes] = refs_ref[rot, :, lanes].astype(F32)
        block_s[:, lanes] = wide_s[:, lanes].astype(BF)
        for chip in range(CHIPS):
            copies.append(
                pltpu.make_async_copy(
                    block_s.at[:, lanes],
                    out_hbm.at[chip * PER_CHIP : (chip + 1) * PER_CHIP, lanes],
                    sems.at[half, chip],
                )
            )
            copies[-1].start()
    for copy in copies:
        copy.wait()


LANES = 1024


def slot_copies(flat_hbm, flat_s, sems, rows_of):
    return [
        pltpu.make_async_copy(
            flat_hbm.at[pl.ds(pl.multiple_of(rows_of(slot) * BOX, BOX), BOX)],
            flat_s.at[slot * BOX : (slot + 1) * BOX],
            sems.at[slot],
        )
        for slot in range(CAP)
    ]


def send_kernel(
    class_ref,
    rot_ref,
    bucket_ref,
    live_ref,
    level_ref,
    flat_hbm,
    send_out,
    own_out,
    count_out,
    slot_rot_out,
    slot_row_out,
    flat_s,
    spread_s,
    sems,
):
    owner = lax.axis_index("rot")
    core = lax.axis_index("dom") & 1
    count = jnp.int32(0)
    slot_row = [jnp.int32(0) for _ in range(CAP)]
    slot_rot = [jnp.int32(-1) for _ in range(CAP)]
    slot_bucket = [jnp.int32(-1) for _ in range(CAP)]
    for p in range(class_ref.shape[0]):
        mine = (class_ref[p] == owner) & (p < live_ref[0])
        for slot in range(CAP):
            here = mine & (count == slot)
            slot_row[slot] = jnp.where(here, p, slot_row[slot])
            slot_rot[slot] = jnp.where(here, rot_ref[p], slot_rot[slot])
            slot_bucket[slot] = jnp.where(here, bucket_ref[p], slot_bucket[slot])
        count = count + mine.astype(jnp.int32)
    copies = slot_copies(flat_hbm, flat_s, sems, lambda slot: slot_row[slot])
    for copy in copies:
        copy.start()
    count_out[0] = count
    for slot in range(CAP):
        slot_rot_out[slot] = slot_rot[slot]
        slot_row_out[slot] = slot_row[slot]
    columns = CAP * BOX
    lane = lax.broadcasted_iota(jnp.int32, (1, columns), 1)
    col_slot, col_x = lane >> 6, lane & (BOX - 1)
    col_rot = jnp.full((1, columns), -1, jnp.int32)
    col_bucket = jnp.full((1, columns), -1, jnp.int32)
    for slot in range(CAP):
        col_rot = jnp.where(col_slot == slot, slot_rot[slot], col_rot)
        col_bucket = jnp.where(col_slot == slot, slot_bucket[slot], col_bucket)
    levels = level_ref[...].astype(F32)
    col_weight = jnp.zeros((1, columns), F32)
    for level in range(levels.shape[1]):
        value = jnp.broadcast_to(levels[:, level : level + 1], (1, columns))
        col_weight = jnp.where(col_bucket == level, value, col_weight)
    row = lax.broadcasted_iota(jnp.int32, (SEND, columns), 0)
    base = (row // PER_CHIP) * (2 * PLANES) + (row & (PLANES - 1))
    right = ((row // PLANES) & (ROT_CLS - 1)) == col_rot
    for half, to_core in enumerate((core, 1 - core)):
        hit = right & (base + to_core * PLANES == col_x)
        spread_s[half * SEND : (half + 1) * SEND] = jnp.where(hit, col_weight, 0.0).astype(BF)
    for copy in copies:
        copy.wait()
    for start in range(0, BOX * BOX, LANES):
        lanes = slice(start, start + LANES)
        part = jnp.dot(spread_s[...], flat_s[:, lanes], preferred_element_type=F32)
        own_out[:, lanes] = part[:SEND].astype(BF)
        send_out[:, lanes] = part[SEND:].astype(BF)


def pair_kernel(own_ref, other_ref, out_ref):
    out_ref[...] = (own_ref[...].astype(F32) + other_ref[...].astype(F32)).astype(BF)


def spectra_kernel(slot_row_ref, count_ref, x_ref, flat_hbm, table_ref, spectra_out, flat_s, sems):
    now = pl.program_id(0)
    copies = slot_copies(flat_hbm, flat_s, sems, lambda slot: slot_row_ref[slot])
    for slot, copy in enumerate(copies):

        @pl.when((now == 0) & (slot < count_ref[0]))
        def _():
            copy.start()

    for slot, copy in enumerate(copies):

        @pl.when((now == slot) & (slot < count_ref[0]))
        def _():
            copy.wait()

    @pl.when(now < count_ref[0])
    def _():
        table = table_ref[...]
        rows = pl.ds(pl.multiple_of(now * BOX, BOX), BOX)
        for start in range(0, PAIRS, CHUNK):
            lanes = slice(128 * start, 128 * (start + CHUNK))
            along_x = jnp.dot(x_ref[...], flat_s[rows, lanes], preferred_element_type=F32)
            part = z_stage(along_x.astype(BF), table, 0, CHUNK)
            spectra_out[start * KXP : (start + CHUNK) * KXP, :] = part.astype(BF)

    @pl.when(now >= count_ref[0])
    def _():
        spectra_out[...] = jnp.zeros_like(spectra_out)


def score_kernel(
    count_ref,
    slot_rot_ref,
    zp_hbm,
    x_ref,
    own_ref,
    other_ref,
    table_ref,
    ex_ref,
    wz_ref,
    out_ref,
    pick_s,
    x_s,
    zp_s,
    p_s,
    r_s,
    a_s,
    sems,
):
    for slot in range(CAP):

        @pl.when(slot < count_ref[0])
        def _():
            pltpu.make_async_copy(zp_hbm.at[slot], zp_s.at[slot], sems.at[slot]).start()

    out_ref[...] = jnp.zeros_like(out_ref)

    @pl.when(count_ref[0] > 0)
    def _():
        core = lax.axis_index("dom") & 1
        ref_lane = lax.broadcasted_iota(jnp.int32, (1, SEND), 1)
        ref_rot = (ref_lane // PLANES) & (ROT_CLS - 1)
        for to in range(CAP):
            rows = slice(to * 2 * KXP, (to + 1) * 2 * KXP)
            wanted = ref_rot == slot_rot_ref[to]
            pick_s[rows, :SEND] = jnp.where(wanted, x_ref[core], 0.0).astype(BF)
            pick_s[rows, SEND:] = jnp.where(wanted, x_ref[1 - core], 0.0).astype(BF)
        for start in range(0, BOX * BOX, 1024):
            lanes = slice(start, start + 1024)
            planes = jnp.concatenate([own_ref[:, lanes], other_ref[:, lanes]], axis=0)
            part = jnp.dot(pick_s[...], planes, preferred_element_type=F32)
            x_s[:, :, lanes] = part.astype(BF).reshape(CAP, 2 * KXP, 1024)

    def one_slot(slot, carry):
        pltpu.make_async_copy(zp_hbm.at[slot], zp_s.at[slot], sems.at[slot]).wait()
        table = table_ref[...]
        xr = x_s.at[slot]
        for start in range(0, PAIRS, STEP):
            part = z_stage(xr, table, start, STEP)
            part = part.astype(BF).astype(F32).reshape(STEP, KXP, 4 * BOX)
            r_s[start : start + STEP] = part[:, :KXV, :]
            mine = zp_s[slot, start * KXP : (start + STEP) * KXP, :].astype(F32)
            p_s[start : start + STEP] = mine.reshape(STEP, KXP, 4 * BOX)[:, :KXV, :]
        first = lax.broadcasted_iota(jnp.int32, (8, 128), 1) < BOX

        def column(col, carry):
            rows = pl.ds(pl.multiple_of(col * 8, 8), 8)

            def pair(m):
                return r_s[m % PAIRS, rows, 0:128], r_s[m % PAIRS, rows, 128:256]

            def shifted(before, now):
                return tuple(
                    pltpu.roll(jnp.where(first, n, b), BOX, 1) for b, n in zip(before, now)
                )

            def three(re, im):
                return re, im, re - im

            tiles = {m: pair(m) for m in range(-2, 2)}
            even = {m: three(*tiles[m]) for m in range(-1, 2)}
            odd = {m: three(*shifted(tiles[m - 1], tiles[m])) for m in range(-1, 2)}
            last = tiles[1]
            sums = [[jnp.zeros((8, 128), F32) for _ in range(3)] for _ in range(SHIFTS)]
            for j in range(PAIRS):
                new = pair(j + 2)
                even[j + 2] = three(*new)
                odd[j + 2] = three(*shifted(last, new))
                last = new
                pr = p_s[j, rows, 0:128]
                pi = p_s[j, rows, 128:256]
                both = pr + pi
                for u in range(-2, 2):
                    for parity, held in ((0, even), (1, odd)):
                        t = 2 * u + parity + SHIFTS // 2
                        rr, ri, rd = held[j - u]
                        sums[t][0] = sums[t][0] + pr * rr
                        sums[t][1] = sums[t][1] + pi * ri
                        sums[t][2] = sums[t][2] + both * rd
                del even[j - 1], odd[j - 1]
            for t in range(SHIFTS):
                one, two, mix = sums[t]
                a_s[t, rows, 0:128] = one + two
                a_s[t, rows, 128:256] = mix - one + two
            return carry

        lax.fori_loop(0, KXV // 8, column, 0)
        ex = ex_ref[...]
        along_x = [
            jnp.dot(ex, a_s[t].astype(BF), preferred_element_type=F32) for t in range(SHIFTS)
        ]
        cos_rows = jnp.concatenate([u[:SHIFTS] for u in along_x], axis=0).astype(BF)
        sin_rows = jnp.concatenate([u[SHIFTS:] for u in along_x], axis=0).astype(BF)
        both_rows = jnp.concatenate([cos_rows, sin_rows], axis=1)
        final = jnp.dot(both_rows, wz_ref[...], preferred_element_type=F32)
        out_ref[slot] = final * (float(BOX) ** -3.5)
        return carry

    lax.fori_loop(0, count_ref[0], one_slot, 0)


def yz_kernel(parts_ref, table_ref, out_ref, z_s, g_s):
    total = parts_ref[0:PER_CHIP].astype(F32)
    for chip in range(1, CHIPS):
        total = total + parts_ref[chip * PER_CHIP : (chip + 1) * PER_CHIP].astype(F32)
    total = total.astype(BF)
    z_ref, y_ref = table_ref[: 2 * BOX], table_ref[2 * BOX :, :BOX]
    stacked = jnp.concatenate([total[:, 128 * j : 128 * (j + 1)] for j in range(PAIRS)], axis=0)
    z_part = jnp.dot(stacked, z_ref, preferred_element_type=F32)
    for j in range(PAIRS):
        for half in range(2):
            start = (2 * j + half) * PER_CHIP
            z_s[start : start + PER_CHIP] = z_part[
                j * PER_CHIP : (j + 1) * PER_CHIP, 128 * half : 128 * (half + 1)
            ]
    by_y = [z_s[pl.ds(n, BOX, stride=PER_CHIP), :].astype(BF) for n in range(PER_CHIP)]
    y_part = jnp.dot(y_ref, jnp.concatenate(by_y, axis=1), preferred_element_type=F32)
    first = lax.broadcasted_iota(jnp.int32, (BOX, 128), 1) < BOX
    for n in range(PER_CHIP):
        lanes = slice(128 * n, 128 * (n + 1))
        turned = pltpu.roll(y_part[BOX:, lanes], BOX, 1)
        g_s[pl.ds(n, BOX, stride=PER_CHIP), :] = y_part[:BOX, lanes] + jnp.where(first, turned, -turned)
    out_ref[...] = g_s[...].astype(BF)


def x_rows_kernel(rows_ref, table_ref, out_hbm, out_s, sems):
    copies = []
    rows = ROT_CLS * (BOX // DOM)
    first = lax.broadcasted_iota(jnp.int32, (ROT_CLS * BOX, 128), 1) < BOX
    for ky in range(BOX // DOM):
        grid = rows_ref[:, ky * rows : (ky + 1) * rows, :].reshape(ROT_CLS * BOX, 128)
        cos_part = jnp.dot(table_ref[0], grid, preferred_element_type=F32)
        sin_part = jnp.dot(table_ref[1], grid, preferred_element_type=F32)
        turned = pltpu.roll(sin_part, BOX, 1)
        total = (cos_part + jnp.where(first, turned, -turned)) * (float(BOX) ** -1.5)
        out_s[ky] = total.reshape(ROT_CLS, BOX, 128)
        copies.append(pltpu.make_async_copy(out_s.at[ky], out_hbm.at[ky], sems.at[ky]))
        copies[-1].start()
    for copy in copies:
        copy.wait()


VMEM = pl.BlockSpec(memory_space=pltpu.VMEM)
HBM = pl.BlockSpec(memory_space=pltpu.HBM)
SMEM = pl.BlockSpec(memory_space=pltpu.SMEM)


def params(mib):
    return pltpu.CompilerParams(vmem_limit_bytes=mib * 1024 * 1024)


def cost(flops, moved):
    return pl.CostEstimate(flops=flops, bytes_accessed=moved, transcendentals=0)


def shards(particles, references, part_class, part_rot, bucket, bucket_weights, live_count):
    block_size = particles.shape[0]
    voxels = BOX * BOX
    columns = block_size * BOX
    to_other = [(i, i ^ 1) for i in range(DOM)]

    mine_refs = pl.pallas_call(
        fan_kernel,
        out_shape=jax.ShapeDtypeStruct((SEND, voxels), BF),
        in_specs=[VMEM],
        out_specs=HBM,
        scratch_shapes=[
            pltpu.VMEM((PER_CHIP, voxels), F32),
            pltpu.VMEM((PER_CHIP, voxels), BF),
            pltpu.SemaphoreType.DMA((2, CHIPS)),
        ],
        compiler_params=params(54),
        cost_estimate=cost(1024, 1024),
        name="fan",
    )(references)

    flat = particles.reshape(columns, voxels)
    classes = part_class.reshape(block_size)
    x_half = x_half_table()
    by_core = x_half.reshape(2 * KXP, CHIPS, 2, 1, PLANES)
    by_core = np.broadcast_to(by_core, (2 * KXP, CHIPS, 2, ROT_CLS, PLANES))
    by_core = by_core.transpose(2, 0, 1, 3, 4).reshape(2, 2 * KXP, SEND)
    held = [
        pltpu.VMEM((CAP * BOX, voxels), BF),
        pltpu.SemaphoreType.DMA((CAP,)),
    ]

    def whole(*shape):
        return pl.BlockSpec(shape, lambda s: (0,) * len(shape))

    to_send, own, count, slot_rot, slot_row = pl.pallas_call(
        send_kernel,
        out_shape=(
            jax.ShapeDtypeStruct((SEND, voxels), BF),
            jax.ShapeDtypeStruct((SEND, voxels), BF),
            jax.ShapeDtypeStruct((1,), jnp.int32),
            jax.ShapeDtypeStruct((CAP,), jnp.int32),
            jax.ShapeDtypeStruct((CAP,), jnp.int32),
        ),
        in_specs=[SMEM, SMEM, SMEM, SMEM, VMEM, HBM],
        out_specs=(VMEM, VMEM, SMEM, SMEM, SMEM),
        scratch_shapes=[held[0], pltpu.VMEM((2 * SEND, CAP * BOX), BF), held[1]],
        compiler_params=params(54),
        cost_estimate=cost(1024, 1024),
        name="send",
    )(
        classes,
        part_rot,
        bucket,
        live_count,
        bucket_weights.reshape(1, -1),
        flat,
    )
    other = lax.ppermute(to_send, "dom", to_other)
    refs_own = lax.all_to_all(
        mine_refs, "dom", 0, 0, tiled=True, axis_index_groups=SAME_CORE
    )
    pair_sum = pl.pallas_call(
        pair_kernel,
        out_shape=jax.ShapeDtypeStruct((SEND, voxels), BF),
        in_specs=[VMEM, VMEM],
        out_specs=VMEM,
        compiler_params=params(50),
        cost_estimate=cost(1024, 1024),
        name="pair",
    )(own, other)

    z_table = jnp.asarray(z_complex_table().astype(BF))
    spectra = pl.pallas_call(
        spectra_kernel,
        out_shape=jax.ShapeDtypeStruct((CAP, PAIRS * KXP, 4 * BOX), BF),
        grid=(CAP,),
        in_specs=[SMEM, SMEM, whole(2 * KXP, BOX), HBM, whole(4 * BOX, 4 * BOX)],
        out_specs=pl.BlockSpec((None, PAIRS * KXP, 4 * BOX), lambda i: (i, 0, 0)),
        scratch_shapes=held,
        compiler_params=params(54),
        cost_estimate=cost(20 * 10**9, 1024),
        name="spectra",
    )(slot_row, count, jnp.asarray(x_half.astype(BF)), flat, z_table)

    refs_own, spectra, pair_sum = lax.optimization_barrier((refs_own, spectra, pair_sum))
    arrived = lax.all_to_all(pair_sum, "dom", 0, 0, tiled=True, axis_index_groups=SAME_CORE)
    refs_other = lax.ppermute(refs_own, "dom", to_other)
    ex, wz = shift_tables()

    slots = pl.pallas_call(
        score_kernel,
        out_shape=jax.ShapeDtypeStruct((CAP, SHIFTS * SHIFTS, 128), F32),
        in_specs=[SMEM, SMEM, HBM] + [VMEM] * 6,
        out_specs=VMEM,
        scratch_shapes=[
            pltpu.VMEM((CAP * 2 * KXP, 2 * SEND), BF),
            pltpu.VMEM((CAP, 2 * KXP, voxels), BF),
            pltpu.VMEM((CAP, PAIRS * KXP, 4 * BOX), BF),
            pltpu.VMEM((PAIRS, KXV, 4 * BOX), F32),
            pltpu.VMEM((PAIRS, KXV, 4 * BOX), F32),
            pltpu.VMEM((SHIFTS, KXV, 4 * BOX), F32),
            pltpu.SemaphoreType.DMA((CAP,)),
        ],
        compiler_params=params(52),
        cost_estimate=cost(1024, 1024),
        name="slot_scores",
    )(
        count,
        slot_rot,
        spectra,
        jnp.asarray(by_core, F32),
        refs_own,
        refs_other,
        z_table,
        jnp.asarray(ex.astype(BF)),
        jnp.asarray(wz.astype(BF)),
    )
    slot_scores = slots[:, :, :SHIFTS].reshape(CAP, SHIFTS, SHIFTS, SHIFTS)
    slot_scores = slot_scores.transpose(0, 2, 1, 3).reshape(CAP, SHIFTS**3)
    everywhere = slot_scores
    for bit in (1, 2, 4):
        held_there = lax.ppermute(everywhere, "rot", [(i, i ^ bit) for i in range(8)])
        everywhere = jnp.concatenate([everywhere, held_there], axis=0)
    rows_all = jnp.arange(block_size, dtype=jnp.int32)
    alive = rows_all < live_count[0]
    before = (classes[:, None] == classes[None, :]) & (rows_all[None, :] < rows_all[:, None])
    place = (classes ^ lax.axis_index("rot")) * CAP + jnp.sum(before.astype(jnp.int32), axis=1)
    found = (place[:, None] == jnp.arange(8 * CAP, dtype=jnp.int32)[None, :]) & alive[:, None]
    scores = jnp.sum(jnp.where(found[:, :, None], everywhere[None, :, :], 0.0), axis=1)

    yz_table = np.zeros((4 * BOX, 4 * BOX))
    yz_table[: 2 * BOX] = z_real_table()
    yz_table[2 * BOX :, :BOX] = y_table()
    grids = pl.pallas_call(
        yz_kernel,
        out_shape=jax.ShapeDtypeStruct((BOX * PER_CHIP, 2 * BOX), BF),
        in_specs=[VMEM, VMEM],
        out_specs=VMEM,
        scratch_shapes=[pltpu.VMEM((BOX * PER_CHIP, 128), F32)] * 2,
        compiler_params=params(50),
        cost_estimate=cost(1024, 1024),
        name="yz_planes",
    )(arrived, jnp.asarray(yz_table.astype(BF)))
    by_rows = lax.all_to_all(grids, "dom", 0, 0, tiled=True)
    sums = pl.pallas_call(
        x_rows_kernel,
        out_shape=jax.ShapeDtypeStruct((BOX // DOM, ROT_CLS, BOX, 2 * BOX), F32),
        in_specs=[VMEM, VMEM],
        out_specs=HBM,
        scratch_shapes=[
            pltpu.VMEM((BOX // DOM, ROT_CLS, BOX, 2 * BOX), F32),
            pltpu.SemaphoreType.DMA((BOX // DOM,)),
        ],
        compiler_params=params(50),
        name="x_rows",
    )(by_rows.reshape(DOM, PLANES * PER_CHIP, 2 * BOX), jnp.asarray(x_rows_table().astype(BF)))
    return (scores, sums)


def solution(mesh):
    return jax.shard_map(
        shards,
        mesh=mesh,
        in_specs=(
            P("dom", None, None),
            P("rot", "dom", None),
            P("dom", None),
            P("dom"),
            P("dom"),
            P(),
            P("dom"),
        ),
        out_specs=(P("dom", None), P("dom", "rot", None, None)),
        check_vma=False,
    )
```
